256 devices in a mesh: row: 8 (over y, core), sim: 32 (over x, z).
Axes of the slice: x: 4, y: 4, z: 8, core: 2. Of those that a mesh axis runs over, the one named last changes fastest.
Arguments:
- sim_points: float32 [24, 131072], P(None, ('row', 'sim')), may hold values from 0 to 1
- weights: float32 [131072], P(('row', 'sim')), may hold values from -0.06629126 to 0.06629126
- hw_points: float32 [24, 32768], P(None, ('row', 'sim')), may hold values from 0 to 1
- high_values: float32 [32768], P(('row', 'sim')), may hold values from -6 to 6
- len_low: float32 [24], replicated, may hold values from 0.6 to 3
- len_high: float32 [24], replicated, may hold values from 0.6 to 3
- rho: float32 [1], replicated, may hold values from 0.5 to 1.5
- noise: float32 [1], replicated, may hold values from 0.3 to 1
Outputs:
- mu_low: float32 [32768], P(('row', 'sim'))
- solution: float32 [32768], P(('row', 'sim'))
- residual: float32 [32768], P(('row', 'sim'))
The draws below stay inside these ranges and needn't reach their ends.
All inputs are finite; a program needn't handle non-finite values.
Results may differ from the reference program's by a relative error of at most 0.0003.
Values sent between devices are 32-bit elements; how exact they have to be, the bound alone decides.
No kernel may reach another device: no remote copies, remote signals or barrier semaphores. Data moves between devices by JAX's collectives and lax.ppermute only.
A program may use at most 64 MiB of HBM per device.

```python
import math
import jax
import jax.numpy as jnp
from jax import lax

F = 24
ITERS = 2
HW = 32768
RUNS = 131072


def level_of(stream_key, extent, pieces, smallest, high):
    gain = 1.0
    for axis_at, shards_of in pieces:
        draws = jax.random.uniform(jax.random.fold_in(jax.random.fold_in(stream_key, 6), axis_at), (shards_of,), jnp.float32, smallest / len(pieces), high / len(pieces))
        gain = gain * jnp.repeat(jnp.exp(draws), extent[axis_at] // shards_of).reshape((-1,) + (1,) * (len(extent) - 1 - axis_at))
    return gain


def gaussian(own_key, dims, spread, bound, shards=(), kind=jnp.bfloat16):
    values = spread * jax.random.normal(own_key, dims, jnp.float32)
    if shards:
        values = values * level_of(own_key, dims, shards, -0.22, 0.18)
    return jnp.clip(values, -bound, bound).astype(kind)


def setup_inputs(seed: int = 0) -> dict:
    key_of = jax.random.split(jax.random.key(seed), 9)
    sim_points = jnp.clip(1.0 * jax.random.uniform(key_of[0], (F, RUNS), jnp.float32) ** level_of(key_of[0], (F, RUNS), ((1, 256),), -0.2, 0.2), 0.0, 1.0)
    weights = gaussian(key_of[1], (RUNS,), (4.0 / RUNS ** 0.5), 0.06629126, ((0, 256),), jnp.float32)
    hw_points = jnp.clip(1.0 * jax.random.uniform(key_of[2], (F, HW), jnp.float32) ** level_of(key_of[2], (F, HW), ((1, 256),), -0.2, 0.2), 0.0, 1.0)
    high_values = gaussian(key_of[3], (HW,), 1.0, 6.0, ((0, 256),), jnp.float32)
    len_low = jnp.clip(jnp.exp(jax.random.uniform(key_of[4], (F,), jnp.float32, math.log(0.6), math.log(3.0))), 0.6, 3.0)
    len_high = jnp.clip(jnp.exp(jax.random.uniform(key_of[5], (F,), jnp.float32, math.log(0.6), math.log(3.0))), 0.6, 3.0)
    rho = jnp.clip(jax.random.uniform(key_of[6], (1,), jnp.float32, 0.5, 1.5), 0.5, 1.5)
    noise = jnp.clip(jax.random.uniform(key_of[7], (1,), jnp.float32, 0.3, 1.0), 0.3, 1.0)
    return dict(sim_points=sim_points, weights=weights, hw_points=hw_points, high_values=high_values, len_low=len_low, len_high=len_high, rho=rho, noise=noise)


def kernel_apply(row_pts, col_pts, col_norms, vector):
    feats, count = row_pts.shape
    block = 512 if count % 512 == 0 else count
    stacked = jnp.moveaxis(row_pts.reshape(feats, count // block, block), 1, 0)

    def single(piece):
        norms = jnp.sum(piece * piece, axis=0)
        cross = lax.dot_general(piece, col_pts, (((0,), (0,)), ((), ())), precision=lax.Precision.HIGHEST, preferred_element_type=jnp.float32)
        dist = norms[:, None] + col_norms[None, :] - 2.0 * cross
        return jnp.dot(jnp.exp(-0.5 * dist), vector, precision=lax.Precision.HIGHEST, preferred_element_type=jnp.float32)

    return lax.map(single, stacked).reshape(count)


def reference(sim_points, weights, hw_points, high_values, len_low, len_high, rho, noise):
    runs_scaled = sim_points / len_low[:, None]
    runs_norms = jnp.sum(runs_scaled * runs_scaled, axis=0)
    mu_low = kernel_apply(hw_points / len_low[:, None], runs_scaled, runs_norms, weights)
    target = high_values - rho[0] * mu_low
    high_scaled = hw_points / len_high[:, None]
    high_norms = jnp.sum(high_scaled * high_scaled, axis=0)
    solution = jnp.zeros_like(target)
    residual = target
    direction = target
    norm_now = jnp.sum(residual * residual)
    for step in range(ITERS):
        image = kernel_apply(high_scaled, high_scaled, high_norms, direction) + noise[0] * direction
        alpha = norm_now / jnp.sum(direction * image)
        solution = solution + alpha * direction
        residual = residual - alpha * image
        norm_next = jnp.sum(residual * residual)
        direction = residual + (norm_next / norm_now) * direction
        norm_now = norm_next
    return mu_low, solution, residual
```

```python
import math

import jax
import jax.numpy as jnp
from jax import lax
from jax.experimental import pallas as pl
from jax.experimental.pallas import tpu as pltpu
from jax.sharding import PartitionSpec as P

F32 = jnp.float32
BF16 = jnp.bfloat16
FEATS = 24
LANES = 128
DEPTH = 160
ROOT = math.sqrt(math.log2(math.e))
VMEM = pl.BlockSpec(memory_space=pltpu.VMEM)
SMEM = pl.BlockSpec(memory_space=pltpu.SMEM)


def params(mib):
    return pltpu.CompilerParams(vmem_limit_bytes=mib * 1024 * 1024)


def shape(dims, kind=F32):
    return jax.ShapeDtypeStruct(dims, kind)


def split(x):
    high = x.astype(BF16).astype(F32)
    rest = x - high
    mid = rest.astype(BF16).astype(F32)
    return high, mid, rest - mid


def norm_rows(norm, at):
    high, mid, low = split(norm)
    row = lax.broadcasted_iota(jnp.int32, (8, norm.shape[1]), 0)
    ones = jnp.where((row >= 3 - at) & (row < 6 - at), 1.0, 0.0)
    return jnp.where(row == at, high, jnp.where(row == at + 1, mid, jnp.where(row == at + 2, low, ones)))


def scaled(points, scale):
    return (points - 0.5) * scale


def half_norm(points):
    return -0.5 * jnp.sum(points * points, axis=0, keepdims=True)


def left(points, scale):
    u = scaled(points, scale)
    high, mid, low = split(u)
    norms = norm_rows(half_norm(u), 0)
    return jnp.concatenate([high, high, high, mid, mid, low, norms, jnp.zeros_like(norms)], 0).astype(BF16)


def right(points, scale):
    v = scaled(points, scale)
    high, mid, low = split(v)
    norms = norm_rows(half_norm(v), 3)
    return jnp.concatenate([high, mid, low, high, mid, high, norms, jnp.zeros_like(norms)], 0)


def pack_kernel(runs, weights, points, len_low, len_high, out_row, out_sim, scale_low, scale_high):
    row = lax.broadcasted_iota(jnp.int32, (FEATS, LANES), 0)
    for lengths, out in ((len_low, scale_low), (len_high, scale_high)):
        column = jnp.ones((FEATS, LANES), F32)
        for i in range(FEATS):
            column = jnp.where(row == i, lengths[i], column)
        out[...] = ROOT / column
    own = points[...]
    for i in range(out_row.shape[0]):
        out_row[i, :FEATS, :512] = runs[...]
        out_row[i, FEATS:, :512] = jnp.broadcast_to(weights[...], (8, 512))
        out_row[i, :FEATS, 512:] = own
        out_row[i, FEATS:, 512:] = jnp.zeros((8, LANES), F32)
    for i in range(out_sim.shape[0]):
        out_sim[i] = own


def prep_kernel(held, scale_low, scale_high, runs_out, cols_out, weights_out):
    wide = jnp.concatenate([scale_low[...]] * 4, 1)

    def step(r, carry):
        parts = right(held[r, :FEATS, :512], wide)
        for q in range(4):
            lanes = slice(q * LANES, (q + 1) * LANES)
            rows = pl.ds(pl.multiple_of(r * 512 + q * LANES, LANES), LANES)
            runs_out[rows, :] = parts[:, lanes].T.astype(BF16)
            weights_out[rows, :] = jnp.broadcast_to(held[r, FEATS : FEATS + 1, lanes], (LANES, LANES)).T
        rows = pl.ds(pl.multiple_of(r * LANES, LANES), LANES)
        cols_out[rows, :] = right(held[r, :FEATS, 512:], scale_high[...]).T.astype(BF16)
        return carry

    lax.fori_loop(0, held.shape[0], step, 0)


def build_left(points, scale, out):
    def step(g, carry):
        for q in range(8):
            k = g * 8 + q
            out[:, pl.ds(pl.multiple_of(k * LANES, LANES), LANES)] = left(points[k], scale[...])
        return carry

    lax.fori_loop(0, points.shape[0] // 8, step, 0)


def mu_kernel(points, scale, runs, weights, high, rho, at, out, parts, total):
    build_left(points, scale, parts)
    wide, chunk = 512, 512

    def step(c, carry):
        u = parts[:, pl.ds(pl.multiple_of(c * wide, wide), wide)]
        acc = jnp.zeros((8, wide), F32)
        for j in range(0, runs.shape[0], chunk):
            power = jnp.dot(runs[j : j + chunk, :], u, preferred_element_type=F32)
            w = weights[j : j + chunk, :]
            term = jnp.exp2(power) * jnp.concatenate([w] * (wide // LANES), 1)
            acc = acc + jnp.sum(term.reshape(chunk // 8, 8, wide), axis=0)
        line = jnp.sum(acc, axis=0, keepdims=True)
        for q in range(wide // LANES):
            total[pl.ds(c * (wide // LANES) + q, 1), :] = line[:, q * LANES : (q + 1) * LANES]
        return carry

    lax.fori_loop(0, parts.shape[1] // wide, step, 0)
    mu = total[...]
    row = lax.broadcasted_iota(jnp.int32, mu.shape, 0)
    target = -rho[0] * mu
    target = jnp.where(row == at[0], target + high[...], target)
    for i in range(out.shape[0]):
        out[i] = jnp.where(row == i, mu, target)


def tile_kernel(points, scale, cols, out, parts):
    build_left(points, scale, parts)
    wide, chunk = 512, 512

    def step(c, carry):
        lanes = pl.ds(pl.multiple_of(c * wide, wide), wide)
        u = parts[:, lanes]
        for j in range(0, cols.shape[0], chunk):
            power = jnp.dot(cols[j : j + chunk, :], u, preferred_element_type=F32)
            out[j : j + chunk, lanes] = jnp.exp2(power)
        return carry

    lax.fori_loop(0, parts.shape[1] // wide, step, 0)


def first_kernel(held, tile, high, rho, noise, at, out, target_out, mu_out, cols):
    total = jnp.sum(held[...], axis=0)
    row = lax.broadcasted_iota(jnp.int32, total.shape, 0)
    own = row == at[0]
    target = jnp.where(own, high[...] - rho[0] * total, total)
    target_out[...] = target
    mu_out[...] = jnp.sum(jnp.where(own, total, 0.0), axis=0, keepdims=True)
    own_target = jnp.sum(jnp.where(own, target, 0.0), axis=0, keepdims=True)

    def step(k, carry):
        rows = pl.ds(pl.multiple_of(k * LANES, LANES), LANES)
        acc = jnp.zeros((LANES, LANES), F32)
        for s in range(held.shape[1]):
            acc = acc + tile[rows, s * LANES : (s + 1) * LANES] * target_out[s : s + 1, :]
        cols[pl.ds(k, 1), :] = jnp.sum(acc.T, axis=0, keepdims=True)
        return carry

    lax.fori_loop(0, cols.shape[0], step, 0)
    image = cols[...]
    image = jnp.where(lax.broadcasted_iota(jnp.int32, image.shape, 0) == at[1], image + noise[0] * own_target, image)
    for i in range(out.shape[0]):
        out[i] = image


def second_kernel(held, tile, noise, at, out, column, rows_out):
    image = jnp.sum(held[...], axis=0)
    mine = lax.broadcasted_iota(jnp.int32, image.shape, 0) == at[1]
    own = jnp.sum(jnp.where(mine, image, 0.0), axis=0, keepdims=True)
    for k in range(image.shape[0]):
        column[k * LANES : (k + 1) * LANES, :] = jnp.broadcast_to(image[k : k + 1, :], (LANES, LANES)).T

    def step(s, carry):
        lanes = pl.ds(pl.multiple_of(s * 2 * LANES, 2 * LANES), 2 * LANES)
        acc = jnp.zeros((8, 2 * LANES), F32)
        for k in range(image.shape[0]):
            rows = slice(k * LANES, (k + 1) * LANES)
            c = column[rows, :]
            term = tile[rows, lanes] * jnp.concatenate([c, c], 1)
            acc = acc + jnp.sum(term.reshape(LANES // 8, 8, 2 * LANES), axis=0)
        line = jnp.sum(acc, axis=0, keepdims=True)
        for q in range(2):
            rows_out[pl.ds(s * 2 + q, 1), :] = line[:, q * LANES : (q + 1) * LANES]
        return carry

    lax.fori_loop(0, rows_out.shape[0] // 2, step, 0)
    total = rows_out[...]
    row = lax.broadcasted_iota(jnp.int32, total.shape, 0)
    total = jnp.where(row == at[0], total + noise[0] * own, total)
    extra = jnp.broadcast_to(own, (8, LANES))
    for i in range(out.shape[0]):
        out[i, : total.shape[0], :] = total
        out[i, total.shape[0] :, :] = extra


def two_sum(a, b):
    s = a + b
    t = s - a
    return s, (a - (s - t)) + (b - t)


def pair_add(x, y):
    s, e = two_sum(x[0], y[0])
    return two_sum(s, e + (x[1] + y[1]))


def product(a, b):
    ah = a.astype(BF16).astype(F32)
    bh = b.astype(BF16).astype(F32)
    al, bl = a - ah, b - bh
    s, e = two_sum(ah * bh, ah * bl + al * bh)
    return two_sum(s, e + al * bl)


def pair_product(x, y):
    s, e = product(x[0], y[0])
    return two_sum(s, e + (x[0] * y[1] + x[1] * y[0]))


def minus(x):
    return -x[0], -x[1]


def pair_ratio(x, y):
    q = x[0] / y[0]
    rest = pair_add(x, minus(pair_product((q, jnp.zeros_like(q)), y)))
    return two_sum(q, (rest[0] + rest[1]) / y[0])


def fold_rows(x):
    high, low = x
    count = high.shape[0]
    while count > 8:
        count //= 2
        high, low = pair_add((high[:count], low[:count]), (high[count:], low[count:]))
    return high, low


def moments_kernel(held, target, at, out, own_out):
    count = target.shape[0]
    last = jnp.sum(held[:, :count, :], axis=0)
    image = held[:, count, :]
    b = target[...]
    for i, (p, q) in enumerate(((b, b), (b, image), (image, image), (image, last))):
        high, low = fold_rows(product(p, q))
        for shift in (4, 2, 1):
            high, low = pair_add((high, low), (pltpu.roll(high, shift, 0), pltpu.roll(low, shift, 0)))
        for j in range(out.shape[0]):
            out[j, 2 * i : 2 * i + 1, :] = high[:1]
            out[j, 2 * i + 1 : 2 * i + 2, :] = low[:1]
    own = lax.broadcasted_iota(jnp.int32, b.shape, 0) == at[0]
    for i, v in enumerate((b, image, last)):
        own_out[i : i + 1, :] = jnp.sum(jnp.where(own, v, 0.0), axis=0, keepdims=True)


def final_kernel(held, own, x_out, r_out):
    sums = []
    for i in range(4):
        h = jnp.concatenate([held[j, 2 * i : 2 * i + 1, :] for j in range(held.shape[0])], 0)
        l = jnp.concatenate([held[j, 2 * i + 1 : 2 * i + 2, :] for j in range(held.shape[0])], 0)
        for axis, shifts in ((0, (4, 2, 1)), (1, (64, 32, 16, 8, 4, 2, 1))):
            for shift in shifts:
                h, l = pair_add((h, l), (pltpu.roll(h, shift, axis), pltpu.roll(l, shift, axis)))
        sums.append((h[:1], l[:1]))
    m0, m1, m2, m3 = sums
    alpha = pair_ratio(m0, m1)
    ratio = pair_ratio(m2, m1)
    v1 = pair_add(m2, minus(pair_product(m1, pair_ratio(m1, m0))))
    v2 = pair_add(m3, minus(pair_product(m2, ratio)))
    scale = pair_product(alpha, ratio)
    alpha0, grow = alpha[0], scale[0]
    alpha1 = (v1[0] + v1[1]) / (v2[0] + v2[1])
    b, image, last = own[0:1, :], own[1:2, :], own[2:3, :]
    x_out[...] = alpha0 * b + alpha1 * (grow * b - alpha0 * image)
    r_out[...] = (b - alpha0 * image) - alpha1 * (grow * image - alpha0 * last)


def exchange(blocks, axes):
    return lax.all_to_all(blocks, axes, 0, 0, tiled=True)


def local(runs, weights, points, high, len_low, len_high, rho, noise):
    n_row, n_sim = lax.axis_size("row"), lax.axis_size("sim")
    at = jnp.stack([lax.axis_index("sim"), lax.axis_index("row")]).astype(jnp.int32)
    high = high.reshape(1, LANES)
    n_runs = n_row * 512
    n_cols = n_row * LANES
    n_rows = n_sim * LANES
    to_row, to_sim, scale_low, scale_high = pl.pallas_call(
        pack_kernel,
        out_shape=(shape((n_row, 32, 640)), shape((n_sim, FEATS, LANES)), shape((FEATS, LANES)), shape((FEATS, LANES))),
        in_specs=[VMEM, VMEM, VMEM, SMEM, SMEM],
        out_specs=(VMEM,) * 4,
        compiler_params=params(16),
        name="pack",
    )(runs, weights.reshape(1, 512), points, len_low, len_high)
    by_row = exchange(to_row, "row")
    by_sim = exchange(to_sim, "sim")
    run_parts, col_parts, weight_cols = pl.pallas_call(
        prep_kernel,
        out_shape=(shape((n_runs, DEPTH), BF16), shape((n_cols, DEPTH), BF16), shape((n_runs, LANES))),
        in_specs=[VMEM] * 3,
        out_specs=(VMEM,) * 3,
        compiler_params=params(20),
        name="prep",
    )(by_row, scale_low, scale_high)
    mu_terms = pl.pallas_call(
        mu_kernel,
        out_shape=shape((n_sim, n_sim, LANES)),
        in_specs=[VMEM] * 5 + [SMEM] * 2,
        out_specs=VMEM,
        scratch_shapes=[pltpu.VMEM((DEPTH, n_rows), BF16), pltpu.VMEM((n_sim, LANES), F32)],
        compiler_params=params(24),
        name="mu",
    )(by_sim, scale_low, run_parts, weight_cols, high, rho, at)
    mu_held = exchange(mu_terms, "sim")
    tile = pl.pallas_call(
        tile_kernel,
        out_shape=shape((n_cols, n_rows)),
        in_specs=[VMEM] * 3,
        out_specs=VMEM,
        scratch_shapes=[pltpu.VMEM((DEPTH, n_rows), BF16)],
        compiler_params=params(28),
        name="tile",
    )(by_sim, scale_high, col_parts)
    image_terms, target, mu = pl.pallas_call(
        first_kernel,
        out_shape=(shape((n_row, n_row, LANES)), shape((n_sim, LANES)), shape((1, LANES))),
        in_specs=[VMEM] * 3 + [SMEM] * 3,
        out_specs=(VMEM,) * 3,
        scratch_shapes=[pltpu.VMEM((n_row, LANES), F32)],
        compiler_params=params(28),
        name="first",
    )(mu_held, tile, high, rho, noise, at)
    image_held = exchange(image_terms, "row")
    last_terms = pl.pallas_call(
        second_kernel,
        out_shape=shape((n_sim, n_sim + 8, LANES)),
        in_specs=[VMEM] * 2 + [SMEM] * 2,
        out_specs=VMEM,
        scratch_shapes=[pltpu.VMEM((n_cols, LANES), F32), pltpu.VMEM((n_sim, LANES), F32)],
        compiler_params=params(28),
        name="second",
    )(image_held, tile, noise, at)
    last_held = exchange(last_terms, "sim")
    moments, own = pl.pallas_call(
        moments_kernel,
        out_shape=(shape((n_row, 8, LANES)), shape((8, LANES))),
        in_specs=[VMEM] * 2 + [SMEM],
        out_specs=(VMEM,) * 2,
        compiler_params=params(16),
        name="moments",
    )(last_held, target, at)
    moments_held = exchange(moments, "row")
    x, r = pl.pallas_call(
        final_kernel,
        out_shape=(shape((1, LANES)), shape((1, LANES))),
        in_specs=[VMEM] * 2,
        out_specs=(VMEM,) * 2,
        compiler_params=params(16),
        name="final",
    )(moments_held, own)
    return mu.reshape(LANES), x.reshape(LANES), r.reshape(LANES)


def solution(mesh):
    placed = (
        P(None, ("row", "sim")),
        P(("row", "sim")),
        P(None, ("row", "sim")),
        P(("row", "sim")),
        P(),
        P(),
        P(),
        P(),
    )
    return jax.shard_map(
        local,
        mesh=mesh,
        in_specs=placed,
        out_specs=(P(("row", "sim")), P(("row", "sim")), P(("row", "sim"))),
        check_vma=False,
    )
```

```python
import math

import jax
import jax.numpy as jnp
from jax import lax
from jax.experimental import pallas as pl
from jax.experimental.pallas import tpu as pltpu
from jax.sharding import Mesh
from jax.sharding import PartitionSpec as P

F32 = jnp.float32
BF16 = jnp.bfloat16
FEATS = 24
LANES = 128
RUN_BLOCKS = 4
WIDE = CHUNK = 512
PACKED = RUN_BLOCKS * FEATS + FEATS + 8
DEPTH = 160
ROOT = math.sqrt(math.log2(math.e))
VMEM = pl.BlockSpec(memory_space=pltpu.VMEM)
AXES = ("y", "core", "x", "z")
ROWS = ("core", "z")
COLS = ("y", "x")
HBM = pl.BlockSpec(memory_space=pltpu.HBM)
SMEM = pl.BlockSpec(memory_space=pltpu.SMEM)


def params(mib):
    return pltpu.CompilerParams(vmem_limit_bytes=mib * 1024 * 1024)


def shape(dims, kind=F32):
    return jax.ShapeDtypeStruct(dims, kind)


def split(x):
    high = x.astype(BF16).astype(F32)
    rest = x - high
    mid = rest.astype(BF16).astype(F32)
    return high, mid, rest - mid


def norm_rows(norm, at):
    high, mid, low = split(norm)
    row = lax.broadcasted_iota(jnp.int32, (8, norm.shape[1]), 0)
    ones = jnp.where((row >= 3 - at) & (row < 6 - at), 1.0, 0.0)
    return jnp.where(row == at, high, jnp.where(row == at + 1, mid, jnp.where(row == at + 2, low, ones)))


def scaled(points, scale):
    return (points - 0.5) * scale


def half_norm(points):
    return -0.5 * jnp.sum(points * points, axis=0, keepdims=True)


def left(points, scale):
    u = scaled(points, scale)
    high, mid, low = split(u)
    norms = norm_rows(half_norm(u), 0)
    return jnp.concatenate([high, high, high, mid, mid, low, norms, jnp.zeros_like(norms)], 0).astype(BF16)


def right(points, scale):
    v = scaled(points, scale)
    high, mid, low = split(v)
    norms = norm_rows(half_norm(v), 3)
    return jnp.concatenate([high, mid, low, high, mid, high, norms, jnp.zeros_like(norms)], 0)


def pack_kernel(*refs):
    sources, (out_col, out_row, scale_low, scale_high), held, sems = refs[:5], refs[5:9], refs[9:14], refs[14]
    copies = [pltpu.make_async_copy(a, b, sems.at[i]) for i, (a, b) in enumerate(zip(sources, held))]
    for copy in copies:
        copy.start()
    for copy in copies:
        copy.wait()
    runs, weights, points, len_low, len_high = held
    row = lax.broadcasted_iota(jnp.int32, (FEATS, LANES), 0)
    for lengths, out in ((len_low, scale_low), (len_high, scale_high)):
        column = jnp.ones((FEATS, LANES), F32)
        for i in range(FEATS):
            column = jnp.where(row == i, lengths[i], column)
        out[...] = ROOT / column
    own = points[...]
    for i in range(out_row.shape[0]):
        out_row[i] = own
    last = jnp.broadcast_to(weights[:, :LANES], (8, LANES))
    row = lax.broadcasted_iota(jnp.int32, (8, LANES), 0)
    for q in range(1, RUN_BLOCKS):
        last = jnp.where(row == q, weights[:, q * LANES : (q + 1) * LANES], last)
    for i in range(out_col.shape[0]):
        for q in range(RUN_BLOCKS):
            out_col[i, q * FEATS : (q + 1) * FEATS, :] = runs[:, q * LANES : (q + 1) * LANES]
        out_col[i, RUN_BLOCKS * FEATS : PACKED - 8, :] = own
        out_col[i, PACKED - 8 :, :] = last


def prep_kernel(held, scale_low, scale_high, runs_out, cols_out, weights_out):
    def step(r, carry):
        for q in range(RUN_BLOCKS):
            rows = pl.ds(pl.multiple_of((r * RUN_BLOCKS + q) * LANES, LANES), LANES)
            runs_out[rows, :] = right(held[r, q * FEATS : (q + 1) * FEATS, :], scale_low[...]).T.astype(BF16)
        weights_out[pl.ds(pl.multiple_of(r * 8, 8), 8), :] = held[r, PACKED - 8 :, :]
        rows = pl.ds(pl.multiple_of(r * LANES, LANES), LANES)
        cols_out[rows, :] = right(held[r, RUN_BLOCKS * FEATS : PACKED - 8, :], scale_high[...]).T.astype(BF16)
        return carry

    lax.fori_loop(0, held.shape[0], step, 0)


def column_of(line, out, rows):
    out[rows, :] = jnp.broadcast_to(line, (LANES, LANES)).T


def weighted(cols, rows, column):
    term = jnp.exp2(jnp.dot(cols, rows, preferred_element_type=F32))
    count, wide = term.shape
    term = term * jnp.concatenate([column] * (wide // LANES), 1)
    return jnp.sum(term.reshape(count // 8, 8, wide), axis=0)


def build_left(points, scale, out):
    def step(g, carry):
        for q in range(8):
            k = g * 8 + q
            out[:, pl.ds(pl.multiple_of(k * LANES, LANES), LANES)] = left(points[k], scale[...])
        return carry

    lax.fori_loop(0, points.shape[0] // 8, step, 0)


def mu_kernel(points, scale, runs_hbm, weights, high, rho, at, out, parts, runs, column, total, sems):
    pieces = sems.shape[0]
    size = runs.shape[0] // pieces
    blocks = size // (RUN_BLOCKS * LANES)

    def copy(i):
        rows = pl.ds(pl.multiple_of(i * size, size), size)
        return pltpu.make_async_copy(runs_hbm.at[rows, :], runs.at[rows, :], sems.at[i])

    for i in range(pieces):
        copy(i).start()
    build_left(points, scale, parts)
    total[...] = jnp.zeros_like(total)

    def step(i, carry):
        copy(i).wait()
        for r in range(blocks):
            lines = weights[pl.ds(pl.multiple_of((i * blocks + r) * 8, 8), 8), :]
            for q in range(RUN_BLOCKS):
                first = (r * RUN_BLOCKS + q) * LANES
                column_of(lines[q : q + 1, :], column, slice(first, first + LANES))
        for c in range(0, parts.shape[1], WIDE):
            acc = total[:, c : c + WIDE]
            for j in range(0, size, CHUNK):
                rows = pl.ds(pl.multiple_of(i * size + j, CHUNK), CHUNK)
                acc = acc + weighted(runs[rows, :], parts[:, c : c + WIDE], column[j : j + CHUNK, :])
            total[:, c : c + WIDE] = acc
        return carry

    lax.fori_loop(0, pieces, step, 0)
    mu = lines_of(total)
    row = lax.broadcasted_iota(jnp.int32, mu.shape, 0)
    target = -rho[0] * mu
    target = jnp.where(row == at[0], target + high[...], target)
    for i in range(out.shape[0]):
        out[i] = jnp.where(row == i, mu, target)


def lines_of(total):
    line = jnp.sum(total[...], axis=0, keepdims=True)
    return jnp.concatenate([line[:, k : k + LANES] for k in range(0, line.shape[1], LANES)], 0)


def sides_kernel(points, scale, out):
    build_left(points, scale, out)


def first_kernel(held, rows_in, cols_in, high, rho, noise, at, out, target_out, mu_out, sums):
    total = jnp.sum(held[...], axis=0)
    row = lax.broadcasted_iota(jnp.int32, total.shape, 0)
    own = row == at[0]
    target = jnp.where(own, high[...] - rho[0] * total, total)
    target_out[...] = target
    mu_out[...] = jnp.sum(jnp.where(own, total, 0.0), axis=0, keepdims=True)
    own_target = jnp.sum(jnp.where(own, target, 0.0), axis=0, keepdims=True)
    size = 2 * LANES

    def step(k, carry):
        cols = cols_in[pl.ds(pl.multiple_of(k * size, size), size), :]
        acc = jnp.zeros((size, LANES), F32)
        for c in range(0, rows_in.shape[1], WIDE):
            term = jnp.exp2(jnp.dot(cols, rows_in[:, c : c + WIDE], preferred_element_type=F32))
            for q in range(0, WIDE, LANES):
                s = (c + q) // LANES
                acc = acc + term[:, q : q + LANES] * target_out[s : s + 1, :]
        for q in range(2):
            block = acc[q * LANES : (q + 1) * LANES, :]
            sums[pl.ds(k * 2 + q, 1), :] = jnp.sum(block.T, axis=0, keepdims=True)
        return carry

    lax.fori_loop(0, cols_in.shape[0] // size, step, 0)
    image = sums[...]
    image = jnp.where(lax.broadcasted_iota(jnp.int32, image.shape, 0) == at[1], image + noise[0] * own_target, image)
    for i in range(out.shape[0]):
        out[i] = image


def second_kernel(held, rows_in, cols_in, noise, at, out, column, total):
    image = jnp.sum(held[...], axis=0)
    mine = lax.broadcasted_iota(jnp.int32, image.shape, 0) == at[1]
    own = jnp.sum(jnp.where(mine, image, 0.0), axis=0, keepdims=True)
    for k in range(image.shape[0]):
        column_of(image[k : k + 1, :], column, slice(k * LANES, (k + 1) * LANES))
    total[...] = jnp.zeros_like(total)

    def step(i, carry):
        rows = pl.ds(pl.multiple_of(i * CHUNK, CHUNK), CHUNK)
        for c in range(0, rows_in.shape[1], WIDE):
            total[:, c : c + WIDE] += weighted(cols_in[rows, :], rows_in[:, c : c + WIDE], column[rows, :])
        return carry

    lax.fori_loop(0, cols_in.shape[0] // CHUNK, step, 0)
    last = lines_of(total)
    row = lax.broadcasted_iota(jnp.int32, last.shape, 0)
    last = jnp.where(row == at[0], last + noise[0] * own, last)
    extra = jnp.broadcast_to(own, (8, LANES))
    for i in range(out.shape[0]):
        out[i, : last.shape[0], :] = last
        out[i, last.shape[0] :, :] = extra


def two_sum(a, b):
    s = a + b
    t = s - a
    return s, (a - (s - t)) + (b - t)


def pair_add(x, y):
    s, e = two_sum(x[0], y[0])
    return two_sum(s, e + (x[1] + y[1]))


def product(a, b):
    ah = a.astype(BF16).astype(F32)
    bh = b.astype(BF16).astype(F32)
    al, bl = a - ah, b - bh
    s, e = two_sum(ah * bh, ah * bl + al * bh)
    return two_sum(s, e + al * bl)


def pair_product(x, y):
    s, e = product(x[0], y[0])
    return two_sum(s, e + (x[0] * y[1] + x[1] * y[0]))


def minus(x):
    return -x[0], -x[1]


def pair_ratio(x, y):
    q = x[0] / y[0]
    rest = pair_add(x, minus(pair_product((q, jnp.zeros_like(q)), y)))
    return two_sum(q, (rest[0] + rest[1]) / y[0])


def fold_rows(x):
    high, low = x
    count = high.shape[0]
    while count > 8:
        count //= 2
        high, low = pair_add((high[:count], low[:count]), (high[count:], low[count:]))
    return high, low


def moments_kernel(held, target, at, out, own_out):
    count = target.shape[0]
    last = jnp.sum(held[:, :count, :], axis=0)
    image = held[:, count, :]
    b = target[...]
    for i, (p, q) in enumerate(((b, b), (b, image), (image, image), (image, last))):
        high, low = fold_rows(product(p, q))
        for shift in (4, 2, 1):
            high, low = pair_add((high, low), (pltpu.roll(high, shift, 0), pltpu.roll(low, shift, 0)))
        for j in range(out.shape[0]):
            out[j, 2 * i : 2 * i + 1, :] = high[:1]
            out[j, 2 * i + 1 : 2 * i + 2, :] = low[:1]
    own = lax.broadcasted_iota(jnp.int32, b.shape, 0) == at[0]
    for i, v in enumerate((b, image, last)):
        own_out[i : i + 1, :] = jnp.sum(jnp.where(own, v, 0.0), axis=0, keepdims=True)


def final_kernel(held, own, x_out, r_out):
    sums = []
    for i in range(4):
        h = jnp.concatenate([held[j, 2 * i : 2 * i + 1, :] for j in range(held.shape[0])], 0)
        l = jnp.concatenate([held[j, 2 * i + 1 : 2 * i + 2, :] for j in range(held.shape[0])], 0)
        h, l = fold_rows((h, l))
        for axis, shifts in ((0, (4, 2, 1)), (1, (64, 32, 16, 8, 4, 2, 1))):
            for shift in shifts:
                h, l = pair_add((h, l), (pltpu.roll(h, shift, axis), pltpu.roll(l, shift, axis)))
        sums.append((h[:1], l[:1]))
    m0, m1, m2, m3 = sums
    alpha = pair_ratio(m0, m1)
    ratio = pair_ratio(m2, m1)
    v1 = pair_add(m2, minus(pair_product(m1, pair_ratio(m1, m0))))
    v2 = pair_add(m3, minus(pair_product(m2, ratio)))
    scale = pair_product(alpha, ratio)
    alpha0, grow = alpha[0], scale[0]
    alpha1 = (v1[0] + v1[1]) / (v2[0] + v2[1])
    b, image, last = own[0:1, :], own[1:2, :], own[2:3, :]
    x_out[...] = alpha0 * b + alpha1 * (grow * b - alpha0 * image)
    r_out[...] = (b - alpha0 * image) - alpha1 * (grow * image - alpha0 * last)


def exchange(blocks, axes):
    return lax.all_to_all(blocks, axes, 0, 0, tiled=True)


def local(runs, weights, points, high, len_low, len_high, rho, noise):
    n_row, n_col = lax.axis_size(ROWS), lax.axis_size(COLS)
    at = jnp.stack([lax.axis_index(ROWS), lax.axis_index(COLS)]).astype(jnp.int32)
    high = high.reshape(1, LANES)
    runs_len, cols_len, rows_len = n_col * RUN_BLOCKS * LANES, n_col * LANES, n_row * LANES
    to_col, to_row, scale_low, scale_high = pl.pallas_call(
        pack_kernel,
        out_shape=(shape((n_col, PACKED, LANES)), shape((n_row, FEATS, LANES)), shape((FEATS, LANES)), shape((FEATS, LANES))),
        in_specs=[HBM] * 5,
        out_specs=(VMEM,) * 4,
        scratch_shapes=[
            pltpu.VMEM((FEATS, RUN_BLOCKS * LANES), F32),
            pltpu.VMEM((1, RUN_BLOCKS * LANES), F32),
            pltpu.VMEM((FEATS, LANES), F32),
            pltpu.SMEM((FEATS,), F32),
            pltpu.SMEM((FEATS,), F32),
            pltpu.SemaphoreType.DMA((5,)),
        ],
        compiler_params=params(60),
        name="pack",
    )(runs, weights.reshape(1, RUN_BLOCKS * LANES), points, len_low, len_high)
    by_col = exchange(to_col, COLS)
    by_row = exchange(to_row, ROWS)
    run_parts, col_parts, weight_lines = pl.pallas_call(
        prep_kernel,
        out_shape=(shape((runs_len, DEPTH), BF16), shape((cols_len, DEPTH), BF16), shape((n_col * 8, LANES))),
        in_specs=[VMEM] * 3,
        out_specs=(VMEM,) * 3,
        compiler_params=params(60),
        name="prep",
    )(by_col, scale_low, scale_high)
    mu_terms = pl.pallas_call(
        mu_kernel,
        out_shape=shape((n_row, n_row, LANES)),
        in_specs=[VMEM, VMEM, HBM, VMEM, VMEM, SMEM, SMEM],
        out_specs=VMEM,
        scratch_shapes=[
            pltpu.VMEM((DEPTH, rows_len), BF16),
            pltpu.VMEM((runs_len, DEPTH), BF16),
            pltpu.VMEM((runs_len // 8, LANES), F32),
            pltpu.VMEM((8, rows_len), F32),
            pltpu.SemaphoreType.DMA((8,)),
        ],
        compiler_params=params(60),
        name="mu",
    )(by_row, scale_low, run_parts, weight_lines, high, rho, at)
    mu_held = exchange(mu_terms, ROWS)
    row_parts = pl.pallas_call(
        sides_kernel,
        out_shape=shape((DEPTH, rows_len), BF16),
        in_specs=[VMEM] * 2,
        out_specs=VMEM,
        compiler_params=params(4),
        name="sides",
    )(by_row, scale_high)
    image_terms, target, mu = pl.pallas_call(
        first_kernel,
        out_shape=(shape((n_col, n_col, LANES)), shape((n_row, LANES)), shape((1, LANES))),
        in_specs=[VMEM] * 4 + [SMEM] * 3,
        out_specs=(VMEM,) * 3,
        scratch_shapes=[pltpu.VMEM((n_col, LANES), F32)],
        compiler_params=params(4),
        name="first",
    )(mu_held, row_parts, col_parts, high, rho, noise, at)
    image_held = exchange(image_terms, COLS)
    last_terms = pl.pallas_call(
        second_kernel,
        out_shape=shape((n_row, n_row + 8, LANES)),
        in_specs=[VMEM] * 3 + [SMEM] * 2,
        out_specs=VMEM,
        scratch_shapes=[pltpu.VMEM((cols_len, LANES), F32), pltpu.VMEM((8, rows_len), F32)],
        compiler_params=params(8),
        name="second",
    )(image_held, row_parts, col_parts, noise, at)
    last_held = exchange(last_terms, ROWS)
    moments, own = pl.pallas_call(
        moments_kernel,
        out_shape=(shape((n_col, 8, LANES)), shape((8, LANES))),
        in_specs=[VMEM] * 2 + [SMEM],
        out_specs=(VMEM,) * 2,
        compiler_params=params(4),
        name="moments",
    )(last_held, target, at)
    moments_held = exchange(moments, COLS)
    x, r = pl.pallas_call(
        final_kernel,
        out_shape=(shape((1, LANES)), shape((1, LANES))),
        in_specs=[VMEM] * 2,
        out_specs=(VMEM,) * 2,
        compiler_params=params(4),
        name="final",
    )(moments_held, own)
    return mu.reshape(LANES), x.reshape(LANES), r.reshape(LANES)


def solution(mesh):
    spread = P(AXES)
    wide = P(None, AXES)
    fine = Mesh(mesh.devices.reshape(4, 2, 4, 8), AXES)
    return jax.shard_map(
        local,
        mesh=fine,
        in_specs=(wide, spread, wide, spread, P(), P(), P(), P()),
        out_specs=(spread,) * 3,
        check_vma=False,
    )
```

```python
import math

import jax
import jax.numpy as jnp
from jax import lax
from jax.experimental import pallas as pl
from jax.experimental.pallas import tpu as pltpu
from jax.sharding import Mesh
from jax.sharding import PartitionSpec as P

F32 = jnp.float32
BF16 = jnp.bfloat16
FEATS = 24
LANES = 128
RUN_BLOCKS = 4
WIDE = CHUNK = 512
MU_CHUNK = 1024
PACKED = RUN_BLOCKS * FEATS + FEATS + 8
DEPTH = 160
ROOT = math.sqrt(math.log2(math.e))
VMEM = pl.BlockSpec(memory_space=pltpu.VMEM)
AXES = ("y", "core", "x", "z")
ROWS = ("core", "z")
COLS = ("y", "x")
HBM = pl.BlockSpec(memory_space=pltpu.HBM)
SMEM = pl.BlockSpec(memory_space=pltpu.SMEM)


def params(mib):
    return pltpu.CompilerParams(vmem_limit_bytes=mib * 1024 * 1024)


def shape(dims, kind=F32):
    return jax.ShapeDtypeStruct(dims, kind)


def split(x):
    high = x.astype(BF16).astype(F32)
    rest = x - high
    mid = rest.astype(BF16).astype(F32)
    return high, mid, rest - mid


def norm_rows(norm, at):
    high, mid, low = split(norm)
    row = lax.broadcasted_iota(jnp.int32, (8, norm.shape[1]), 0)
    ones = jnp.where((row >= 3 - at) & (row < 6 - at), 1.0, 0.0)
    return jnp.where(row == at, high, jnp.where(row == at + 1, mid, jnp.where(row == at + 2, low, ones)))


def scaled(points, scale):
    return (points - 0.5) * scale


def half_norm(points):
    return -0.5 * jnp.sum(points * points, axis=0, keepdims=True)


def left(points, scale):
    u = scaled(points, scale)
    high, mid, low = split(u)
    norms = norm_rows(half_norm(u), 0)
    return jnp.concatenate([high, high, high, mid, mid, low, norms, jnp.zeros_like(norms)], 0)


def right(points, scale):
    v = scaled(points, scale)
    high, mid, low = split(v)
    norms = norm_rows(half_norm(v), 3)
    return jnp.concatenate([high, mid, low, high, mid, high, norms, jnp.zeros_like(norms)], 0)


def pack_kernel(*refs):
    sources, (out_col, scale_low, scale_high), held, sems = refs[:5], refs[5:8], refs[8:13], refs[13]
    copies = [pltpu.make_async_copy(a, b, sems.at[i]) for i, (a, b) in enumerate(zip(sources, held))]
    for copy in copies:
        copy.start()
    for copy in copies:
        copy.wait()
    runs, weights, points, len_low, len_high = held
    row = lax.broadcasted_iota(jnp.int32, (FEATS, LANES), 0)
    for lengths, out in ((len_low, scale_low), (len_high, scale_high)):
        column = jnp.ones((FEATS, LANES), F32)
        for i in range(FEATS):
            column = jnp.where(row == i, lengths[i], column)
        out[...] = ROOT / column
    own = points[...]
    last = jnp.broadcast_to(weights[:, :LANES], (8, LANES))
    row = lax.broadcasted_iota(jnp.int32, (8, LANES), 0)
    for q in range(1, RUN_BLOCKS):
        last = jnp.where(row == q, weights[:, q * LANES : (q + 1) * LANES], last)
    for i in range(out_col.shape[0]):
        for q in range(RUN_BLOCKS):
            out_col[i, q * FEATS : (q + 1) * FEATS, :] = runs[:, q * LANES : (q + 1) * LANES]
        out_col[i, RUN_BLOCKS * FEATS : PACKED - 8, :] = own
        out_col[i, PACKED - 8 :, :] = last


def prep_kernel(points, scale, out):
    def step(k, carry):
        out[pl.ds(pl.multiple_of(k * LANES, LANES), LANES), :] = left(points[k], scale[...]).T.astype(BF16)
        return carry

    lax.fori_loop(0, points.shape[0], step, 0, unroll=4)


def column_of(line, out, rows):
    out[rows, :] = jnp.broadcast_to(line, (LANES, LANES)).T


def weighted(cols, rows, column):
    term = jnp.exp2(jnp.dot(cols, rows, preferred_element_type=F32))
    count, wide = term.shape
    term = term * jnp.concatenate([column] * (wide // LANES), 1)
    return jnp.sum(term.reshape(count // 8, 8, wide), axis=0)


def mu_kernel(held, rows_in, scale, high, rho, at, out, cols_out, even, odd, total, lines):
    blocks = held.shape[0]

    def side(r):
        parts = [right(held[r, q * FEATS : (q + 1) * FEATS, :], scale[...]) for q in range(RUN_BLOCKS)]
        return jnp.concatenate([p.astype(BF16) for p in parts], 1)

    def work(r, runs):
        weights = held[r, PACKED - 8 :, :]
        for i in range(0, rows_in.shape[0], MU_CHUNK):
            rows = slice(i, i + MU_CHUNK)
            acc = total[rows, :]
            term = jnp.exp2(jnp.dot(rows_in[rows, :], runs[...], preferred_element_type=F32))
            for q in range(RUN_BLOCKS):
                acc = acc + term[:, q * LANES : (q + 1) * LANES] * weights[q : q + 1, :]
            total[rows, :] = acc

    total[...] = jnp.zeros_like(total)
    even[...] = side(0)

    def step(k, carry):
        odd[...] = side(2 * k + 1)
        work(2 * k, even)
        even[...] = side(jnp.minimum(2 * k + 2, blocks - 1))
        work(2 * k + 1, odd)
        return carry

    lax.fori_loop(0, blocks // 2, step, 0)
    for r in range(blocks):
        cols_out[r] = held[r, RUN_BLOCKS * FEATS : PACKED - 8, :]
    for k in range(lines.shape[0]):
        lines[k : k + 1, :] = jnp.sum(total[k * LANES : (k + 1) * LANES, :].T, axis=0, keepdims=True)
    mu = lines[...]
    row = lax.broadcasted_iota(jnp.int32, mu.shape, 0)
    target = -rho[0] * mu
    target = jnp.where(row == at[0], target + high[...], target)
    for i in range(out.shape[0]):
        out[i] = jnp.where(row == i, mu, target)


def lines_of(total):
    line = jnp.sum(total[...], axis=0, keepdims=True)
    return jnp.concatenate([line[:, k : k + LANES] for k in range(0, line.shape[1], LANES)], 0)


def sides_kernel(rows, cols, scale, rows_out, cols_out):
    def step(k, carry):
        place = pl.ds(pl.multiple_of(k * LANES, LANES), LANES)
        rows_out[:, place] = left(rows[k], scale[...]).astype(BF16)
        cols_out[place, :] = right(cols[k], scale[...]).T.astype(BF16)
        return carry

    lax.fori_loop(0, rows.shape[0], step, 0, unroll=4)


def first_kernel(held, rows_in, cols_in, high, rho, noise, at, out, target_out, mu_out, sums):
    total = jnp.sum(held[...], axis=0)
    row = lax.broadcasted_iota(jnp.int32, total.shape, 0)
    own = row == at[0]
    target = jnp.where(own, high[...] - rho[0] * total, total)
    target_out[...] = target
    mu_out[...] = jnp.sum(jnp.where(own, total, 0.0), axis=0, keepdims=True)
    own_target = jnp.sum(jnp.where(own, target, 0.0), axis=0, keepdims=True)
    size = 2 * LANES

    def step(k, carry):
        cols = cols_in[pl.ds(pl.multiple_of(k * size, size), size), :]
        acc = jnp.zeros((size, LANES), F32)
        for c in range(0, rows_in.shape[1], WIDE):
            term = jnp.exp2(jnp.dot(cols, rows_in[:, c : c + WIDE], preferred_element_type=F32))
            for q in range(0, WIDE, LANES):
                s = (c + q) // LANES
                acc = acc + term[:, q : q + LANES] * target_out[s : s + 1, :]
        for q in range(2):
            block = acc[q * LANES : (q + 1) * LANES, :]
            sums[pl.ds(k * 2 + q, 1), :] = jnp.sum(block.T, axis=0, keepdims=True)
        return carry

    lax.fori_loop(0, cols_in.shape[0] // size, step, 0)
    image = sums[...]
    image = jnp.where(lax.broadcasted_iota(jnp.int32, image.shape, 0) == at[1], image + noise[0] * own_target, image)
    for i in range(out.shape[0]):
        out[i] = image


def second_kernel(held, rows_in, cols_in, noise, at, out, column, total):
    image = jnp.sum(held[...], axis=0)
    mine = lax.broadcasted_iota(jnp.int32, image.shape, 0) == at[1]
    own = jnp.sum(jnp.where(mine, image, 0.0), axis=0, keepdims=True)
    for k in range(image.shape[0]):
        column_of(image[k : k + 1, :], column, slice(k * LANES, (k + 1) * LANES))
    total[...] = jnp.zeros_like(total)

    def step(i, carry):
        rows = pl.ds(pl.multiple_of(i * CHUNK, CHUNK), CHUNK)
        for c in range(0, rows_in.shape[1], WIDE):
            total[:, c : c + WIDE] += weighted(cols_in[rows, :], rows_in[:, c : c + WIDE], column[rows, :])
        return carry

    lax.fori_loop(0, cols_in.shape[0] // CHUNK, step, 0)
    last = lines_of(total)
    row = lax.broadcasted_iota(jnp.int32, last.shape, 0)
    last = jnp.where(row == at[0], last + noise[0] * own, last)
    extra = jnp.broadcast_to(own, (8, LANES))
    for i in range(out.shape[0]):
        out[i, : last.shape[0], :] = last
        out[i, last.shape[0] :, :] = extra


def two_sum(a, b):
    s = a + b
    t = s - a
    return s, (a - (s - t)) + (b - t)


def pair_add(x, y):
    s, e = two_sum(x[0], y[0])
    return two_sum(s, e + (x[1] + y[1]))


def product(a, b):
    ah = a.astype(BF16).astype(F32)
    bh = b.astype(BF16).astype(F32)
    al, bl = a - ah, b - bh
    s, e = two_sum(ah * bh, ah * bl + al * bh)
    return two_sum(s, e + al * bl)


def pair_product(x, y):
    s, e = product(x[0], y[0])
    return two_sum(s, e + (x[0] * y[1] + x[1] * y[0]))


def minus(x):
    return -x[0], -x[1]


def pair_ratio(x, y):
    q = x[0] / y[0]
    rest = pair_add(x, minus(pair_product((q, jnp.zeros_like(q)), y)))
    return two_sum(q, (rest[0] + rest[1]) / y[0])


def fold_rows(x):
    high, low = x
    count = high.shape[0]
    while count > 8:
        count //= 2
        high, low = pair_add((high[:count], low[:count]), (high[count:], low[count:]))
    return high, low


def moments_kernel(held, target, at, out, own_out):
    count = target.shape[0]
    last = jnp.sum(held[:, :count, :], axis=0)
    image = held[:, count, :]
    b = target[...]
    for i, (p, q) in enumerate(((b, b), (b, image), (image, image), (image, last))):
        high, low = fold_rows(product(p, q))
        for shift in (4, 2, 1):
            high, low = pair_add((high, low), (pltpu.roll(high, shift, 0), pltpu.roll(low, shift, 0)))
        for j in range(out.shape[0]):
            out[j, 2 * i : 2 * i + 1, :] = high[:1]
            out[j, 2 * i + 1 : 2 * i + 2, :] = low[:1]
    own = lax.broadcasted_iota(jnp.int32, b.shape, 0) == at[0]
    for i, v in enumerate((b, image, last)):
        own_out[i : i + 1, :] = jnp.sum(jnp.where(own, v, 0.0), axis=0, keepdims=True)


def final_kernel(held, own, x_out, r_out):
    sums = []
    for i in range(4):
        h = jnp.concatenate([held[j, 2 * i : 2 * i + 1, :] for j in range(held.shape[0])], 0)
        l = jnp.concatenate([held[j, 2 * i + 1 : 2 * i + 2, :] for j in range(held.shape[0])], 0)
        h, l = fold_rows((h, l))
        for axis, shifts in ((0, (4, 2, 1)), (1, (64, 32, 16, 8, 4, 2, 1))):
            for shift in shifts:
                h, l = pair_add((h, l), (pltpu.roll(h, shift, axis), pltpu.roll(l, shift, axis)))
        sums.append((h[:1], l[:1]))
    m0, m1, m2, m3 = sums
    alpha = pair_ratio(m0, m1)
    ratio = pair_ratio(m2, m1)
    v1 = pair_add(m2, minus(pair_product(m1, pair_ratio(m1, m0))))
    v2 = pair_add(m3, minus(pair_product(m2, ratio)))
    scale = pair_product(alpha, ratio)
    alpha0, grow = alpha[0], scale[0]
    alpha1 = (v1[0] + v1[1]) / (v2[0] + v2[1])
    b, image, last = own[0:1, :], own[1:2, :], own[2:3, :]
    x_out[...] = alpha0 * b + alpha1 * (grow * b - alpha0 * image)
    r_out[...] = (b - alpha0 * image) - alpha1 * (grow * image - alpha0 * last)


def exchange(blocks, axes):
    return lax.all_to_all(blocks, axes, 0, 0, tiled=True)


def local(runs, weights, points, high, len_low, len_high, rho, noise):
    n_row, n_col = lax.axis_size(ROWS), lax.axis_size(COLS)
    at = jnp.stack([lax.axis_index(ROWS), lax.axis_index(COLS)]).astype(jnp.int32)
    high = high.reshape(1, LANES)
    cols_len, rows_len = n_col * LANES, n_row * LANES
    to_col, scale_low, scale_high = pl.pallas_call(
        pack_kernel,
        out_shape=(shape((n_col, PACKED, LANES)), shape((FEATS, LANES)), shape((FEATS, LANES))),
        in_specs=[HBM] * 5,
        out_specs=(VMEM,) * 3,
        scratch_shapes=[
            pltpu.VMEM((FEATS, RUN_BLOCKS * LANES), F32),
            pltpu.VMEM((1, RUN_BLOCKS * LANES), F32),
            pltpu.VMEM((FEATS, LANES), F32),
            pltpu.SMEM((FEATS,), F32),
            pltpu.SMEM((FEATS,), F32),
            pltpu.SemaphoreType.DMA((5,)),
        ],
        compiler_params=params(60),
        name="pack",
    )(runs, weights.reshape(1, RUN_BLOCKS * LANES), points, len_low, len_high)
    by_col = exchange(to_col, COLS)
    by_row = lax.all_gather(points, "z", axis=0)
    by_row = lax.all_gather(by_row, "core", axis=0).reshape(n_row, FEATS, LANES)
    row_low = pl.pallas_call(
        prep_kernel,
        out_shape=shape((rows_len, DEPTH), BF16),
        in_specs=[VMEM] * 2,
        out_specs=VMEM,
        compiler_params=params(4),
        name="prep",
    )(by_row, scale_low)
    mu_terms, col_points = pl.pallas_call(
        mu_kernel,
        out_shape=(shape((n_row, n_row, LANES)), shape((n_col, FEATS, LANES))),
        in_specs=[VMEM] * 4 + [SMEM] * 2,
        out_specs=(VMEM,) * 2,
        scratch_shapes=[
            pltpu.VMEM((DEPTH, RUN_BLOCKS * LANES), BF16),
            pltpu.VMEM((DEPTH, RUN_BLOCKS * LANES), BF16),
            pltpu.VMEM((rows_len, LANES), F32),
            pltpu.VMEM((n_row, LANES), F32),
        ],
        compiler_params=params(16),
        name="mu",
    )(by_col, row_low, scale_low, high, rho, at)
    mu_held = exchange(mu_terms, ROWS)
    row_parts, col_parts = pl.pallas_call(
        sides_kernel,
        out_shape=(shape((DEPTH, rows_len), BF16), shape((cols_len, DEPTH), BF16)),
        in_specs=[VMEM] * 3,
        out_specs=(VMEM,) * 2,
        compiler_params=params(4),
        name="sides",
    )(by_row, col_points, scale_high)
    image_terms, target, mu = pl.pallas_call(
        first_kernel,
        out_shape=(shape((n_col, n_col, LANES)), shape((n_row, LANES)), shape((1, LANES))),
        in_specs=[VMEM] * 4 + [SMEM] * 3,
        out_specs=(VMEM,) * 3,
        scratch_shapes=[pltpu.VMEM((n_col, LANES), F32)],
        compiler_params=params(4),
        name="first",
    )(mu_held, row_parts, col_parts, high, rho, noise, at)
    image_held = exchange(image_terms, COLS)
    last_terms = pl.pallas_call(
        second_kernel,
        out_shape=shape((n_row, n_row + 8, LANES)),
        in_specs=[VMEM] * 3 + [SMEM] * 2,
        out_specs=VMEM,
        scratch_shapes=[pltpu.VMEM((cols_len, LANES), F32), pltpu.VMEM((8, rows_len), F32)],
        compiler_params=params(8),
        name="second",
    )(image_held, row_parts, col_parts, noise, at)
    last_held = exchange(last_terms, ROWS)
    moments, own = pl.pallas_call(
        moments_kernel,
        out_shape=(shape((n_col, 8, LANES)), shape((8, LANES))),
        in_specs=[VMEM] * 2 + [SMEM],
        out_specs=(VMEM,) * 2,
        compiler_params=params(4),
        name="moments",
    )(last_held, target, at)
    moments_held = exchange(moments, COLS)
    x, r = pl.pallas_call(
        final_kernel,
        out_shape=(shape((1, LANES)), shape((1, LANES))),
        in_specs=[VMEM] * 2,
        out_specs=(VMEM,) * 2,
        compiler_params=params(4),
        name="final",
    )(moments_held, own)
    return mu.reshape(LANES), x.reshape(LANES), r.reshape(LANES)


def solution(mesh):
    spread = P(AXES)
    wide = P(None, AXES)
    fine = Mesh(mesh.devices.reshape(4, 2, 4, 8), AXES)
    return jax.shard_map(
        local,
        mesh=fine,
        in_specs=(wide, spread, wide, spread, P(), P(), P(), P()),
        out_specs=(spread,) * 3,
        check_vma=False,
    )
```

```python
import math

import jax
import jax.numpy as jnp
from jax import lax
from jax.experimental import pallas as pl
from jax.experimental.pallas import tpu as pltpu
from jax.sharding import Mesh
from jax.sharding import PartitionSpec as P

F32 = jnp.float32
BF16 = jnp.bfloat16
FEATS = 24
LANES = 128
RUN_BLOCKS = 4
STEPS = (4, 2, 1)
WIDE = CHUNK = 512
MU_CHUNK = 1024
PACKED = RUN_BLOCKS * FEATS + FEATS + 8
DEPTH = 160
ROOT = math.sqrt(math.log2(math.e))
VMEM = pl.BlockSpec(memory_space=pltpu.VMEM)
AXES = ("y", "core", "x", "z")
ROWS = ("core", "z")
COLS = ("y", "x")
HBM = pl.BlockSpec(memory_space=pltpu.HBM)
SMEM = pl.BlockSpec(memory_space=pltpu.SMEM)


def params(mib):
    return pltpu.CompilerParams(vmem_limit_bytes=mib * 1024 * 1024)


def shape(dims, kind=F32):
    return jax.ShapeDtypeStruct(dims, kind)


def split(x):
    high = x.astype(BF16).astype(F32)
    rest = x - high
    mid = rest.astype(BF16).astype(F32)
    return high, mid, rest - mid


def norm_rows(norm, at):
    high, mid, low = split(norm)
    row = lax.broadcasted_iota(jnp.int32, (8, norm.shape[1]), 0)
    ones = jnp.where((row >= 3 - at) & (row < 6 - at), 1.0, 0.0)
    return jnp.where(row == at, high, jnp.where(row == at + 1, mid, jnp.where(row == at + 2, low, ones)))


def scaled(points, scale):
    return (points - 0.5) * scale


def half_norm(points):
    return -0.5 * jnp.sum(points * points, axis=0, keepdims=True)


def left(points, scale):
    u = scaled(points, scale)
    high, mid, low = split(u)
    norms = norm_rows(half_norm(u), 0)
    return jnp.concatenate([high, high, high, mid, mid, low, norms, jnp.zeros_like(norms)], 0)


def right(points, scale):
    v = scaled(points, scale)
    high, mid, low = split(v)
    norms = norm_rows(half_norm(v), 3)
    return jnp.concatenate([high, mid, low, high, mid, high, norms, jnp.zeros_like(norms)], 0)


def pack_kernel(*refs):
    sources, (out_col, scale_low, scale_high), held, sems = refs[:5], refs[5:8], refs[8:13], refs[13]
    copies = [pltpu.make_async_copy(a, b, sems.at[i]) for i, (a, b) in enumerate(zip(sources, held))]
    for copy in copies:
        copy.start()
    for copy in copies:
        copy.wait()
    runs, weights, points, len_low, len_high = held
    row = lax.broadcasted_iota(jnp.int32, (FEATS, LANES), 0)
    for lengths, out in ((len_low, scale_low), (len_high, scale_high)):
        column = jnp.ones((FEATS, LANES), F32)
        for i in range(FEATS):
            column = jnp.where(row == i, lengths[i], column)
        out[...] = ROOT / column
    own = points[...]
    last = jnp.broadcast_to(weights[:, :LANES], (8, LANES))
    row = lax.broadcasted_iota(jnp.int32, (8, LANES), 0)
    for q in range(1, RUN_BLOCKS):
        last = jnp.where(row == q, weights[:, q * LANES : (q + 1) * LANES], last)
    for i in range(out_col.shape[0]):
        for q in range(RUN_BLOCKS):
            out_col[i, q * FEATS : (q + 1) * FEATS, :] = runs[:, q * LANES : (q + 1) * LANES]
        out_col[i, RUN_BLOCKS * FEATS : PACKED - 8, :] = own
        out_col[i, PACKED - 8 :, :] = last


def place_of(k, at):
    depth = len(STEPS)
    offset = sum(step for i, step in enumerate(STEPS) if k >> i & 1)
    block = (k >> depth << depth) + ((at[0] & (1 << depth) - 1) ^ offset)
    return pl.ds(pl.multiple_of(block * LANES, LANES), LANES)


def prep_kernel(points, scale, at, out):
    for k in range(points.shape[0]):
        out[place_of(k, at), :] = left(points[k], scale[...]).T.astype(BF16)


def column_of(line, out, rows):
    out[rows, :] = jnp.broadcast_to(line, (LANES, LANES)).T


def weighted(cols, rows, column):
    term = jnp.exp2(jnp.dot(cols, rows, preferred_element_type=F32))
    count, wide = term.shape
    term = term * jnp.concatenate([column] * (wide // LANES), 1)
    return jnp.sum(term.reshape(count // 8, 8, wide), axis=0)


def mu_kernel(held, rows_in, scale, high, rho, at, out, cols_out, even, odd, total, lines):
    blocks = held.shape[0]

    def side(r):
        parts = [right(held[r, q * FEATS : (q + 1) * FEATS, :], scale[...]) for q in range(RUN_BLOCKS)]
        return jnp.concatenate([p.astype(BF16) for p in parts], 1)

    def work(r, runs):
        weights = held[r, PACKED - 8 :, :]
        for i in range(0, rows_in.shape[0], MU_CHUNK):
            rows = slice(i, i + MU_CHUNK)
            acc = total[rows, :]
            term = jnp.exp2(jnp.dot(rows_in[rows, :], runs[...], preferred_element_type=F32))
            for q in range(RUN_BLOCKS):
                acc = acc + term[:, q * LANES : (q + 1) * LANES] * weights[q : q + 1, :]
            total[rows, :] = acc

    total[...] = jnp.zeros_like(total)
    even[...] = side(0)

    def step(k, carry):
        odd[...] = side(2 * k + 1)
        work(2 * k, even)
        even[...] = side(jnp.minimum(2 * k + 2, blocks - 1))
        work(2 * k + 1, odd)
        return carry

    lax.fori_loop(0, blocks // 2, step, 0)
    for r in range(blocks):
        cols_out[r] = held[r, RUN_BLOCKS * FEATS : PACKED - 8, :]
    for k in range(lines.shape[0]):
        lines[k : k + 1, :] = jnp.sum(total[k * LANES : (k + 1) * LANES, :].T, axis=0, keepdims=True)
    mu = lines[...]
    row = lax.broadcasted_iota(jnp.int32, mu.shape, 0)
    target = -rho[0] * mu
    target = jnp.where(row == at[0], target + high[...], target)
    for i in range(out.shape[0]):
        out[i] = jnp.where(row == i, mu, target)


def lines_of(total):
    line = jnp.sum(total[...], axis=0, keepdims=True)
    return jnp.concatenate([line[:, k : k + LANES] for k in range(0, line.shape[1], LANES)], 0)


def sides_kernel(rows, cols, scale, at, rows_out, cols_out):
    for k in range(rows.shape[0]):
        rows_out[:, place_of(k, at)] = left(rows[k], scale[...]).astype(BF16)
    for k in range(cols.shape[0]):
        cols_out[k * LANES : (k + 1) * LANES, :] = right(cols[k], scale[...]).T.astype(BF16)


def first_kernel(held, rows_in, cols_in, high, rho, noise, at, out, target_out, mu_out, sums):
    total = jnp.sum(held[...], axis=0)
    row = lax.broadcasted_iota(jnp.int32, total.shape, 0)
    own = row == at[0]
    target = jnp.where(own, high[...] - rho[0] * total, total)
    target_out[...] = target
    mu_out[...] = jnp.sum(jnp.where(own, total, 0.0), axis=0, keepdims=True)
    own_target = jnp.sum(jnp.where(own, target, 0.0), axis=0, keepdims=True)
    size = 2 * LANES

    def step(k, carry):
        cols = cols_in[pl.ds(pl.multiple_of(k * size, size), size), :]
        acc = jnp.zeros((size, LANES), F32)
        for c in range(0, rows_in.shape[1], WIDE):
            term = jnp.exp2(jnp.dot(cols, rows_in[:, c : c + WIDE], preferred_element_type=F32))
            for q in range(0, WIDE, LANES):
                s = (c + q) // LANES
                acc = acc + term[:, q : q + LANES] * target_out[s : s + 1, :]
        for q in range(2):
            block = acc[q * LANES : (q + 1) * LANES, :]
            sums[pl.ds(k * 2 + q, 1), :] = jnp.sum(block.T, axis=0, keepdims=True)
        return carry

    lax.fori_loop(0, cols_in.shape[0] // size, step, 0)
    image = sums[...]
    image = jnp.where(lax.broadcasted_iota(jnp.int32, image.shape, 0) == at[1], image + noise[0] * own_target, image)
    for i in range(out.shape[0]):
        out[i] = image


def second_kernel(held, rows_in, cols_in, noise, at, out, column, total):
    image = jnp.sum(held[...], axis=0)
    mine = lax.broadcasted_iota(jnp.int32, image.shape, 0) == at[1]
    own = jnp.sum(jnp.where(mine, image, 0.0), axis=0, keepdims=True)
    for k in range(image.shape[0]):
        column_of(image[k : k + 1, :], column, slice(k * LANES, (k + 1) * LANES))
    total[...] = jnp.zeros_like(total)

    def step(i, carry):
        rows = pl.ds(pl.multiple_of(i * CHUNK, CHUNK), CHUNK)
        for c in range(0, rows_in.shape[1], WIDE):
            total[:, c : c + WIDE] += weighted(cols_in[rows, :], rows_in[:, c : c + WIDE], column[rows, :])
        return carry

    lax.fori_loop(0, cols_in.shape[0] // CHUNK, step, 0)
    last = lines_of(total)
    row = lax.broadcasted_iota(jnp.int32, last.shape, 0)
    last = jnp.where(row == at[0], last + noise[0] * own, last)
    extra = jnp.broadcast_to(own, (8, LANES))
    for i in range(out.shape[0]):
        out[i, : last.shape[0], :] = last
        out[i, last.shape[0] :, :] = extra


def two_sum(a, b):
    s = a + b
    t = s - a
    return s, (a - (s - t)) + (b - t)


def pair_add(x, y):
    s, e = two_sum(x[0], y[0])
    return two_sum(s, e + (x[1] + y[1]))


def product(a, b):
    ah = a.astype(BF16).astype(F32)
    bh = b.astype(BF16).astype(F32)
    al, bl = a - ah, b - bh
    s, e = two_sum(ah * bh, ah * bl + al * bh)
    return two_sum(s, e + al * bl)


def pair_product(x, y):
    s, e = product(x[0], y[0])
    return two_sum(s, e + (x[0] * y[1] + x[1] * y[0]))


def minus(x):
    return -x[0], -x[1]


def pair_ratio(x, y):
    q = x[0] / y[0]
    rest = pair_add(x, minus(pair_product((q, jnp.zeros_like(q)), y)))
    return two_sum(q, (rest[0] + rest[1]) / y[0])


def fold_rows(x):
    high, low = x
    count = high.shape[0]
    while count > 8:
        count //= 2
        high, low = pair_add((high[:count], low[:count]), (high[count:], low[count:]))
    return high, low


def moments_kernel(held, target, at, out, own_out):
    count = target.shape[0]
    last = jnp.sum(held[:, :count, :], axis=0)
    image = held[:, count, :]
    b = target[...]
    for i, (p, q) in enumerate(((b, b), (b, image), (image, image), (image, last))):
        high, low = fold_rows(product(p, q))
        for shift in (4, 2, 1):
            high, low = pair_add((high, low), (pltpu.roll(high, shift, 0), pltpu.roll(low, shift, 0)))
        for j in range(out.shape[0]):
            out[j, 2 * i : 2 * i + 1, :] = high[:1]
            out[j, 2 * i + 1 : 2 * i + 2, :] = low[:1]
    own = lax.broadcasted_iota(jnp.int32, b.shape, 0) == at[0]
    for i, v in enumerate((b, image, last)):
        own_out[i : i + 1, :] = jnp.sum(jnp.where(own, v, 0.0), axis=0, keepdims=True)


def final_kernel(held, own, x_out, r_out):
    sums = []
    for i in range(4):
        h = jnp.concatenate([held[j, 2 * i : 2 * i + 1, :] for j in range(held.shape[0])], 0)
        l = jnp.concatenate([held[j, 2 * i + 1 : 2 * i + 2, :] for j in range(held.shape[0])], 0)
        h, l = fold_rows((h, l))
        for axis, shifts in ((0, (4, 2, 1)), (1, (64, 32, 16, 8, 4, 2, 1))):
            for shift in shifts:
                h, l = pair_add((h, l), (pltpu.roll(h, shift, axis), pltpu.roll(l, shift, axis)))
        sums.append((h[:1], l[:1]))
    m0, m1, m2, m3 = sums
    alpha = pair_ratio(m0, m1)
    ratio = pair_ratio(m2, m1)
    v1 = pair_add(m2, minus(pair_product(m1, pair_ratio(m1, m0))))
    v2 = pair_add(m3, minus(pair_product(m2, ratio)))
    scale = pair_product(alpha, ratio)
    alpha0, grow = alpha[0], scale[0]
    alpha1 = (v1[0] + v1[1]) / (v2[0] + v2[1])
    b, image, last = own[0:1, :], own[1:2, :], own[2:3, :]
    x_out[...] = alpha0 * b + alpha1 * (grow * b - alpha0 * image)
    r_out[...] = (b - alpha0 * image) - alpha1 * (grow * image - alpha0 * last)


def exchange(blocks, axes):
    return lax.all_to_all(blocks, axes, 0, 0, tiled=True)


def local(runs, weights, points, high, len_low, len_high, rho, noise):
    n_row, n_col = lax.axis_size(ROWS), lax.axis_size(COLS)
    at = jnp.stack([lax.axis_index(ROWS), lax.axis_index(COLS)]).astype(jnp.int32)
    high = high.reshape(1, LANES)
    cols_len, rows_len = n_col * LANES, n_row * LANES
    to_col, scale_low, scale_high = pl.pallas_call(
        pack_kernel,
        out_shape=(shape((n_col, PACKED, LANES)), shape((FEATS, LANES)), shape((FEATS, LANES))),
        in_specs=[HBM] * 5,
        out_specs=(VMEM,) * 3,
        scratch_shapes=[
            pltpu.VMEM((FEATS, RUN_BLOCKS * LANES), F32),
            pltpu.VMEM((1, RUN_BLOCKS * LANES), F32),
            pltpu.VMEM((FEATS, LANES), F32),
            pltpu.SMEM((FEATS,), F32),
            pltpu.SMEM((FEATS,), F32),
            pltpu.SemaphoreType.DMA((5,)),
        ],
        compiler_params=params(60),
        name="pack",
    )(runs, weights.reshape(1, RUN_BLOCKS * LANES), points, len_low, len_high)
    by_col = exchange(to_col, COLS)
    by_row = points[None]
    for step in STEPS:
        pairs = [(i, i ^ step) for i in range(lax.axis_size("z"))]
        by_row = jnp.concatenate([by_row, lax.ppermute(by_row, "z", pairs)], 0)
    by_row = lax.all_gather(by_row, "core", axis=0, tiled=True)
    row_low = pl.pallas_call(
        prep_kernel,
        out_shape=shape((rows_len, DEPTH), BF16),
        in_specs=[VMEM, VMEM, SMEM],
        out_specs=VMEM,
        compiler_params=params(4),
        name="prep",
    )(by_row, scale_low, at)
    mu_terms, col_points = pl.pallas_call(
        mu_kernel,
        out_shape=(shape((n_row, n_row, LANES)), shape((n_col, FEATS, LANES))),
        in_specs=[VMEM] * 4 + [SMEM] * 2,
        out_specs=(VMEM,) * 2,
        scratch_shapes=[
            pltpu.VMEM((DEPTH, RUN_BLOCKS * LANES), BF16),
            pltpu.VMEM((DEPTH, RUN_BLOCKS * LANES), BF16),
            pltpu.VMEM((rows_len, LANES), F32),
            pltpu.VMEM((n_row, LANES), F32),
        ],
        compiler_params=params(16),
        name="mu",
    )(by_col, row_low, scale_low, high, rho, at)
    mu_held = exchange(mu_terms, ROWS)
    row_parts, col_parts = pl.pallas_call(
        sides_kernel,
        out_shape=(shape((DEPTH, rows_len), BF16), shape((cols_len, DEPTH), BF16)),
        in_specs=[VMEM] * 3 + [SMEM],
        out_specs=(VMEM,) * 2,
        compiler_params=params(4),
        name="sides",
    )(by_row, col_points, scale_high, at)
    image_terms, target, mu = pl.pallas_call(
        first_kernel,
        out_shape=(shape((n_col, n_col, LANES)), shape((n_row, LANES)), shape((1, LANES))),
        in_specs=[VMEM] * 4 + [SMEM] * 3,
        out_specs=(VMEM,) * 3,
        scratch_shapes=[pltpu.VMEM((n_col, LANES), F32)],
        compiler_params=params(4),
        name="first",
    )(mu_held, row_parts, col_parts, high, rho, noise, at)
    image_held = exchange(image_terms, COLS)
    last_terms = pl.pallas_call(
        second_kernel,
        out_shape=shape((n_row, n_row + 8, LANES)),
        in_specs=[VMEM] * 3 + [SMEM] * 2,
        out_specs=VMEM,
        scratch_shapes=[pltpu.VMEM((cols_len, LANES), F32), pltpu.VMEM((8, rows_len), F32)],
        compiler_params=params(8),
        name="second",
    )(image_held, row_parts, col_parts, noise, at)
    last_held = exchange(last_terms, ROWS)
    moments, own = pl.pallas_call(
        moments_kernel,
        out_shape=(shape((n_col, 8, LANES)), shape((8, LANES))),
        in_specs=[VMEM] * 2 + [SMEM],
        out_specs=(VMEM,) * 2,
        compiler_params=params(4),
        name="moments",
    )(last_held, target, at)
    moments_held = exchange(moments, COLS)
    x, r = pl.pallas_call(
        final_kernel,
        out_shape=(shape((1, LANES)), shape((1, LANES))),
        in_specs=[VMEM] * 2,
        out_specs=(VMEM,) * 2,
        compiler_params=params(4),
        name="final",
    )(moments_held, own)
    return mu.reshape(LANES), x.reshape(LANES), r.reshape(LANES)


def solution(mesh):
    spread = P(AXES)
    wide = P(None, AXES)
    fine = Mesh(mesh.devices.reshape(4, 2, 4, 8), AXES)
    return jax.shard_map(
        local,
        mesh=fine,
        in_specs=(wide, spread, wide, spread, P(), P(), P(), P()),
        out_specs=(spread,) * 3,
        check_vma=False,
    )
```

```python
import math

import jax
import jax.numpy as jnp
from jax import lax
from jax.experimental import pallas as pl
from jax.experimental.pallas import tpu as pltpu
from jax.sharding import Mesh
from jax.sharding import PartitionSpec as P

F32 = jnp.float32
BF16 = jnp.bfloat16
FEATS = 24
LANES = 128
RUN_BLOCKS = 4
WIDE = CHUNK = 512
MU_CHUNK = 256
PACKED = RUN_BLOCKS * FEATS + FEATS + 8
DEPTH = 160
ROOT = math.sqrt(math.log2(math.e))
VMEM = pl.BlockSpec(memory_space=pltpu.VMEM)
AXES = ("y", "core", "x", "z")
ROWS = ("core", "z")
COLS = ("y", "x")
HBM = pl.BlockSpec(memory_space=pltpu.HBM)
SMEM = pl.BlockSpec(memory_space=pltpu.SMEM)


def params(mib):
    return pltpu.CompilerParams(vmem_limit_bytes=mib * 1024 * 1024)


def shape(dims, kind=F32):
    return jax.ShapeDtypeStruct(dims, kind)


def split(x):
    high = x.astype(BF16).astype(F32)
    rest = x - high
    mid = rest.astype(BF16).astype(F32)
    return high, mid, rest - mid


def norm_rows(norm, at):
    high, mid, low = split(norm)
    row = lax.broadcasted_iota(jnp.int32, (8, norm.shape[1]), 0)
    ones = jnp.where((row >= 3 - at) & (row < 6 - at), 1.0, 0.0)
    return jnp.where(row == at, high, jnp.where(row == at + 1, mid, jnp.where(row == at + 2, low, ones)))


def scaled(points, scale):
    return (points - 0.5) * scale


def half_norm(points):
    return -0.5 * jnp.sum(points * points, axis=0, keepdims=True)


def left(points, scale):
    u = scaled(points, scale)
    high, mid, low = split(u)
    norms = norm_rows(half_norm(u), 0)
    return jnp.concatenate([high, high, high, mid, mid, low, norms, jnp.zeros_like(norms)], 0)


def right(points, scale):
    v = scaled(points, scale)
    high, mid, low = split(v)
    norms = norm_rows(half_norm(v), 3)
    return jnp.concatenate([high, mid, low, high, mid, high, norms, jnp.zeros_like(norms)], 0)


def pack_kernel(*refs):
    sources, (out_col, scale_low, scale_high), held, sems = refs[:5], refs[5:8], refs[8:13], refs[13]
    copies = [pltpu.make_async_copy(a, b, sems.at[i]) for i, (a, b) in enumerate(zip(sources, held))]
    for copy in copies:
        copy.start()
    for copy in copies:
        copy.wait()
    runs, weights, points, len_low, len_high = held
    row = lax.broadcasted_iota(jnp.int32, (FEATS, LANES), 0)
    for lengths, out in ((len_low, scale_low), (len_high, scale_high)):
        column = jnp.ones((FEATS, LANES), F32)
        for i in range(FEATS):
            column = jnp.where(row == i, lengths[i], column)
        out[...] = ROOT / column
    own = points[...]
    last = jnp.broadcast_to(weights[:, :LANES], (8, LANES))
    row = lax.broadcasted_iota(jnp.int32, (8, LANES), 0)
    for q in range(1, RUN_BLOCKS):
        last = jnp.where(row == q, weights[:, q * LANES : (q + 1) * LANES], last)
    for i in range(out_col.shape[0]):
        for q in range(RUN_BLOCKS):
            out_col[i, q * FEATS : (q + 1) * FEATS, :] = runs[:, q * LANES : (q + 1) * LANES]
        out_col[i, RUN_BLOCKS * FEATS : PACKED - 8, :] = own
        out_col[i, PACKED - 8 :, :] = last


def place_of(j, m, at):
    block = (m & 1) * 8 + ((at[0] & 7) ^ (j ^ 4 * (m >> 1)))
    return pl.ds(pl.multiple_of(block * LANES, LANES), LANES)


def prep_kernel(*refs):
    points, scale, at, out = refs[:4], refs[4], refs[5], refs[6]
    for j, ref in enumerate(points):
        for m in range(ref.shape[0]):
            out[place_of(j, m, at), :] = left(ref[m], scale[...]).T.astype(BF16)


def column_of(line, out, rows):
    out[rows, :] = jnp.broadcast_to(line, (LANES, LANES)).T


def weighted(cols, rows, column):
    term = jnp.exp2(jnp.dot(cols, rows, preferred_element_type=F32))
    count, wide = term.shape
    term = term * jnp.concatenate([column] * (wide // LANES), 1)
    return jnp.sum(term.reshape(count // 8, 8, wide), axis=0)


def mu_kernel(held, rows_in, scale, high, rho, at, out, cols_out, even, odd, total, lines):
    blocks = held.shape[0]

    def side(r):
        parts = [right(held[r, q * FEATS : (q + 1) * FEATS, :], scale[...]) for q in range(RUN_BLOCKS)]
        return jnp.concatenate([p.astype(BF16) for p in parts], 1)

    def work(r, runs):
        weights = held[r, PACKED - 8 :, :]
        for i in range(0, rows_in.shape[0], MU_CHUNK):
            rows = slice(i, i + MU_CHUNK)
            acc = total[rows, :]
            term = jnp.exp2(jnp.dot(rows_in[rows, :], runs[...], preferred_element_type=F32))
            for q in range(RUN_BLOCKS):
                acc = acc + term[:, q * LANES : (q + 1) * LANES] * weights[q : q + 1, :]
            total[rows, :] = acc

    total[...] = jnp.zeros_like(total)
    held_sides = (even, odd)
    even[...] = side(0)
    for r in range(blocks):
        if r + 1 < blocks:
            held_sides[(r + 1) % 2][...] = side(r + 1)
        work(r, held_sides[r % 2])
    for r in range(blocks):
        cols_out[r] = held[r, RUN_BLOCKS * FEATS : PACKED - 8, :]
    for k in range(lines.shape[0]):
        lines[k : k + 1, :] = jnp.sum(total[k * LANES : (k + 1) * LANES, :].T, axis=0, keepdims=True)
    mu = lines[...]
    row = lax.broadcasted_iota(jnp.int32, mu.shape, 0)
    target = -rho[0] * mu
    target = jnp.where(row == at[0], target + high[...], target)
    for i in range(out.shape[0]):
        out[i] = jnp.where(row == i, mu, target)


def lines_of(total):
    line = jnp.sum(total[...], axis=0, keepdims=True)
    return jnp.concatenate([line[:, k : k + LANES] for k in range(0, line.shape[1], LANES)], 0)


def sides_kernel(*refs):
    points, (cols, scale, at, rows_out, cols_out) = refs[:4], refs[4:]
    for j, ref in enumerate(points):
        for m in range(ref.shape[0]):
            rows_out[:, place_of(j, m, at)] = left(ref[m], scale[...]).astype(BF16)
    for k in range(cols.shape[0]):
        cols_out[k * LANES : (k + 1) * LANES, :] = right(cols[k], scale[...]).T.astype(BF16)


def first_kernel(held, rows_in, cols_in, high, rho, noise, at, out, target_out, mu_out, sums):
    total = jnp.sum(held[...], axis=0)
    row = lax.broadcasted_iota(jnp.int32, total.shape, 0)
    own = row == at[0]
    target = jnp.where(own, high[...] - rho[0] * total, total)
    target_out[...] = target
    mu_out[...] = jnp.sum(jnp.where(own, total, 0.0), axis=0, keepdims=True)
    own_target = jnp.sum(jnp.where(own, target, 0.0), axis=0, keepdims=True)
    size = 2 * LANES

    for k in range(0, cols_in.shape[0], size):
        cols = cols_in[k : k + size, :]
        acc = jnp.zeros((size, LANES), F32)
        for c in range(0, rows_in.shape[1], WIDE):
            term = jnp.exp2(jnp.dot(cols, rows_in[:, c : c + WIDE], preferred_element_type=F32))
            for q in range(0, WIDE, LANES):
                s = (c + q) // LANES
                acc = acc + term[:, q : q + LANES] * target_out[s : s + 1, :]
        for q in range(0, size, LANES):
            at_row = (k + q) // LANES
            sums[at_row : at_row + 1, :] = jnp.sum(acc[q : q + LANES, :].T, axis=0, keepdims=True)
    image = sums[...]
    image = jnp.where(lax.broadcasted_iota(jnp.int32, image.shape, 0) == at[1], image + noise[0] * own_target, image)
    for i in range(out.shape[0]):
        out[i] = image


def second_kernel(held, rows_in, cols_in, noise, at, out, column, total):
    image = jnp.sum(held[...], axis=0)
    mine = lax.broadcasted_iota(jnp.int32, image.shape, 0) == at[1]
    own = jnp.sum(jnp.where(mine, image, 0.0), axis=0, keepdims=True)
    for k in range(image.shape[0]):
        column_of(image[k : k + 1, :], column, slice(k * LANES, (k + 1) * LANES))
    total[...] = jnp.zeros_like(total)

    for i in range(0, cols_in.shape[0], CHUNK):
        rows = slice(i, i + CHUNK)
        for c in range(0, rows_in.shape[1], WIDE):
            total[:, c : c + WIDE] += weighted(cols_in[rows, :], rows_in[:, c : c + WIDE], column[rows, :])
    last = lines_of(total)
    row = lax.broadcasted_iota(jnp.int32, last.shape, 0)
    last = jnp.where(row == at[0], last + noise[0] * own, last)
    extra = jnp.broadcast_to(own, (8, LANES))
    for i in range(out.shape[0]):
        out[i, : last.shape[0], :] = last
        out[i, last.shape[0] :, :] = extra


def two_sum(a, b):
    s = a + b
    t = s - a
    return s, (a - (s - t)) + (b - t)


def pair_add(x, y):
    s, e = two_sum(x[0], y[0])
    return two_sum(s, e + (x[1] + y[1]))


def product(a, b):
    ah = a.astype(BF16).astype(F32)
    bh = b.astype(BF16).astype(F32)
    al, bl = a - ah, b - bh
    s, e = two_sum(ah * bh, ah * bl + al * bh)
    return two_sum(s, e + al * bl)


def pair_product(x, y):
    s, e = product(x[0], y[0])
    return two_sum(s, e + (x[0] * y[1] + x[1] * y[0]))


def minus(x):
    return -x[0], -x[1]


def pair_ratio(x, y):
    q = x[0] / y[0]
    rest = pair_add(x, minus(pair_product((q, jnp.zeros_like(q)), y)))
    return two_sum(q, (rest[0] + rest[1]) / y[0])


def fold_rows(x):
    high, low = x
    count = high.shape[0]
    while count > 8:
        count //= 2
        high, low = pair_add((high[:count], low[:count]), (high[count:], low[count:]))
    return high, low


def moments_kernel(held, target, at, out, own_out):
    count = target.shape[0]
    last = jnp.sum(held[:, :count, :], axis=0)
    image = held[:, count, :]
    b = target[...]
    for i, (p, q) in enumerate(((b, b), (b, image), (image, image), (image, last))):
        high, low = fold_rows(product(p, q))
        for shift in (4, 2, 1):
            high, low = pair_add((high, low), (pltpu.roll(high, shift, 0), pltpu.roll(low, shift, 0)))
        for j in range(out.shape[0]):
            out[j, 2 * i : 2 * i + 1, :] = high[:1]
            out[j, 2 * i + 1 : 2 * i + 2, :] = low[:1]
    own = lax.broadcasted_iota(jnp.int32, b.shape, 0) == at[0]
    for i, v in enumerate((b, image, last)):
        own_out[i : i + 1, :] = jnp.sum(jnp.where(own, v, 0.0), axis=0, keepdims=True)


def final_kernel(held, own, x_out, r_out):
    sums = []
    for i in range(4):
        h = jnp.concatenate([held[j, 2 * i : 2 * i + 1, :] for j in range(held.shape[0])], 0)
        l = jnp.concatenate([held[j, 2 * i + 1 : 2 * i + 2, :] for j in range(held.shape[0])], 0)
        h, l = fold_rows((h, l))
        for axis, shifts in ((0, (4, 2, 1)), (1, (64, 32, 16, 8, 4, 2, 1))):
            for shift in shifts:
                h, l = pair_add((h, l), (pltpu.roll(h, shift, axis), pltpu.roll(l, shift, axis)))
        sums.append((h[:1], l[:1]))
    m0, m1, m2, m3 = sums
    alpha = pair_ratio(m0, m1)
    ratio = pair_ratio(m2, m1)
    v1 = pair_add(m2, minus(pair_product(m1, pair_ratio(m1, m0))))
    v2 = pair_add(m3, minus(pair_product(m2, ratio)))
    scale = pair_product(alpha, ratio)
    alpha0, grow = alpha[0], scale[0]
    alpha1 = (v1[0] + v1[1]) / (v2[0] + v2[1])
    b, image, last = own[0:1, :], own[1:2, :], own[2:3, :]
    x_out[...] = alpha0 * b + alpha1 * (grow * b - alpha0 * image)
    r_out[...] = (b - alpha0 * image) - alpha1 * (grow * image - alpha0 * last)


def exchange_z(blocks, step, size):
    return lax.ppermute(blocks, "z", [(i, i ^ step) for i in range(size)])


def exchange(blocks, axes):
    return lax.all_to_all(blocks, axes, 0, 0, tiled=True)


def local(runs, weights, points, high, len_low, len_high, rho, noise):
    n_row, n_col = lax.axis_size(ROWS), lax.axis_size(COLS)
    at = jnp.stack([lax.axis_index(ROWS), lax.axis_index(COLS)]).astype(jnp.int32)
    high = high.reshape(1, LANES)
    cols_len, rows_len = n_col * LANES, n_row * LANES
    near_core = lax.all_gather(points, "core", axis=0)
    near_core, weights = lax.optimization_barrier((near_core, weights))
    to_col, scale_low, scale_high = pl.pallas_call(
        pack_kernel,
        out_shape=(shape((n_col, PACKED, LANES)), shape((FEATS, LANES)), shape((FEATS, LANES))),
        in_specs=[HBM] * 5,
        out_specs=(VMEM,) * 3,
        scratch_shapes=[
            pltpu.VMEM((FEATS, RUN_BLOCKS * LANES), F32),
            pltpu.VMEM((1, RUN_BLOCKS * LANES), F32),
            pltpu.VMEM((FEATS, LANES), F32),
            pltpu.SMEM((FEATS,), F32),
            pltpu.SMEM((FEATS,), F32),
            pltpu.SemaphoreType.DMA((5,)),
        ],
        compiler_params=params(60),
        name="pack",
    )(runs, weights.reshape(1, RUN_BLOCKS * LANES), points, len_low, len_high)
    by_col = exchange(to_col, COLS)
    size = lax.axis_size("z")
    near = exchange_z(near_core, 4, size)
    near = jnp.concatenate([near_core, near], 0)
    by_row = [near] + [exchange_z(near, step, size) for step in (1, 2, 3)]
    row_low = pl.pallas_call(
        prep_kernel,
        out_shape=shape((rows_len, DEPTH), BF16),
        in_specs=[VMEM] * 5 + [SMEM],
        out_specs=VMEM,
        compiler_params=params(4),
        name="prep",
    )(*by_row, scale_low, at)
    mu_terms, col_points = pl.pallas_call(
        mu_kernel,
        out_shape=(shape((n_row, n_row, LANES)), shape((n_col, FEATS, LANES))),
        in_specs=[VMEM] * 4 + [SMEM] * 2,
        out_specs=(VMEM,) * 2,
        scratch_shapes=[
            pltpu.VMEM((DEPTH, RUN_BLOCKS * LANES), BF16),
            pltpu.VMEM((DEPTH, RUN_BLOCKS * LANES), BF16),
            pltpu.VMEM((rows_len, LANES), F32),
            pltpu.VMEM((n_row, LANES), F32),
        ],
        compiler_params=params(16),
        name="mu",
    )(by_col, row_low, scale_low, high, rho, at)
    mu_held = exchange(mu_terms, ROWS)
    row_parts, col_parts = pl.pallas_call(
        sides_kernel,
        out_shape=(shape((DEPTH, rows_len), BF16), shape((cols_len, DEPTH), BF16)),
        in_specs=[VMEM] * 6 + [SMEM],
        out_specs=(VMEM,) * 2,
        compiler_params=params(4),
        name="sides",
    )(*by_row, col_points, scale_high, at)
    image_terms, target, mu = pl.pallas_call(
        first_kernel,
        out_shape=(shape((n_col, n_col, LANES)), shape((n_row, LANES)), shape((1, LANES))),
        in_specs=[VMEM] * 4 + [SMEM] * 3,
        out_specs=(VMEM,) * 3,
        scratch_shapes=[pltpu.VMEM((n_col, LANES), F32)],
        compiler_params=params(4),
        name="first",
    )(mu_held, row_parts, col_parts, high, rho, noise, at)
    image_held = exchange(image_terms, COLS)
    last_terms = pl.pallas_call(
        second_kernel,
        out_shape=shape((n_row, n_row + 8, LANES)),
        in_specs=[VMEM] * 3 + [SMEM] * 2,
        out_specs=VMEM,
        scratch_shapes=[pltpu.VMEM((cols_len, LANES), F32), pltpu.VMEM((8, rows_len), F32)],
        compiler_params=params(8),
        name="second",
    )(image_held, row_parts, col_parts, noise, at)
    last_held = exchange(last_terms, ROWS)
    moments, own = pl.pallas_call(
        moments_kernel,
        out_shape=(shape((n_col, 8, LANES)), shape((8, LANES))),
        in_specs=[VMEM] * 2 + [SMEM],
        out_specs=(VMEM,) * 2,
        compiler_params=params(4),
        name="moments",
    )(last_held, target, at)
    moments_held = exchange(moments, COLS)
    x, r = pl.pallas_call(
        final_kernel,
        out_shape=(shape((1, LANES)), shape((1, LANES))),
        in_specs=[VMEM] * 2,
        out_specs=(VMEM,) * 2,
        compiler_params=params(4),
        name="final",
    )(moments_held, own)
    return mu.reshape(LANES), x.reshape(LANES), r.reshape(LANES)


def solution(mesh):
    spread = P(AXES)
    wide = P(None, AXES)
    fine = Mesh(mesh.devices.reshape(4, 2, 4, 8), AXES)
    return jax.shard_map(
        local,
        mesh=fine,
        in_specs=(wide, spread, wide, spread, P(), P(), P(), P()),
        out_specs=(spread,) * 3,
        check_vma=False,
    )
```

```python
import math

import jax
import jax.numpy as jnp
from jax import lax
from jax.experimental import pallas as pl
from jax.experimental.pallas import tpu as pltpu
from jax.sharding import Mesh
from jax.sharding import PartitionSpec as P

F32 = jnp.float32
BF16 = jnp.bfloat16
FEATS = 24
LANES = 128
RUN_BLOCKS = 4
WIDE = CHUNK = 512
MU_CHUNK = 256
PACKED = RUN_BLOCKS * FEATS + FEATS + 8
DEPTH = 160
ROOT = math.sqrt(math.log2(math.e))
VMEM = pl.BlockSpec(memory_space=pltpu.VMEM)
AXES = ("y", "core", "x", "z")
ROWS = ("core", "z")
COLS = ("y", "x")
HBM = pl.BlockSpec(memory_space=pltpu.HBM)
SMEM = pl.BlockSpec(memory_space=pltpu.SMEM)


def params(mib):
    return pltpu.CompilerParams(vmem_limit_bytes=mib * 1024 * 1024)


def shape(dims, kind=F32):
    return jax.ShapeDtypeStruct(dims, kind)


def split(x):
    high = x.astype(BF16).astype(F32)
    rest = x - high
    mid = rest.astype(BF16).astype(F32)
    return high, mid, rest - mid


def norm_rows(norm, at):
    high, mid, low = split(norm)
    row = lax.broadcasted_iota(jnp.int32, (8, norm.shape[1]), 0)
    ones = jnp.where((row >= 3 - at) & (row < 6 - at), 1.0, 0.0)
    return jnp.where(row == at, high, jnp.where(row == at + 1, mid, jnp.where(row == at + 2, low, ones)))


def scaled(points, scale):
    return (points - 0.5) * scale


def half_norm(points):
    return -0.5 * jnp.sum(points * points, axis=0, keepdims=True)


def left(points, scale):
    u = scaled(points, scale)
    high, mid, low = split(u)
    norms = norm_rows(half_norm(u), 0)
    return jnp.concatenate([high, high, high, mid, mid, low, norms, jnp.zeros_like(norms)], 0)


def right(points, scale):
    v = scaled(points, scale)
    high, mid, low = split(v)
    norms = norm_rows(half_norm(v), 3)
    return jnp.concatenate([high, mid, low, high, mid, high, norms, jnp.zeros_like(norms)], 0)


def pack_kernel(runs_hbm, weights_hbm, points_hbm, out, runs, weights, points, block, sems, out_sems):
    sources, held = (runs_hbm, weights_hbm, points_hbm), (runs, weights, points)
    copies = [pltpu.make_async_copy(a, b, sems.at[i]) for i, (a, b) in enumerate(zip(sources, held))]
    for copy in copies:
        copy.start()
    for copy in copies:
        copy.wait()
    last = jnp.broadcast_to(weights[:, :LANES], (8, LANES))
    row = lax.broadcasted_iota(jnp.int32, (8, LANES), 0)
    for q in range(RUN_BLOCKS):
        lanes = slice(q * LANES, (q + 1) * LANES)
        block[q * FEATS : (q + 1) * FEATS, :] = runs[:, lanes]
        if q:
            last = jnp.where(row == q, weights[:, lanes], last)
    block[RUN_BLOCKS * FEATS : PACKED - 8, :] = points[...]
    block[PACKED - 8 :, :] = last
    copies = [pltpu.make_async_copy(block, out.at[i], out_sems.at[i]) for i in range(out.shape[0])]
    for copy in copies:
        copy.start()
    for copy in copies:
        copy.wait()


def scale_column(lengths):
    row = lax.broadcasted_iota(jnp.int32, (FEATS, LANES), 0)
    column = jnp.ones((FEATS, LANES), F32)
    for i in range(FEATS):
        column = jnp.where(row == i, lengths[i], column)
    return ROOT / column


def place_of(m, at):
    block = (m >> 3) * 8 + ((at[0] & 7) ^ (m >> 1 & 3) ^ 4 * (m & 1))
    return pl.ds(pl.multiple_of(block * LANES, LANES), LANES)


def prep_kernel(points, len_low, len_high, high, at, out, scale_low, scale_high, high_out):
    scale_low[...] = scale_column(len_low)
    scale_high[...] = scale_column(len_high)
    high_out[...] = high[...]
    for m in range(points.shape[0]):
        out[place_of(m, at), :] = left(points[m], scale_low[...]).T.astype(BF16)


def column_of(line, out, rows):
    out[rows, :] = jnp.broadcast_to(line, (LANES, LANES)).T


def weighted(cols, rows, column):
    term = jnp.exp2(jnp.dot(cols, rows, preferred_element_type=F32))
    count, wide = term.shape
    term = term * jnp.concatenate([column] * (wide // LANES), 1)
    return jnp.sum(term.reshape(count // 8, 8, wide), axis=0)


def mu_kernel(held, rows_in, scale, high, rho, at, out, cols_out, even, odd, total, lines):
    blocks = held.shape[0]

    def side(r):
        parts = [right(held[r, q * FEATS : (q + 1) * FEATS, :], scale[...]) for q in range(RUN_BLOCKS)]
        return jnp.concatenate([p.astype(BF16) for p in parts], 1)

    def work(r, runs):
        weights = held[r, PACKED - 8 :, :]
        for i in range(0, rows_in.shape[0], MU_CHUNK):
            rows = slice(i, i + MU_CHUNK)
            acc = total[rows, :]
            term = jnp.exp2(jnp.dot(rows_in[rows, :], runs[...], preferred_element_type=F32))
            for q in range(RUN_BLOCKS):
                acc = acc + term[:, q * LANES : (q + 1) * LANES] * weights[q : q + 1, :]
            total[rows, :] = acc

    total[...] = jnp.zeros_like(total)
    held_sides = (even, odd)
    even[...] = side(0)
    for r in range(blocks):
        if r + 1 < blocks:
            held_sides[(r + 1) % 2][...] = side(r + 1)
        work(r, held_sides[r % 2])
    for r in range(blocks):
        cols_out[r] = held[r, RUN_BLOCKS * FEATS : PACKED - 8, :]
    for k in range(lines.shape[0]):
        lines[k : k + 1, :] = jnp.sum(total[k * LANES : (k + 1) * LANES, :].T, axis=0, keepdims=True)
    mu = lines[...]
    row = lax.broadcasted_iota(jnp.int32, mu.shape, 0)
    target = -rho[0] * mu
    target = jnp.where(row == at[0], target + high[...], target)
    for i in range(out.shape[0]):
        out[i] = jnp.where(row == i, mu, target)


def lines_of(total):
    line = jnp.sum(total[...], axis=0, keepdims=True)
    return jnp.concatenate([line[:, k : k + LANES] for k in range(0, line.shape[1], LANES)], 0)


def sides_kernel(points, cols, scale, at, rows_out, cols_out):
    for m in range(points.shape[0]):
        rows_out[:, place_of(m, at)] = left(points[m], scale[...]).astype(BF16)
    for k in range(cols.shape[0]):
        cols_out[k * LANES : (k + 1) * LANES, :] = right(cols[k], scale[...]).T.astype(BF16)


def first_kernel(held, rows_in, cols_in, high, rho, noise, at, out, target_out, mu_out, sums):
    total = jnp.sum(held[...], axis=0)
    row = lax.broadcasted_iota(jnp.int32, total.shape, 0)
    own = row == at[0]
    target = jnp.where(own, high[...] - rho[0] * total, total)
    target_out[...] = target
    mu_out[...] = jnp.sum(jnp.where(own, total, 0.0), axis=0, keepdims=True)
    own_target = jnp.sum(jnp.where(own, target, 0.0), axis=0, keepdims=True)
    size = 2 * LANES

    for k in range(0, cols_in.shape[0], size):
        cols = cols_in[k : k + size, :]
        acc = jnp.zeros((size, LANES), F32)
        for c in range(0, rows_in.shape[1], WIDE):
            term = jnp.exp2(jnp.dot(cols, rows_in[:, c : c + WIDE], preferred_element_type=F32))
            for q in range(0, WIDE, LANES):
                s = (c + q) // LANES
                acc = acc + term[:, q : q + LANES] * target_out[s : s + 1, :]
        for q in range(0, size, LANES):
            at_row = (k + q) // LANES
            sums[at_row : at_row + 1, :] = jnp.sum(acc[q : q + LANES, :].T, axis=0, keepdims=True)
    image = sums[...]
    image = jnp.where(lax.broadcasted_iota(jnp.int32, image.shape, 0) == at[1], image + noise[0] * own_target, image)
    for i in range(out.shape[0]):
        out[i] = image


def second_kernel(held, rows_in, cols_in, noise, at, out, column, total):
    image = jnp.sum(held[...], axis=0)
    mine = lax.broadcasted_iota(jnp.int32, image.shape, 0) == at[1]
    own = jnp.sum(jnp.where(mine, image, 0.0), axis=0, keepdims=True)
    for k in range(image.shape[0]):
        column_of(image[k : k + 1, :], column, slice(k * LANES, (k + 1) * LANES))
    total[...] = jnp.zeros_like(total)

    for i in range(0, cols_in.shape[0], CHUNK):
        rows = slice(i, i + CHUNK)
        for c in range(0, rows_in.shape[1], WIDE):
            total[:, c : c + WIDE] += weighted(cols_in[rows, :], rows_in[:, c : c + WIDE], column[rows, :])
    last = lines_of(total)
    row = lax.broadcasted_iota(jnp.int32, last.shape, 0)
    last = jnp.where(row == at[0], last + noise[0] * own, last)
    extra = jnp.broadcast_to(own, (8, LANES))
    for i in range(out.shape[0]):
        out[i, : last.shape[0], :] = last
        out[i, last.shape[0] :, :] = extra


def two_sum(a, b):
    s = a + b
    t = s - a
    return s, (a - (s - t)) + (b - t)


def pair_add(x, y):
    s, e = two_sum(x[0], y[0])
    return two_sum(s, e + (x[1] + y[1]))


def product(a, b):
    ah = a.astype(BF16).astype(F32)
    bh = b.astype(BF16).astype(F32)
    al, bl = a - ah, b - bh
    s, e = two_sum(ah * bh, ah * bl + al * bh)
    return two_sum(s, e + al * bl)


def pair_product(x, y):
    s, e = product(x[0], y[0])
    return two_sum(s, e + (x[0] * y[1] + x[1] * y[0]))


def minus(x):
    return -x[0], -x[1]


def pair_ratio(x, y):
    q = x[0] / y[0]
    rest = pair_add(x, minus(pair_product((q, jnp.zeros_like(q)), y)))
    return two_sum(q, (rest[0] + rest[1]) / y[0])


def fold_rows(x):
    high, low = x
    count = high.shape[0]
    while count > 8:
        count //= 2
        high, low = pair_add((high[:count], low[:count]), (high[count:], low[count:]))
    return high, low


def moments_kernel(held, target, at, out, own_out):
    count = target.shape[0]
    last = jnp.sum(held[:, :count, :], axis=0)
    image = held[:, count, :]
    b = target[...]
    for i, (p, q) in enumerate(((b, b), (b, image), (image, image), (image, last))):
        high, low = fold_rows(product(p, q))
        for shift in (4, 2, 1):
            high, low = pair_add((high, low), (pltpu.roll(high, shift, 0), pltpu.roll(low, shift, 0)))
        for j in range(out.shape[0]):
            out[j, i : i + 1, :] = high[:1]
            out[j, 4 + i : 5 + i, :] = low[:1]
    own = lax.broadcasted_iota(jnp.int32, b.shape, 0) == at[0]
    for i, v in enumerate((b, image, last)):
        own_out[i : i + 1, :] = jnp.sum(jnp.where(own, v, 0.0), axis=0, keepdims=True)


def final_kernel(held, own, x_out, r_out):
    pairs = [(held[j], pltpu.roll(held[j], 4, 0)) for j in range(held.shape[0])]
    while len(pairs) > 1:
        pairs = [pair_add(a, b) for a, b in zip(pairs[::2], pairs[1::2])]
    h, l = pairs[0]
    for shift in (64, 32, 16, 8, 4, 2, 1):
        h, l = pair_add((h, l), (pltpu.roll(h, shift, 1), pltpu.roll(l, shift, 1)))
    sums = [(h[i : i + 1], l[i : i + 1]) for i in range(4)]
    m0, m1, m2, m3 = sums
    alpha = pair_ratio(m0, m1)
    ratio = pair_ratio(m2, m1)
    v1 = pair_add(m2, minus(pair_product(m1, pair_ratio(m1, m0))))
    v2 = pair_add(m3, minus(pair_product(m2, ratio)))
    scale = pair_product(alpha, ratio)
    alpha0, grow = alpha[0], scale[0]
    alpha1 = (v1[0] + v1[1]) / (v2[0] + v2[1])
    b, image, last = own[0:1, :], own[1:2, :], own[2:3, :]
    x_out[...] = alpha0 * b + alpha1 * (grow * b - alpha0 * image)
    r_out[...] = (b - alpha0 * image) - alpha1 * (grow * image - alpha0 * last)


def exchange_z(blocks, step, size):
    return lax.ppermute(blocks, "z", [(i, i ^ step) for i in range(size)])


def exchange(blocks, axes):
    return lax.all_to_all(blocks, axes, 0, 0, tiled=True)


def local(runs, weights, points, high, len_low, len_high, rho, noise):
    n_row, n_col = lax.axis_size(ROWS), lax.axis_size(COLS)
    at = jnp.stack([lax.axis_index(ROWS), lax.axis_index(COLS)]).astype(jnp.int32)
    high = high.reshape(1, LANES)
    cols_len, rows_len = n_col * LANES, n_row * LANES
    size = lax.axis_size("z")
    to_col = pl.pallas_call(
        pack_kernel,
        out_shape=shape((n_col, PACKED, LANES)),
        in_specs=[HBM] * 3,
        out_specs=HBM,
        scratch_shapes=[
            pltpu.VMEM((FEATS, RUN_BLOCKS * LANES), F32),
            pltpu.VMEM((1, RUN_BLOCKS * LANES), F32),
            pltpu.VMEM((FEATS, LANES), F32),
            pltpu.VMEM((PACKED, LANES), F32),
            pltpu.SemaphoreType.DMA((3,)),
            pltpu.SemaphoreType.DMA((n_col,)),
        ],
        compiler_params=params(60),
        name="pack",
    )(runs, weights.reshape(1, RUN_BLOCKS * LANES), points)
    far = exchange_z(points, 4, size)
    to_col, far = lax.optimization_barrier((to_col, far))
    by_col = exchange(to_col, COLS)
    near = jnp.stack([points, far])
    by_row = jnp.concatenate([near] + [exchange_z(near, step, size) for step in (1, 2, 3)], 0)
    by_row = lax.all_gather(by_row, "core", axis=0, tiled=True)
    row_low, scale_low, scale_high, high = pl.pallas_call(
        prep_kernel,
        out_shape=(shape((rows_len, DEPTH), BF16), shape((FEATS, LANES)), shape((FEATS, LANES)), shape((1, LANES))),
        in_specs=[VMEM, SMEM, SMEM, VMEM, SMEM],
        out_specs=(VMEM,) * 4,
        compiler_params=params(4),
        name="prep",
    )(by_row, len_low, len_high, high, at)
    mu_terms, col_points = pl.pallas_call(
        mu_kernel,
        out_shape=(shape((n_row, n_row, LANES)), shape((n_col, FEATS, LANES))),
        in_specs=[VMEM] * 4 + [SMEM] * 2,
        out_specs=(VMEM,) * 2,
        scratch_shapes=[
            pltpu.VMEM((DEPTH, RUN_BLOCKS * LANES), BF16),
            pltpu.VMEM((DEPTH, RUN_BLOCKS * LANES), BF16),
            pltpu.VMEM((rows_len, LANES), F32),
            pltpu.VMEM((n_row, LANES), F32),
        ],
        compiler_params=params(16),
        name="mu",
    )(by_col, row_low, scale_low, high, rho, at)
    mu_held = exchange(mu_terms, ROWS)
    row_parts, col_parts = pl.pallas_call(
        sides_kernel,
        out_shape=(shape((DEPTH, rows_len), BF16), shape((cols_len, DEPTH), BF16)),
        in_specs=[VMEM] * 3 + [SMEM],
        out_specs=(VMEM,) * 2,
        compiler_params=params(4),
        name="sides",
    )(by_row, col_points, scale_high, at)
    image_terms, target, mu = pl.pallas_call(
        first_kernel,
        out_shape=(shape((n_col, n_col, LANES)), shape((n_row, LANES)), shape((1, LANES))),
        in_specs=[VMEM] * 4 + [SMEM] * 3,
        out_specs=(VMEM,) * 3,
        scratch_shapes=[pltpu.VMEM((n_col, LANES), F32)],
        compiler_params=params(4),
        name="first",
    )(mu_held, row_parts, col_parts, high, rho, noise, at)
    image_held = exchange(image_terms, COLS)
    last_terms = pl.pallas_call(
        second_kernel,
        out_shape=shape((n_row, n_row + 8, LANES)),
        in_specs=[VMEM] * 3 + [SMEM] * 2,
        out_specs=VMEM,
        scratch_shapes=[pltpu.VMEM((cols_len, LANES), F32), pltpu.VMEM((8, rows_len), F32)],
        compiler_params=params(8),
        name="second",
    )(image_held, row_parts, col_parts, noise, at)
    last_held = exchange(last_terms, ROWS)
    moments, own = pl.pallas_call(
        moments_kernel,
        out_shape=(shape((n_col, 8, LANES)), shape((8, LANES))),
        in_specs=[VMEM] * 2 + [SMEM],
        out_specs=(VMEM,) * 2,
        compiler_params=params(4),
        name="moments",
    )(last_held, target, at)
    moments_held = exchange(moments, COLS)
    x, r = pl.pallas_call(
        final_kernel,
        out_shape=(shape((1, LANES)), shape((1, LANES))),
        in_specs=[VMEM] * 2,
        out_specs=(VMEM,) * 2,
        compiler_params=params(4),
        name="final",
    )(moments_held, own)
    return mu.reshape(LANES), x.reshape(LANES), r.reshape(LANES)


def solution(mesh):
    spread = P(AXES)
    wide = P(None, AXES)
    fine = Mesh(mesh.devices.reshape(4, 2, 4, 8), AXES)
    return jax.shard_map(
        local,
        mesh=fine,
        in_specs=(wide, spread, wide, spread, P(), P(), P(), P()),
        out_specs=(spread,) * 3,
        check_vma=False,
    )
```

```python
import math

import jax
import jax.numpy as jnp
from jax import lax
from jax.experimental import pallas as pl
from jax.experimental.pallas import tpu as pltpu
from jax.sharding import Mesh
from jax.sharding import PartitionSpec as P

F32 = jnp.float32
BF16 = jnp.bfloat16
FEATS = 24
LANES = 128
RUN_BLOCKS = 4
WIDE = CHUNK = 512
MU_CHUNK = 256
PACKED = RUN_BLOCKS * FEATS + FEATS + 8
DEPTH = 160
ROOT = math.sqrt(math.log2(math.e))
VMEM = pl.BlockSpec(memory_space=pltpu.VMEM)
AXES = ("y", "core", "x", "z")
ROWS = ("core", "z")
COLS = ("y", "x")
HBM = pl.BlockSpec(memory_space=pltpu.HBM)
SMEM = pl.BlockSpec(memory_space=pltpu.SMEM)


def params(mib):
    return pltpu.CompilerParams(vmem_limit_bytes=mib * 1024 * 1024)


def shape(dims, kind=F32):
    return jax.ShapeDtypeStruct(dims, kind)


def split(x):
    high = x.astype(BF16).astype(F32)
    rest = x - high
    mid = rest.astype(BF16).astype(F32)
    return high, mid, rest - mid


def norm_rows(norm, at):
    high, mid, low = split(norm)
    row = lax.broadcasted_iota(jnp.int32, (8, norm.shape[1]), 0)
    ones = jnp.where((row >= 3 - at) & (row < 6 - at), 1.0, 0.0)
    return jnp.where(row == at, high, jnp.where(row == at + 1, mid, jnp.where(row == at + 2, low, ones)))


def scaled(points, scale):
    return (points - 0.5) * scale


def half_norm(points):
    return -0.5 * jnp.sum(points * points, axis=0, keepdims=True)


def left(points, scale):
    u = scaled(points, scale)
    high, mid, low = split(u)
    norms = norm_rows(half_norm(u), 0)
    return jnp.concatenate([high, high, high, mid, mid, low, norms, jnp.zeros_like(norms)], 0)


def right(points, scale):
    v = scaled(points, scale)
    high, mid, low = split(v)
    norms = norm_rows(half_norm(v), 3)
    return jnp.concatenate([high, mid, low, high, mid, high, norms, jnp.zeros_like(norms)], 0)


def pack_kernel(runs_hbm, weights_hbm, points_hbm, out, runs, weights, points, block, sems, out_sems):
    sources, held = (runs_hbm, weights_hbm, points_hbm), (runs, weights, points)
    copies = [pltpu.make_async_copy(a, b, sems.at[i]) for i, (a, b) in enumerate(zip(sources, held))]
    for copy in copies:
        copy.start()
    for copy in copies:
        copy.wait()
    last = jnp.broadcast_to(weights[:, :LANES], (8, LANES))
    row = lax.broadcasted_iota(jnp.int32, (8, LANES), 0)
    for q in range(RUN_BLOCKS):
        lanes = slice(q * LANES, (q + 1) * LANES)
        block[q * FEATS : (q + 1) * FEATS, :] = runs[:, lanes]
        if q:
            last = jnp.where(row == q, weights[:, lanes], last)
    block[RUN_BLOCKS * FEATS : PACKED - 8, :] = points[...]
    block[PACKED - 8 :, :] = last
    copies = [pltpu.make_async_copy(block, out.at[i], out_sems.at[i]) for i in range(out.shape[0])]
    for copy in copies:
        copy.start()
    for copy in copies:
        copy.wait()


def scale_column(lengths):
    row = lax.broadcasted_iota(jnp.int32, (FEATS, LANES), 0)
    column = jnp.ones((FEATS, LANES), F32)
    for i in range(FEATS):
        column = jnp.where(row == i, lengths[i], column)
    return ROOT / column


def place_of(m, at):
    block = (m >> 3) * 8 + ((at[0] & 7) ^ (m >> 1 & 3) ^ 4 * (m & 1))
    return pl.ds(pl.multiple_of(block * LANES, LANES), LANES)


def prep_kernel(points, len_low, len_high, high, at, out, rows_out, scale_low, scale_high, high_out):
    scale_low[...] = scale_column(len_low)
    scale_high[...] = scale_column(len_high)
    high_out[...] = high[...]
    for m in range(points.shape[0]):
        place = place_of(m, at)
        out[place, :] = left(points[m], scale_low[...]).T.astype(BF16)
        rows_out[:, place] = left(points[m], scale_high[...]).astype(BF16)


def column_of(line, out, rows):
    out[rows, :] = jnp.broadcast_to(line, (LANES, LANES)).T


def weighted(cols, rows, column):
    term = jnp.exp2(jnp.dot(cols, rows, preferred_element_type=F32))
    count, wide = term.shape
    term = term * jnp.concatenate([column] * (wide // LANES), 1)
    return jnp.sum(term.reshape(count // 8, 8, wide), axis=0)


def mu_kernel(held, rows_in, scale, scale_high, high, rho, noise, at, out, cols_out, even, odd, total, lines):
    blocks = held.shape[0]

    def side(r):
        parts = [right(held[r, q * FEATS : (q + 1) * FEATS, :], scale[...]) for q in range(RUN_BLOCKS)]
        return jnp.concatenate([p.astype(BF16) for p in parts], 1)

    def work(r, runs):
        weights = held[r, PACKED - 8 :, :]
        for i in range(0, rows_in.shape[0], MU_CHUNK):
            rows = slice(i, i + MU_CHUNK)
            acc = total[rows, :]
            term = jnp.exp2(jnp.dot(rows_in[rows, :], runs[...], preferred_element_type=F32))
            for q in range(RUN_BLOCKS):
                acc = acc + term[:, q * LANES : (q + 1) * LANES] * weights[q : q + 1, :]
            total[rows, :] = acc

    total[...] = jnp.zeros_like(total)
    held_sides = (even, odd)
    even[...] = side(0)
    for r in range(blocks):
        if r + 1 < blocks:
            held_sides[(r + 1) % 2][...] = side(r + 1)
        work(r, held_sides[r % 2])
        cols = right(held[r, RUN_BLOCKS * FEATS : PACKED - 8, :], scale_high[...])
        cols_out[r * LANES : (r + 1) * LANES, :] = cols.T.astype(BF16)
    for k in range(lines.shape[0]):
        lines[k : k + 1, :] = jnp.sum(total[k * LANES : (k + 1) * LANES, :].T, axis=0, keepdims=True)
    mu = lines[...]
    row = lax.broadcasted_iota(jnp.int32, mu.shape, 0)
    target = -rho[0] * mu
    target = jnp.where(row == at[0], target + high[...], target)
    for i in range(out.shape[0]):
        out[i] = jnp.where(row == i, mu, target)


def lines_of(total):
    line = jnp.sum(total[...], axis=0, keepdims=True)
    return jnp.concatenate([line[:, k : k + LANES] for k in range(0, line.shape[1], LANES)], 0)


def first_kernel(held, rows_in, cols_in, high, rho, noise, at, out, target_out, mu_out, sums):
    total = jnp.sum(held[...], axis=0)
    row = lax.broadcasted_iota(jnp.int32, total.shape, 0)
    own = row == at[0]
    target = jnp.where(own, high[...] - rho[0] * total, total)
    target_out[...] = target
    mu_out[...] = jnp.sum(jnp.where(own, total, 0.0), axis=0, keepdims=True)
    own_target = jnp.sum(jnp.where(own, target, 0.0), axis=0, keepdims=True)
    size = 2 * LANES

    for k in range(0, cols_in.shape[0], size):
        cols = cols_in[k : k + size, :]
        acc = jnp.zeros((size, LANES), F32)
        for c in range(0, rows_in.shape[1], WIDE):
            term = jnp.exp2(jnp.dot(cols, rows_in[:, c : c + WIDE], preferred_element_type=F32))
            for q in range(0, WIDE, LANES):
                s = (c + q) // LANES
                acc = acc + term[:, q : q + LANES] * target_out[s : s + 1, :]
        for q in range(0, size, LANES):
            at_row = (k + q) // LANES
            sums[at_row : at_row + 1, :] = jnp.sum(acc[q : q + LANES, :].T, axis=0, keepdims=True)
    image = sums[...]
    image = jnp.where(lax.broadcasted_iota(jnp.int32, image.shape, 0) == at[1], image + noise[0] * own_target, image)
    for i in range(out.shape[0]):
        out[i] = image


def second_kernel(held, rows_in, cols_in, noise, at, out, column, total):
    image = jnp.sum(held[...], axis=0)
    mine = lax.broadcasted_iota(jnp.int32, image.shape, 0) == at[1]
    own = jnp.sum(jnp.where(mine, image, 0.0), axis=0, keepdims=True)
    for k in range(image.shape[0]):
        column_of(image[k : k + 1, :], column, slice(k * LANES, (k + 1) * LANES))
    total[...] = jnp.zeros_like(total)

    for i in range(0, cols_in.shape[0], CHUNK):
        rows = slice(i, i + CHUNK)
        for c in range(0, rows_in.shape[1], WIDE):
            total[:, c : c + WIDE] += weighted(cols_in[rows, :], rows_in[:, c : c + WIDE], column[rows, :])
    last = lines_of(total)
    row = lax.broadcasted_iota(jnp.int32, last.shape, 0)
    last = jnp.where(row == at[0], last + noise[0] * own, last)
    extra = jnp.broadcast_to(own, (8, LANES))
    for i in range(out.shape[0]):
        out[i, : last.shape[0], :] = last
        out[i, last.shape[0] :, :] = extra


def two_sum(a, b):
    s = a + b
    t = s - a
    return s, (a - (s - t)) + (b - t)


def pair_add(x, y):
    s, e = two_sum(x[0], y[0])
    return two_sum(s, e + (x[1] + y[1]))


def product(a, b):
    ah = a.astype(BF16).astype(F32)
    bh = b.astype(BF16).astype(F32)
    al, bl = a - ah, b - bh
    s, e = two_sum(ah * bh, ah * bl + al * bh)
    return two_sum(s, e + al * bl)


def pair_product(x, y):
    s, e = product(x[0], y[0])
    return two_sum(s, e + (x[0] * y[1] + x[1] * y[0]))


def minus(x):
    return -x[0], -x[1]


def pair_ratio(x, y):
    q = x[0] / y[0]
    rest = pair_add(x, minus(pair_product((q, jnp.zeros_like(q)), y)))
    return two_sum(q, (rest[0] + rest[1]) / y[0])


def fold_rows(x):
    high, low = x
    count = high.shape[0]
    while count > 8:
        count //= 2
        high, low = pair_add((high[:count], low[:count]), (high[count:], low[count:]))
    return high, low


def moments_kernel(held, target, at, out, own_out):
    count = target.shape[0]
    last = jnp.sum(held[:, :count, :], axis=0)
    image = held[:, count, :]
    b = target[...]
    for i, (p, q) in enumerate(((b, b), (b, image), (image, image), (image, last))):
        high, low = fold_rows(product(p, q))
        for shift in (4, 2, 1):
            high, low = pair_add((high, low), (pltpu.roll(high, shift, 0), pltpu.roll(low, shift, 0)))
        for j in range(out.shape[0]):
            out[j, i : i + 1, :] = high[:1]
            out[j, 4 + i : 5 + i, :] = low[:1]
    own = lax.broadcasted_iota(jnp.int32, b.shape, 0) == at[0]
    for i, v in enumerate((b, image, last)):
        own_out[i : i + 1, :] = jnp.sum(jnp.where(own, v, 0.0), axis=0, keepdims=True)


def final_kernel(held, own, x_out, r_out):
    pairs = [(held[j], pltpu.roll(held[j], 4, 0)) for j in range(held.shape[0])]
    while len(pairs) > 1:
        pairs = [pair_add(a, b) for a, b in zip(pairs[::2], pairs[1::2])]
    h, l = pairs[0]
    for shift in (64, 32, 16, 8, 4, 2, 1):
        h, l = pair_add((h, l), (pltpu.roll(h, shift, 1), pltpu.roll(l, shift, 1)))
    sums = [(h[i : i + 1], l[i : i + 1]) for i in range(4)]
    m0, m1, m2, m3 = sums
    alpha = pair_ratio(m0, m1)
    ratio = pair_ratio(m2, m1)
    v1 = pair_add(m2, minus(pair_product(m1, pair_ratio(m1, m0))))
    v2 = pair_add(m3, minus(pair_product(m2, ratio)))
    scale = pair_product(alpha, ratio)
    alpha0, grow = alpha[0], scale[0]
    alpha1 = (v1[0] + v1[1]) / (v2[0] + v2[1])
    b, image, last = own[0:1, :], own[1:2, :], own[2:3, :]
    x_out[...] = alpha0 * b + alpha1 * (grow * b - alpha0 * image)
    r_out[...] = (b - alpha0 * image) - alpha1 * (grow * image - alpha0 * last)


def exchange_z(blocks, step, size):
    return lax.ppermute(blocks, "z", [(i, i ^ step) for i in range(size)])


def exchange(blocks, axes):
    return lax.all_to_all(blocks, axes, 0, 0, tiled=True)


def local(runs, weights, points, high, len_low, len_high, rho, noise):
    n_row, n_col = lax.axis_size(ROWS), lax.axis_size(COLS)
    at = jnp.stack([lax.axis_index(ROWS), lax.axis_index(COLS)]).astype(jnp.int32)
    high = high.reshape(1, LANES)
    cols_len, rows_len = n_col * LANES, n_row * LANES
    size = lax.axis_size("z")
    to_col = pl.pallas_call(
        pack_kernel,
        out_shape=shape((n_col, PACKED, LANES)),
        in_specs=[HBM] * 3,
        out_specs=HBM,
        scratch_shapes=[
            pltpu.VMEM((FEATS, RUN_BLOCKS * LANES), F32),
            pltpu.VMEM((1, RUN_BLOCKS * LANES), F32),
            pltpu.VMEM((FEATS, LANES), F32),
            pltpu.VMEM((PACKED, LANES), F32),
            pltpu.SemaphoreType.DMA((3,)),
            pltpu.SemaphoreType.DMA((n_col,)),
        ],
        compiler_params=params(60),
        name="pack",
    )(runs, weights.reshape(1, RUN_BLOCKS * LANES), points)
    far = exchange_z(points, 4, size)
    to_col, far = lax.optimization_barrier((to_col, far))
    by_col = exchange(to_col, COLS)
    near = jnp.stack([points, far])
    by_row = jnp.concatenate([near] + [exchange_z(near, step, size) for step in (1, 2, 3)], 0)
    by_row = lax.all_gather(by_row, "core", axis=0, tiled=True)
    row_low, row_parts, scale_low, scale_high, high = pl.pallas_call(
        prep_kernel,
        out_shape=(
            shape((rows_len, DEPTH), BF16),
            shape((DEPTH, rows_len), BF16),
            shape((FEATS, LANES)),
            shape((FEATS, LANES)),
            shape((1, LANES)),
        ),
        in_specs=[VMEM, SMEM, SMEM, VMEM, SMEM],
        out_specs=(VMEM,) * 5,
        compiler_params=params(4),
        name="prep",
    )(by_row, len_low, len_high, high, at)
    mu_terms, col_parts = pl.pallas_call(
        mu_kernel,
        out_shape=(shape((n_row, n_row, LANES)), shape((cols_len, DEPTH), BF16)),
        in_specs=[VMEM] * 5 + [SMEM] * 3,
        out_specs=(VMEM,) * 2,
        scratch_shapes=[
            pltpu.VMEM((DEPTH, RUN_BLOCKS * LANES), BF16),
            pltpu.VMEM((DEPTH, RUN_BLOCKS * LANES), BF16),
            pltpu.VMEM((rows_len, LANES), F32),
            pltpu.VMEM((n_row, LANES), F32),
        ],
        compiler_params=params(16),
        name="mu",
    )(by_col, row_low, scale_low, scale_high, high, rho, noise, at)
    mu_held = exchange(mu_terms, ROWS)
    image_terms, target, mu = pl.pallas_call(
        first_kernel,
        out_shape=(shape((n_col, n_col, LANES)), shape((n_row, LANES)), shape((1, LANES))),
        in_specs=[VMEM] * 4 + [SMEM] * 3,
        out_specs=(VMEM,) * 3,
        scratch_shapes=[pltpu.VMEM((n_col, LANES), F32)],
        compiler_params=params(4),
        name="first",
    )(mu_held, row_parts, col_parts, high, rho, noise, at)
    image_held = exchange(image_terms, COLS)
    last_terms = pl.pallas_call(
        second_kernel,
        out_shape=shape((n_row, n_row + 8, LANES)),
        in_specs=[VMEM] * 3 + [SMEM] * 2,
        out_specs=VMEM,
        scratch_shapes=[pltpu.VMEM((cols_len, LANES), F32), pltpu.VMEM((8, rows_len), F32)],
        compiler_params=params(8),
        name="second",
    )(image_held, row_parts, col_parts, noise, at)
    last_held = exchange(last_terms, ROWS)
    moments, own = pl.pallas_call(
        moments_kernel,
        out_shape=(shape((n_col, 8, LANES)), shape((8, LANES))),
        in_specs=[VMEM] * 2 + [SMEM],
        out_specs=(VMEM,) * 2,
        compiler_params=params(4),
        name="moments",
    )(last_held, target, at)
    moments_held = exchange(moments, COLS)
    x, r = pl.pallas_call(
        final_kernel,
        out_shape=(shape((1, LANES)), shape((1, LANES))),
        in_specs=[VMEM] * 2,
        out_specs=(VMEM,) * 2,
        compiler_params=params(4),
        name="final",
    )(moments_held, own)
    return mu.reshape(LANES), x.reshape(LANES), r.reshape(LANES)


def solution(mesh):
    spread = P(AXES)
    wide = P(None, AXES)
    fine = Mesh(mesh.devices.reshape(4, 2, 4, 8), AXES)
    return jax.shard_map(
        local,
        mesh=fine,
        in_specs=(wide, spread, wide, spread, P(), P(), P(), P()),
        out_specs=(spread,) * 3,
        check_vma=False,
    )
```

```python
import math

import jax
import jax.numpy as jnp
from jax import lax
from jax.experimental import pallas as pl
from jax.experimental.pallas import tpu as pltpu
from jax.sharding import Mesh
from jax.sharding import PartitionSpec as P

F32 = jnp.float32
BF16 = jnp.bfloat16
FEATS = 24
LANES = 128
RUN_BLOCKS = 4
WIDE = CHUNK = 512
MU_CHUNK = 256
PACKED = RUN_BLOCKS * FEATS + FEATS + 8
DEPTH = 160
ROOT = math.sqrt(math.log2(math.e))
VMEM = pl.BlockSpec(memory_space=pltpu.VMEM)
AXES = ("y", "core", "x", "z")
ROWS = ("core", "z")
COLS = ("y", "x")
HBM = pl.BlockSpec(memory_space=pltpu.HBM)
SMEM = pl.BlockSpec(memory_space=pltpu.SMEM)


def params(mib):
    return pltpu.CompilerParams(vmem_limit_bytes=mib * 1024 * 1024)


def shape(dims, kind=F32):
    return jax.ShapeDtypeStruct(dims, kind)


def split(x):
    high = x.astype(BF16).astype(F32)
    rest = x - high
    mid = rest.astype(BF16).astype(F32)
    return high, mid, rest - mid


def norm_rows(norm, at):
    high, mid, low = split(norm)
    row = lax.broadcasted_iota(jnp.int32, (8, norm.shape[1]), 0)
    ones = jnp.where((row >= 3 - at) & (row < 6 - at), 1.0, 0.0)
    return jnp.where(row == at, high, jnp.where(row == at + 1, mid, jnp.where(row == at + 2, low, ones)))


def scaled(points, scale):
    return (points - 0.5) * scale


def half_norm(points):
    return -0.5 * jnp.sum(points * points, axis=0, keepdims=True)


def left(points, scale):
    u = scaled(points, scale)
    high, mid, low = split(u)
    norms = norm_rows(half_norm(u), 0)
    return jnp.concatenate([high, high, high, mid, mid, low, norms, jnp.zeros_like(norms)], 0)


def right(points, scale):
    v = scaled(points, scale)
    high, mid, low = split(v)
    norms = norm_rows(half_norm(v), 3)
    return jnp.concatenate([high, mid, low, high, mid, high, norms, jnp.zeros_like(norms)], 0)


def scale_column(lengths):
    row = lax.broadcasted_iota(jnp.int32, (FEATS, LANES), 0)
    column = jnp.ones((FEATS, LANES), F32)
    for i in range(FEATS):
        column = jnp.where(row == i, lengths[i], column)
    return ROOT / column


def pack_kernel(*refs):
    sources, (out, scale_low, scale_high) = refs[:5], refs[5:8]
    held, (block, sems, out_sems) = refs[8:13], refs[13:]
    copies = [pltpu.make_async_copy(a, b, sems.at[i]) for i, (a, b) in enumerate(zip(sources, held))]
    for copy in copies:
        copy.start()
    for copy in copies:
        copy.wait()
    runs, weights, points, len_low, len_high = held
    last = jnp.broadcast_to(weights[:, :LANES], (8, LANES))
    row = lax.broadcasted_iota(jnp.int32, (8, LANES), 0)
    for q in range(RUN_BLOCKS):
        lanes = slice(q * LANES, (q + 1) * LANES)
        block[q * FEATS : (q + 1) * FEATS, :] = runs[:, lanes]
        if q:
            last = jnp.where(row == q, weights[:, lanes], last)
    block[RUN_BLOCKS * FEATS : PACKED - 8, :] = points[...]
    block[PACKED - 8 :, :] = last
    copies = [pltpu.make_async_copy(block, out.at[i], out_sems.at[i]) for i in range(out.shape[0])]
    for copy in copies:
        copy.start()
    scale_low[...] = scale_column(len_low)
    scale_high[...] = scale_column(len_high)
    for copy in copies:
        copy.wait()


def place_of(m, at):
    block = (m >> 3) * 8 + ((at[0] & 7) ^ (m >> 1 & 3) ^ 4 * (m & 1))
    return pl.ds(pl.multiple_of(block * LANES, LANES), LANES)


def prep_kernel(points, scale_low, scale_high, high, at, out, rows_out, high_out):
    high_out[...] = high[...]
    for m in range(points.shape[0]):
        place = place_of(m, at)
        out[place, :] = left(points[m], scale_low[...]).T.astype(BF16)
        rows_out[:, place] = left(points[m], scale_high[...]).astype(BF16)


def column_of(line, out, rows):
    out[rows, :] = jnp.broadcast_to(line, (LANES, LANES)).T


def weighted(cols, rows, column):
    term = jnp.exp2(jnp.dot(cols, rows, preferred_element_type=F32))
    count, wide = term.shape
    term = term * jnp.concatenate([column] * (wide // LANES), 1)
    return jnp.sum(term.reshape(count // 8, 8, wide), axis=0)


def mu_kernel(held, rows_in, scale, scale_high, high, rho, noise, at, out, cols_out, even, odd, total, lines):
    blocks = held.shape[0]

    def side(r):
        parts = [right(held[r, q * FEATS : (q + 1) * FEATS, :], scale[...]) for q in range(RUN_BLOCKS)]
        return jnp.concatenate([p.astype(BF16) for p in parts], 1)

    def work(r, runs):
        weights = held[r, PACKED - 8 :, :]
        for i in range(0, rows_in.shape[0], MU_CHUNK):
            rows = slice(i, i + MU_CHUNK)
            acc = total[rows, :]
            term = jnp.exp2(jnp.dot(rows_in[rows, :], runs[...], preferred_element_type=F32))
            for q in range(RUN_BLOCKS):
                acc = acc + term[:, q * LANES : (q + 1) * LANES] * weights[q : q + 1, :]
            total[rows, :] = acc

    total[...] = jnp.zeros_like(total)
    held_sides = (even, odd)
    even[...] = side(0)
    for r in range(blocks):
        if r + 1 < blocks:
            held_sides[(r + 1) % 2][...] = side(r + 1)
        work(r, held_sides[r % 2])
        cols = right(held[r, RUN_BLOCKS * FEATS : PACKED - 8, :], scale_high[...])
        cols_out[r * LANES : (r + 1) * LANES, :] = cols.T.astype(BF16)
    for k in range(lines.shape[0]):
        lines[k : k + 1, :] = jnp.sum(total[k * LANES : (k + 1) * LANES, :].T, axis=0, keepdims=True)
    mu = lines[...]
    row = lax.broadcasted_iota(jnp.int32, mu.shape, 0)
    target = -rho[0] * mu
    target = jnp.where(row == at[0], target + high[...], target)
    for i in range(out.shape[0]):
        out[i] = jnp.where(row == i, mu, target)


def lines_of(total):
    line = jnp.sum(total[...], axis=0, keepdims=True)
    return jnp.concatenate([line[:, k : k + LANES] for k in range(0, line.shape[1], LANES)], 0)


def first_kernel(held, rows_in, cols_in, high, rho, noise, at, out, target_out, mu_out, sums):
    total = jnp.sum(held[...], axis=0)
    row = lax.broadcasted_iota(jnp.int32, total.shape, 0)
    own = row == at[0]
    target = jnp.where(own, high[...] - rho[0] * total, total)
    target_out[...] = target
    mu_out[...] = jnp.sum(jnp.where(own, total, 0.0), axis=0, keepdims=True)
    own_target = jnp.sum(jnp.where(own, target, 0.0), axis=0, keepdims=True)
    size = 2 * LANES

    for k in range(0, cols_in.shape[0], size):
        cols = cols_in[k : k + size, :]
        acc = jnp.zeros((size, LANES), F32)
        for c in range(0, rows_in.shape[1], WIDE):
            term = jnp.exp2(jnp.dot(cols, rows_in[:, c : c + WIDE], preferred_element_type=F32))
            for q in range(0, WIDE, LANES):
                s = (c + q) // LANES
                acc = acc + term[:, q : q + LANES] * target_out[s : s + 1, :]
        for q in range(0, size, LANES):
            at_row = (k + q) // LANES
            sums[at_row : at_row + 1, :] = jnp.sum(acc[q : q + LANES, :].T, axis=0, keepdims=True)
    image = sums[...]
    image = jnp.where(lax.broadcasted_iota(jnp.int32, image.shape, 0) == at[1], image + noise[0] * own_target, image)
    for i in range(out.shape[0]):
        out[i] = image


def second_kernel(held, rows_in, cols_in, noise, at, out, column, total):
    image = jnp.sum(held[...], axis=0)
    mine = lax.broadcasted_iota(jnp.int32, image.shape, 0) == at[1]
    own = jnp.sum(jnp.where(mine, image, 0.0), axis=0, keepdims=True)
    for k in range(image.shape[0]):
        column_of(image[k : k + 1, :], column, slice(k * LANES, (k + 1) * LANES))
    total[...] = jnp.zeros_like(total)

    for i in range(0, cols_in.shape[0], CHUNK):
        rows = slice(i, i + CHUNK)
        for c in range(0, rows_in.shape[1], WIDE):
            total[:, c : c + WIDE] += weighted(cols_in[rows, :], rows_in[:, c : c + WIDE], column[rows, :])
    last = lines_of(total)
    row = lax.broadcasted_iota(jnp.int32, last.shape, 0)
    last = jnp.where(row == at[0], last + noise[0] * own, last)
    for i in range(out.shape[0]):
        for k in range(last.shape[0]):
            out[i, k] = last[k : k + 1, :]
        out[i, last.shape[0]] = own


def two_sum(a, b):
    s = a + b
    t = s - a
    return s, (a - (s - t)) + (b - t)


def pair_add(x, y):
    s, e = two_sum(x[0], y[0])
    return two_sum(s, e + (x[1] + y[1]))


def product(a, b):
    ah = a.astype(BF16).astype(F32)
    bh = b.astype(BF16).astype(F32)
    al, bl = a - ah, b - bh
    s, e = two_sum(ah * bh, ah * bl + al * bh)
    return two_sum(s, e + al * bl)


def pair_product(x, y):
    s, e = product(x[0], y[0])
    return two_sum(s, e + (x[0] * y[1] + x[1] * y[0]))


def minus(x):
    return -x[0], -x[1]


def pair_ratio(x, y):
    q = x[0] / y[0]
    rest = pair_add(x, minus(pair_product((q, jnp.zeros_like(q)), y)))
    return two_sum(q, (rest[0] + rest[1]) / y[0])


def fold_rows(x):
    high, low = x
    count = high.shape[0]
    while count > 8:
        count //= 2
        high, low = pair_add((high[:count], low[:count]), (high[count:], low[count:]))
    return high, low


def moments_kernel(held, target, at, out, own_out):
    count = target.shape[0]
    senders = range(held.shape[0])
    last = jnp.concatenate([sum(held[j, k] for j in senders) for k in range(count)], 0)
    image = jnp.concatenate([held[j, count] for j in senders], 0)
    b = target[...]
    for i, (p, q) in enumerate(((b, b), (b, image), (image, image), (image, last))):
        high, low = fold_rows(product(p, q))
        for shift in (4, 2, 1):
            high, low = pair_add((high, low), (pltpu.roll(high, shift, 0), pltpu.roll(low, shift, 0)))
        for j in range(out.shape[0]):
            out[j, i : i + 1, :] = high[:1]
            out[j, 4 + i : 5 + i, :] = low[:1]
    own = lax.broadcasted_iota(jnp.int32, b.shape, 0) == at[0]
    for i, v in enumerate((b, image, last)):
        own_out[i : i + 1, :] = jnp.sum(jnp.where(own, v, 0.0), axis=0, keepdims=True)


def final_kernel(held, own, x_out, r_out):
    pairs = [(held[j], pltpu.roll(held[j], 4, 0)) for j in range(held.shape[0])]
    while len(pairs) > 1:
        pairs = [pair_add(a, b) for a, b in zip(pairs[::2], pairs[1::2])]
    h, l = pairs[0]
    for shift in (64, 32, 16, 8, 4, 2, 1):
        h, l = pair_add((h, l), (pltpu.roll(h, shift, 1), pltpu.roll(l, shift, 1)))
    sums = [(h[i : i + 1], l[i : i + 1]) for i in range(4)]
    m0, m1, m2, m3 = sums
    alpha = pair_ratio(m0, m1)
    ratio = pair_ratio(m2, m1)
    v1 = pair_add(m2, minus(pair_product(m1, pair_ratio(m1, m0))))
    v2 = pair_add(m3, minus(pair_product(m2, ratio)))
    scale = pair_product(alpha, ratio)
    alpha0, grow = alpha[0], scale[0]
    alpha1 = (v1[0] + v1[1]) / (v2[0] + v2[1])
    b, image, last = own[0:1, :], own[1:2, :], own[2:3, :]
    x_out[...] = alpha0 * b + alpha1 * (grow * b - alpha0 * image)
    r_out[...] = (b - alpha0 * image) - alpha1 * (grow * image - alpha0 * last)


def exchange_z(blocks, step, size):
    return lax.ppermute(blocks, "z", [(i, i ^ step) for i in range(size)])


def exchange(blocks, axes):
    return lax.all_to_all(blocks, axes, 0, 0, tiled=True)


def local(runs, weights, points, high, len_low, len_high, rho, noise):
    n_row, n_col = lax.axis_size(ROWS), lax.axis_size(COLS)
    at = jnp.stack([lax.axis_index(ROWS), lax.axis_index(COLS)]).astype(jnp.int32)
    high = high.reshape(1, LANES)
    cols_len, rows_len = n_col * LANES, n_row * LANES
    size = lax.axis_size("z")
    to_col, scale_low, scale_high = pl.pallas_call(
        pack_kernel,
        out_shape=(shape((n_col, PACKED, LANES)), shape((FEATS, LANES)), shape((FEATS, LANES))),
        in_specs=[HBM] * 5,
        out_specs=(HBM, VMEM, VMEM),
        scratch_shapes=[
            pltpu.VMEM((FEATS, RUN_BLOCKS * LANES), F32),
            pltpu.VMEM((1, RUN_BLOCKS * LANES), F32),
            pltpu.VMEM((FEATS, LANES), F32),
            pltpu.SMEM((FEATS,), F32),
            pltpu.SMEM((FEATS,), F32),
            pltpu.VMEM((PACKED, LANES), F32),
            pltpu.SemaphoreType.DMA((5,)),
            pltpu.SemaphoreType.DMA((n_col,)),
        ],
        compiler_params=params(60),
        name="pack",
    )(runs, weights.reshape(1, RUN_BLOCKS * LANES), points, len_low, len_high)
    far = exchange_z(points, 4, size)
    by_col = exchange(to_col, COLS)
    near = jnp.stack([points, far])
    by_row = jnp.concatenate([near] + [exchange_z(near, step, size) for step in (1, 2, 3)], 0)
    by_row = lax.all_gather(by_row, "core", axis=0, tiled=True)
    row_low, row_parts, high = pl.pallas_call(
        prep_kernel,
        out_shape=(shape((rows_len, DEPTH), BF16), shape((DEPTH, rows_len), BF16), shape((1, LANES))),
        in_specs=[VMEM] * 4 + [SMEM],
        out_specs=(VMEM,) * 3,
        compiler_params=params(4),
        name="prep",
    )(by_row, scale_low, scale_high, high, at)
    mu_terms, col_parts = pl.pallas_call(
        mu_kernel,
        out_shape=(shape((n_row, n_row, LANES)), shape((cols_len, DEPTH), BF16)),
        in_specs=[VMEM] * 5 + [SMEM] * 3,
        out_specs=(VMEM,) * 2,
        scratch_shapes=[
            pltpu.VMEM((DEPTH, RUN_BLOCKS * LANES), BF16),
            pltpu.VMEM((DEPTH, RUN_BLOCKS * LANES), BF16),
            pltpu.VMEM((rows_len, LANES), F32),
            pltpu.VMEM((n_row, LANES), F32),
        ],
        compiler_params=params(16),
        name="mu",
    )(by_col, row_low, scale_low, scale_high, high, rho, noise, at)
    mu_held = exchange(mu_terms, ROWS)
    image_terms, target, mu = pl.pallas_call(
        first_kernel,
        out_shape=(shape((n_col, n_col, LANES)), shape((n_row, LANES)), shape((1, LANES))),
        in_specs=[VMEM] * 4 + [SMEM] * 3,
        out_specs=(VMEM,) * 3,
        scratch_shapes=[pltpu.VMEM((n_col, LANES), F32)],
        compiler_params=params(4),
        name="first",
    )(mu_held, row_parts, col_parts, high, rho, noise, at)
    image_held = exchange(image_terms, COLS)
    last_terms = pl.pallas_call(
        second_kernel,
        out_shape=shape((n_row, n_row + 1, 1, LANES)),
        in_specs=[VMEM] * 3 + [SMEM] * 2,
        out_specs=VMEM,
        scratch_shapes=[pltpu.VMEM((cols_len, LANES), F32), pltpu.VMEM((8, rows_len), F32)],
        compiler_params=params(8),
        name="second",
    )(image_held, row_parts, col_parts, noise, at)
    last_held = exchange(last_terms, ROWS)
    moments, own = pl.pallas_call(
        moments_kernel,
        out_shape=(shape((n_col, 8, LANES)), shape((8, LANES))),
        in_specs=[VMEM] * 2 + [SMEM],
        out_specs=(VMEM,) * 2,
        compiler_params=params(4),
        name="moments",
    )(last_held, target, at)
    moments_held = exchange(moments, COLS)
    x, r = pl.pallas_call(
        final_kernel,
        out_shape=(shape((1, LANES)), shape((1, LANES))),
        in_specs=[VMEM] * 2,
        out_specs=(VMEM,) * 2,
        compiler_params=params(4),
        name="final",
    )(moments_held, own)
    return mu.reshape(LANES), x.reshape(LANES), r.reshape(LANES)


def solution(mesh):
    spread = P(AXES)
    wide = P(None, AXES)
    fine = Mesh(mesh.devices.reshape(4, 2, 4, 8), AXES)
    return jax.shard_map(
        local,
        mesh=fine,
        in_specs=(wide, spread, wide, spread, P(), P(), P(), P()),
        out_specs=(spread,) * 3,
        check_vma=False,
    )
```

```python
import math

import jax
import jax.numpy as jnp
from jax import lax
from jax.experimental import pallas as pl
from jax.experimental.pallas import tpu as pltpu
from jax.sharding import Mesh
from jax.sharding import PartitionSpec as P

F32 = jnp.float32
BF16 = jnp.bfloat16
FEATS = 24
LANES = 128
RUN_BLOCKS = 4
WIDE = CHUNK = 512
MU_CHUNK = 256
PACKED = RUN_BLOCKS * FEATS + FEATS + 8
DEPTH = 160
ROOT = math.sqrt(math.log2(math.e))
VMEM = pl.BlockSpec(memory_space=pltpu.VMEM)
AXES = ("y", "core", "x", "z")
ROWS = ("core", "z")
COLS = ("y", "x")
HBM = pl.BlockSpec(memory_space=pltpu.HBM)
SMEM = pl.BlockSpec(memory_space=pltpu.SMEM)


def params(mib):
    return pltpu.CompilerParams(vmem_limit_bytes=mib * 1024 * 1024)


def shape(dims, kind=F32):
    return jax.ShapeDtypeStruct(dims, kind)


def split(x):
    high = x.astype(BF16).astype(F32)
    rest = x - high
    mid = rest.astype(BF16).astype(F32)
    return high, mid, rest - mid


def norm_rows(norm, at):
    high, mid, low = split(norm)
    row = lax.broadcasted_iota(jnp.int32, (8, norm.shape[1]), 0)
    ones = jnp.where((row >= 3 - at) & (row < 6 - at), 1.0, 0.0)
    return jnp.where(row == at, high, jnp.where(row == at + 1, mid, jnp.where(row == at + 2, low, ones)))


def scaled(points, scale):
    return (points - 0.5) * scale


def half_norm(points):
    return -0.5 * jnp.sum(points * points, axis=0, keepdims=True)


def left(points, scale):
    u = scaled(points, scale)
    high, mid, low = split(u)
    norms = norm_rows(half_norm(u), 0)
    return jnp.concatenate([high, high, high, mid, mid, low, norms, jnp.zeros_like(norms)], 0)


def right(points, scale):
    v = scaled(points, scale)
    high, mid, low = split(v)
    norms = norm_rows(half_norm(v), 3)
    return jnp.concatenate([high, mid, low, high, mid, high, norms, jnp.zeros_like(norms)], 0)


def scale_column(lengths):
    row = lax.broadcasted_iota(jnp.int32, (FEATS, LANES), 0)
    column = jnp.ones((FEATS, LANES), F32)
    for i in range(FEATS):
        column = jnp.where(row == i, lengths[i], column)
    return ROOT / column


def pack_kernel(*refs):
    sources, (out, scale_low, scale_high) = refs[:5], refs[5:8]
    held, (block, sems, out_sems) = refs[8:13], refs[13:]
    copies = [pltpu.make_async_copy(a, b, sems.at[i]) for i, (a, b) in enumerate(zip(sources, held))]
    for copy in copies:
        copy.start()
    for copy in copies:
        copy.wait()
    runs, weights, points, len_low, len_high = held
    last = jnp.broadcast_to(weights[:, :LANES], (8, LANES))
    row = lax.broadcasted_iota(jnp.int32, (8, LANES), 0)
    for q in range(RUN_BLOCKS):
        lanes = slice(q * LANES, (q + 1) * LANES)
        block[q * FEATS : (q + 1) * FEATS, :] = runs[:, lanes]
        if q:
            last = jnp.where(row == q, weights[:, lanes], last)
    block[RUN_BLOCKS * FEATS : PACKED - 8, :] = points[...]
    block[PACKED - 8 :, :] = last
    copies = [pltpu.make_async_copy(block, out.at[i], out_sems.at[i]) for i in range(out.shape[0])]
    for copy in copies:
        copy.start()
    scale_low[...] = scale_column(len_low)
    scale_high[...] = scale_column(len_high)
    for copy in copies:
        copy.wait()


def place_of(m, at):
    block = (m >> 3) * 8 + ((at[0] & 7) ^ (m >> 1 & 3) ^ 4 * (m & 1))
    return pl.ds(pl.multiple_of(block * LANES, LANES), LANES)


def prep_kernel(points, scale_low, scale_high, high, at, out, rows_out, high_out):
    high_out[...] = high[...]
    for m in range(points.shape[0]):
        place = place_of(m, at)
        out[place, :] = left(points[m], scale_low[...]).T.astype(BF16)
        rows_out[:, place] = left(points[m], scale_high[...]).astype(BF16)


def column_of(line, out, rows):
    out[rows, :] = jnp.broadcast_to(line, (LANES, LANES)).T


def weighted(cols, rows, column):
    term = jnp.exp2(jnp.dot(cols, rows, preferred_element_type=F32))
    count, wide = term.shape
    term = term * jnp.concatenate([column] * (wide // LANES), 1)
    return jnp.sum(term.reshape(count // 8, 8, wide), axis=0)


def mu_kernel(held, rows_in, scale, scale_high, high, rho, noise, at, out, cols_out, even, odd, total, lines):
    blocks = held.shape[0]

    def side(r):
        parts = [right(held[r, q * FEATS : (q + 1) * FEATS, :], scale[...]) for q in range(RUN_BLOCKS)]
        return jnp.concatenate([p.astype(BF16) for p in parts], 1)

    def work(r, runs):
        weights = held[r, PACKED - 8 :, :]
        for i in range(0, rows_in.shape[0], MU_CHUNK):
            rows = slice(i, i + MU_CHUNK)
            acc = total[rows, :]
            term = jnp.exp2(jnp.dot(rows_in[rows, :], runs[...], preferred_element_type=F32))
            for q in range(RUN_BLOCKS):
                acc = acc + term[:, q * LANES : (q + 1) * LANES] * weights[q : q + 1, :]
            total[rows, :] = acc

    total[...] = jnp.zeros_like(total)
    held_sides = (even, odd)
    even[...] = side(0)
    for r in range(blocks):
        if r + 1 < blocks:
            held_sides[(r + 1) % 2][...] = side(r + 1)
        work(r, held_sides[r % 2])
        cols = right(held[r, RUN_BLOCKS * FEATS : PACKED - 8, :], scale_high[...])
        cols_out[r * LANES : (r + 1) * LANES, :] = cols.T.astype(BF16)
    for k in range(lines.shape[0]):
        lines[k : k + 1, :] = jnp.sum(total[k * LANES : (k + 1) * LANES, :].T, axis=0, keepdims=True)
    mu = lines[...]
    row = lax.broadcasted_iota(jnp.int32, mu.shape, 0)
    target = -rho[0] * mu
    target = jnp.where(row == at[0], target + high[...], target)
    for i in range(out.shape[0]):
        out[i] = jnp.where(row == i, mu, target)


def lines_of(total):
    line = jnp.sum(total[...], axis=0, keepdims=True)
    return jnp.concatenate([line[:, k : k + LANES] for k in range(0, line.shape[1], LANES)], 0)


def first_kernel(held, rows_in, cols_in, high, rho, noise, at, out, target_out, mu_out, sums):
    total = jnp.sum(held[...], axis=0)
    row = lax.broadcasted_iota(jnp.int32, total.shape, 0)
    own = row == at[0]
    target = jnp.where(own, high[...] - rho[0] * total, total)
    target_out[...] = target
    mu_out[...] = jnp.sum(jnp.where(own, total, 0.0), axis=0, keepdims=True)
    own_target = jnp.sum(jnp.where(own, target, 0.0), axis=0, keepdims=True)
    size = 2 * LANES

    for k in range(0, cols_in.shape[0], size):
        cols = cols_in[k : k + size, :]
        acc = jnp.zeros((size, LANES), F32)
        for c in range(0, rows_in.shape[1], WIDE):
            term = jnp.exp2(jnp.dot(cols, rows_in[:, c : c + WIDE], preferred_element_type=F32))
            for q in range(0, WIDE, LANES):
                s = (c + q) // LANES
                acc = acc + term[:, q : q + LANES] * target_out[s : s + 1, :]
        for q in range(0, size, LANES):
            at_row = (k + q) // LANES
            sums[at_row : at_row + 1, :] = jnp.sum(acc[q : q + LANES, :].T, axis=0, keepdims=True)
    image = sums[...]
    image = jnp.where(lax.broadcasted_iota(jnp.int32, image.shape, 0) == at[1], image + noise[0] * own_target, image)
    for i in range(out.shape[0]):
        out[i] = image


def second_kernel(held, rows_in, cols_in, noise, at, out, column, total):
    image = jnp.sum(held[...], axis=0)
    mine = lax.broadcasted_iota(jnp.int32, image.shape, 0) == at[1]
    own = jnp.sum(jnp.where(mine, image, 0.0), axis=0, keepdims=True)
    for k in range(image.shape[0]):
        column_of(image[k : k + 1, :], column, slice(k * LANES, (k + 1) * LANES))
    total[...] = jnp.zeros_like(total)

    for i in range(0, cols_in.shape[0], CHUNK):
        rows = slice(i, i + CHUNK)
        for c in range(0, rows_in.shape[1], WIDE):
            total[:, c : c + WIDE] += weighted(cols_in[rows, :], rows_in[:, c : c + WIDE], column[rows, :])
    last = lines_of(total)
    row = lax.broadcasted_iota(jnp.int32, last.shape, 0)
    last = jnp.where(row == at[0], last + noise[0] * own, last)
    for i in range(out.shape[0]):
        for k in range(last.shape[0]):
            out[i, k] = last[k : k + 1, :]
        out[i, last.shape[0]] = own


def two_sum(a, b):
    s = a + b
    t = s - a
    return s, (a - (s - t)) + (b - t)


def pair_add(x, y):
    s, e = two_sum(x[0], y[0])
    return two_sum(s, e + (x[1] + y[1]))


def product(a, b):
    ah = a.astype(BF16).astype(F32)
    bh = b.astype(BF16).astype(F32)
    al, bl = a - ah, b - bh
    s, e = two_sum(ah * bh, ah * bl + al * bh)
    return two_sum(s, e + al * bl)


def pair_product(x, y):
    s, e = product(x[0], y[0])
    return two_sum(s, e + (x[0] * y[1] + x[1] * y[0]))


def minus(x):
    return -x[0], -x[1]


def pair_ratio(x, y):
    q = x[0] / y[0]
    rest = pair_add(x, minus(pair_product((q, jnp.zeros_like(q)), y)))
    return two_sum(q, (rest[0] + rest[1]) / y[0])


def fold_rows(x):
    high, low = x
    count = high.shape[0]
    while count > 8:
        count //= 2
        high, low = pair_add((high[:count], low[:count]), (high[count:], low[count:]))
    return high, low


def moments_kernel(held, target, at, out, own_out):
    count = target.shape[0]
    senders = range(held.shape[0])
    last = jnp.concatenate([sum(held[j, k] for j in senders) for k in range(count)], 0)
    image = jnp.concatenate([held[j, count] for j in senders], 0)
    b = target[...]
    for i, (p, q) in enumerate(((b, b), (b, image), (image, image), (image, last))):
        high, low = fold_rows(product(p, q))
        for shift in (4, 2, 1):
            high, low = pair_add((high, low), (pltpu.roll(high, shift, 0), pltpu.roll(low, shift, 0)))
        for j in range(out.shape[0]):
            out[j, i : i + 1, :] = high[:1]
            out[j, 4 + i : 5 + i, :] = low[:1]
    own = lax.broadcasted_iota(jnp.int32, b.shape, 0) == at[0]
    for i, v in enumerate((b, image, last)):
        own_out[i : i + 1, :] = jnp.sum(jnp.where(own, v, 0.0), axis=0, keepdims=True)


def final_kernel(held, own, x_out, r_out):
    pairs = [(held[j], pltpu.roll(held[j], 4, 0)) for j in range(held.shape[0])]
    while len(pairs) > 1:
        pairs = [pair_add(a, b) for a, b in zip(pairs[::2], pairs[1::2])]
    h, l = pairs[0]
    for shift in (64, 32, 16, 8, 4, 2, 1):
        h, l = pair_add((h, l), (pltpu.roll(h, shift, 1), pltpu.roll(l, shift, 1)))
    sums = [(h[i : i + 1], l[i : i + 1]) for i in range(4)]
    m0, m1, m2, m3 = sums
    alpha = pair_ratio(m0, m1)
    ratio = pair_ratio(m2, m1)
    v1 = pair_add(m2, minus(pair_product(m1, pair_ratio(m1, m0))))
    v2 = pair_add(m3, minus(pair_product(m2, ratio)))
    scale = pair_product(alpha, ratio)
    alpha0, grow = alpha[0], scale[0]
    alpha1 = (v1[0] + v1[1]) / (v2[0] + v2[1])
    b, image, last = own[0:1, :], own[1:2, :], own[2:3, :]
    x_out[...] = alpha0 * b + alpha1 * (grow * b - alpha0 * image)
    r_out[...] = (b - alpha0 * image) - alpha1 * (grow * image - alpha0 * last)


def exchange_z(blocks, step, size):
    return lax.ppermute(blocks, "z", [(i, i ^ step) for i in range(size)])


def exchange(blocks, axes):
    return lax.all_to_all(blocks, axes, 0, 0, tiled=True)


def local(runs, weights, points, high, len_low, len_high, rho, noise):
    n_row, n_col = lax.axis_size(ROWS), lax.axis_size(COLS)
    at = jnp.stack([lax.axis_index(ROWS), lax.axis_index(COLS)]).astype(jnp.int32)
    high = high.reshape(1, LANES)
    cols_len, rows_len = n_col * LANES, n_row * LANES
    size = lax.axis_size("z")
    to_col, scale_low, scale_high = pl.pallas_call(
        pack_kernel,
        out_shape=(shape((n_col, PACKED, LANES)), shape((FEATS, LANES)), shape((FEATS, LANES))),
        in_specs=[HBM] * 5,
        out_specs=(HBM, VMEM, VMEM),
        scratch_shapes=[
            pltpu.VMEM((FEATS, RUN_BLOCKS * LANES), F32),
            pltpu.VMEM((1, RUN_BLOCKS * LANES), F32),
            pltpu.VMEM((FEATS, LANES), F32),
            pltpu.SMEM((FEATS,), F32),
            pltpu.SMEM((FEATS,), F32),
            pltpu.VMEM((PACKED, LANES), F32),
            pltpu.SemaphoreType.DMA((5,)),
            pltpu.SemaphoreType.DMA((n_col,)),
        ],
        compiler_params=params(60),
        name="pack",
    )(runs, weights.reshape(1, RUN_BLOCKS * LANES), points, len_low, len_high)
    to_col, later_points = lax.optimization_barrier((to_col, points))
    far = exchange_z(later_points, 4, size)
    by_col = exchange(to_col, COLS)
    near = jnp.stack([points, far])
    by_row = jnp.concatenate([near] + [exchange_z(near, step, size) for step in (1, 2, 3)], 0)
    by_row = lax.all_gather(by_row, "core", axis=0, tiled=True)
    row_low, row_parts, high = pl.pallas_call(
        prep_kernel,
        out_shape=(shape((rows_len, DEPTH), BF16), shape((DEPTH, rows_len), BF16), shape((1, LANES))),
        in_specs=[VMEM] * 4 + [SMEM],
        out_specs=(VMEM,) * 3,
        compiler_params=params(4),
        name="prep",
    )(by_row, scale_low, scale_high, high, at)
    mu_terms, col_parts = pl.pallas_call(
        mu_kernel,
        out_shape=(shape((n_row, n_row, LANES)), shape((cols_len, DEPTH), BF16)),
        in_specs=[VMEM] * 5 + [SMEM] * 3,
        out_specs=(VMEM,) * 2,
        scratch_shapes=[
            pltpu.VMEM((DEPTH, RUN_BLOCKS * LANES), BF16),
            pltpu.VMEM((DEPTH, RUN_BLOCKS * LANES), BF16),
            pltpu.VMEM((rows_len, LANES), F32),
            pltpu.VMEM((n_row, LANES), F32),
        ],
        compiler_params=params(16),
        name="mu",
    )(by_col, row_low, scale_low, scale_high, high, rho, noise, at)
    mu_held = exchange(mu_terms, ROWS)
    image_terms, target, mu = pl.pallas_call(
        first_kernel,
        out_shape=(shape((n_col, n_col, LANES)), shape((n_row, LANES)), shape((1, LANES))),
        in_specs=[VMEM] * 4 + [SMEM] * 3,
        out_specs=(VMEM,) * 3,
        scratch_shapes=[pltpu.VMEM((n_col, LANES), F32)],
        compiler_params=params(4),
        name="first",
    )(mu_held, row_parts, col_parts, high, rho, noise, at)
    image_held = exchange(image_terms, COLS)
    last_terms = pl.pallas_call(
        second_kernel,
        out_shape=shape((n_row, n_row + 1, 1, LANES)),
        in_specs=[VMEM] * 3 + [SMEM] * 2,
        out_specs=VMEM,
        scratch_shapes=[pltpu.VMEM((cols_len, LANES), F32), pltpu.VMEM((8, rows_len), F32)],
        compiler_params=params(8),
        name="second",
    )(image_held, row_parts, col_parts, noise, at)
    last_held = exchange(last_terms, ROWS)
    moments, own = pl.pallas_call(
        moments_kernel,
        out_shape=(shape((n_col, 8, LANES)), shape((8, LANES))),
        in_specs=[VMEM] * 2 + [SMEM],
        out_specs=(VMEM,) * 2,
        compiler_params=params(4),
        name="moments",
    )(last_held, target, at)
    moments_held = exchange(moments, COLS)
    x, r = pl.pallas_call(
        final_kernel,
        out_shape=(shape((1, LANES)), shape((1, LANES))),
        in_specs=[VMEM] * 2,
        out_specs=(VMEM,) * 2,
        compiler_params=params(4),
        name="final",
    )(moments_held, own)
    return mu.reshape(LANES), x.reshape(LANES), r.reshape(LANES)


def solution(mesh):
    spread = P(AXES)
    wide = P(None, AXES)
    fine = Mesh(mesh.devices.reshape(4, 2, 4, 8), AXES)
    return jax.shard_map(
        local,
        mesh=fine,
        in_specs=(wide, spread, wide, spread, P(), P(), P(), P()),
        out_specs=(spread,) * 3,
        check_vma=False,
    )
```

```python
import math

import jax
import jax.numpy as jnp
from jax import lax
from jax.experimental import pallas as pl
from jax.experimental.pallas import tpu as pltpu
from jax.sharding import Mesh
from jax.sharding import PartitionSpec as P

F32 = jnp.float32
BF16 = jnp.bfloat16
FEATS = 24
LANES = 128
RUN_BLOCKS = 4
WIDE = CHUNK = 512
MU_CHUNK = 256
PACKED = RUN_BLOCKS * FEATS + FEATS + 8
DEPTH = 160
ROOT = math.sqrt(math.log2(math.e))
VMEM = pl.BlockSpec(memory_space=pltpu.VMEM)
AXES = ("y", "core", "x", "z")
ROWS = ("core", "z")
COLS = ("y", "x")
HBM = pl.BlockSpec(memory_space=pltpu.HBM)
SMEM = pl.BlockSpec(memory_space=pltpu.SMEM)


def params(mib):
    return pltpu.CompilerParams(vmem_limit_bytes=mib * 1024 * 1024)


def shape(dims, kind=F32):
    return jax.ShapeDtypeStruct(dims, kind)


def split(x):
    high = x.astype(BF16).astype(F32)
    rest = x - high
    mid = rest.astype(BF16).astype(F32)
    return high, mid, rest - mid


def norm_rows(norm, at):
    high, mid, low = split(norm)
    row = lax.broadcasted_iota(jnp.int32, (8, norm.shape[1]), 0)
    ones = jnp.where((row >= 3 - at) & (row < 6 - at), 1.0, 0.0)
    return jnp.where(row == at, high, jnp.where(row == at + 1, mid, jnp.where(row == at + 2, low, ones)))


def scaled(points, scale):
    return (points - 0.5) * scale


def half_norm(points):
    return -0.5 * jnp.sum(points * points, axis=0, keepdims=True)


def left(points, scale):
    u = scaled(points, scale)
    high, mid, low = split(u)
    norms = norm_rows(half_norm(u), 0)
    return jnp.concatenate([high, high, high, mid, mid, low, norms, jnp.zeros_like(norms)], 0)


def right(points, scale):
    v = scaled(points, scale)
    high, mid, low = split(v)
    norms = norm_rows(half_norm(v), 3)
    return jnp.concatenate([high, mid, low, high, mid, high, norms, jnp.zeros_like(norms)], 0)


def scale_column(lengths):
    row = lax.broadcasted_iota(jnp.int32, (FEATS, LANES), 0)
    column = jnp.ones((FEATS, LANES), F32)
    for i in range(FEATS):
        column = jnp.where(row == i, lengths[i], column)
    return ROOT / column


def pack_kernel(*refs):
    sources, (out, scale_low, scale_high) = refs[:5], refs[5:8]
    held, (block, sems, out_sems) = refs[8:13], refs[13:]
    copies = [pltpu.make_async_copy(a, b, sems.at[i]) for i, (a, b) in enumerate(zip(sources, held))]
    for copy in copies:
        copy.start()
    for copy in copies:
        copy.wait()
    runs, weights, points, len_low, len_high = held
    last = jnp.broadcast_to(weights[:, :LANES], (8, LANES))
    row = lax.broadcasted_iota(jnp.int32, (8, LANES), 0)
    for q in range(RUN_BLOCKS):
        lanes = slice(q * LANES, (q + 1) * LANES)
        block[q * FEATS : (q + 1) * FEATS, :] = runs[:, lanes]
        if q:
            last = jnp.where(row == q, weights[:, lanes], last)
    block[RUN_BLOCKS * FEATS : PACKED - 8, :] = points[...]
    block[PACKED - 8 :, :] = last
    copies = [pltpu.make_async_copy(block, out.at[i], out_sems.at[i]) for i in range(out.shape[0])]
    for copy in copies:
        copy.start()
    scale_low[...] = scale_column(len_low)
    scale_high[...] = scale_column(len_high)
    for copy in copies:
        copy.wait()


def place_of(m, at):
    block = (m >> 3) * 8 + ((at[0] & 7) ^ (m & 7))
    return pl.ds(pl.multiple_of(block * LANES, LANES), LANES)


def prep_kernel(points, scale_low, scale_high, at, out, rows_out):
    for m in range(points.shape[0]):
        place = place_of(m, at)
        out[place, :] = left(points[m], scale_low[...]).T.astype(BF16)
        rows_out[:, place] = left(points[m], scale_high[...]).astype(BF16)


def column_of(line, out, rows):
    out[rows, :] = jnp.broadcast_to(line, (LANES, LANES)).T


def weighted(cols, rows, column):
    term = jnp.exp2(jnp.dot(cols, rows, preferred_element_type=F32))
    count, wide = term.shape
    term = term * jnp.concatenate([column] * (wide // LANES), 1)
    return jnp.sum(term.reshape(count // 8, 8, wide), axis=0)


def mu_kernel(held, rows_in, scale, scale_high, high, rho, noise, at, out, cols_out, even, odd, total, lines):
    blocks = held.shape[0]

    def side(r):
        parts = [right(held[r, q * FEATS : (q + 1) * FEATS, :], scale[...]) for q in range(RUN_BLOCKS)]
        return jnp.concatenate([p.astype(BF16) for p in parts], 1)

    def work(r, runs):
        weights = held[r, PACKED - 8 :, :]
        for i in range(0, rows_in.shape[0], MU_CHUNK):
            rows = slice(i, i + MU_CHUNK)
            acc = total[rows, :]
            term = jnp.exp2(jnp.dot(rows_in[rows, :], runs[...], preferred_element_type=F32))
            for q in range(RUN_BLOCKS):
                acc = acc + term[:, q * LANES : (q + 1) * LANES] * weights[q : q + 1, :]
            total[rows, :] = acc

    total[...] = jnp.zeros_like(total)
    held_sides = (even, odd)
    even[...] = side(0)
    for r in range(blocks):
        if r + 1 < blocks:
            held_sides[(r + 1) % 2][...] = side(r + 1)
        work(r, held_sides[r % 2])
        cols = right(held[r, RUN_BLOCKS * FEATS : PACKED - 8, :], scale_high[...])
        cols_out[r * LANES : (r + 1) * LANES, :] = cols.T.astype(BF16)
    for k in range(lines.shape[0]):
        lines[k : k + 1, :] = jnp.sum(total[k * LANES : (k + 1) * LANES, :].T, axis=0, keepdims=True)
    mu = lines[...]
    row = lax.broadcasted_iota(jnp.int32, mu.shape, 0)
    target = -rho[0] * mu
    target = jnp.where(row == at[0], target + high[...], target)
    for i in range(out.shape[0]):
        out[i] = jnp.where(row == i, mu, target)


def lines_of(total):
    line = jnp.sum(total[...], axis=0, keepdims=True)
    return jnp.concatenate([line[:, k : k + LANES] for k in range(0, line.shape[1], LANES)], 0)


def first_kernel(held, rows_in, cols_in, high, rho, noise, at, out, target_out, mu_out, sums):
    total = jnp.sum(held[...], axis=0)
    row = lax.broadcasted_iota(jnp.int32, total.shape, 0)
    own = row == at[0]
    target = jnp.where(own, high[...] - rho[0] * total, total)
    target_out[...] = target
    mu_out[...] = jnp.sum(jnp.where(own, total, 0.0), axis=0, keepdims=True)
    own_target = jnp.sum(jnp.where(own, target, 0.0), axis=0, keepdims=True)
    size = 2 * LANES

    for k in range(0, cols_in.shape[0], size):
        cols = cols_in[k : k + size, :]
        acc = jnp.zeros((size, LANES), F32)
        for c in range(0, rows_in.shape[1], WIDE):
            term = jnp.exp2(jnp.dot(cols, rows_in[:, c : c + WIDE], preferred_element_type=F32))
            for q in range(0, WIDE, LANES):
                s = (c + q) // LANES
                acc = acc + term[:, q : q + LANES] * target_out[s : s + 1, :]
        for q in range(0, size, LANES):
            at_row = (k + q) // LANES
            sums[at_row : at_row + 1, :] = jnp.sum(acc[q : q + LANES, :].T, axis=0, keepdims=True)
    image = sums[...]
    image = jnp.where(lax.broadcasted_iota(jnp.int32, image.shape, 0) == at[1], image + noise[0] * own_target, image)
    for i in range(out.shape[0]):
        out[i] = image


def second_kernel(held, rows_in, cols_in, noise, at, out, column, total):
    image = jnp.sum(held[...], axis=0)
    mine = lax.broadcasted_iota(jnp.int32, image.shape, 0) == at[1]
    own = jnp.sum(jnp.where(mine, image, 0.0), axis=0, keepdims=True)
    for k in range(image.shape[0]):
        column_of(image[k : k + 1, :], column, slice(k * LANES, (k + 1) * LANES))
    total[...] = jnp.zeros_like(total)

    for i in range(0, cols_in.shape[0], CHUNK):
        rows = slice(i, i + CHUNK)
        for c in range(0, rows_in.shape[1], WIDE):
            total[:, c : c + WIDE] += weighted(cols_in[rows, :], rows_in[:, c : c + WIDE], column[rows, :])
    last = lines_of(total)
    row = lax.broadcasted_iota(jnp.int32, last.shape, 0)
    last = jnp.where(row == at[0], last + noise[0] * own, last)
    for i in range(out.shape[0]):
        for k in range(last.shape[0]):
            out[i, k] = last[k : k + 1, :]
        out[i, last.shape[0]] = own


def two_sum(a, b):
    s = a + b
    t = s - a
    return s, (a - (s - t)) + (b - t)


def pair_add(x, y):
    s, e = two_sum(x[0], y[0])
    return two_sum(s, e + (x[1] + y[1]))


def product(a, b):
    ah = a.astype(BF16).astype(F32)
    bh = b.astype(BF16).astype(F32)
    al, bl = a - ah, b - bh
    s, e = two_sum(ah * bh, ah * bl + al * bh)
    return two_sum(s, e + al * bl)


def pair_product(x, y):
    s, e = product(x[0], y[0])
    return two_sum(s, e + (x[0] * y[1] + x[1] * y[0]))


def minus(x):
    return -x[0], -x[1]


def pair_ratio(x, y):
    q = x[0] / y[0]
    rest = pair_add(x, minus(pair_product((q, jnp.zeros_like(q)), y)))
    return two_sum(q, (rest[0] + rest[1]) / y[0])


def fold_rows(x):
    high, low = x
    count = high.shape[0]
    while count > 8:
        count //= 2
        high, low = pair_add((high[:count], low[:count]), (high[count:], low[count:]))
    return high, low


def moments_kernel(held, target, at, out, own_out):
    count = target.shape[0]
    senders = range(held.shape[0])
    last = jnp.concatenate([sum(held[j, k] for j in senders) for k in range(count)], 0)
    image = jnp.concatenate([held[j, count] for j in senders], 0)
    b = target[...]
    for i, (p, q) in enumerate(((b, b), (b, image), (image, image), (image, last))):
        high, low = fold_rows(product(p, q))
        for shift in (4, 2, 1):
            high, low = pair_add((high, low), (pltpu.roll(high, shift, 0), pltpu.roll(low, shift, 0)))
        for j in range(out.shape[0]):
            out[j, i : i + 1, :] = high[:1]
            out[j, 4 + i : 5 + i, :] = low[:1]
    own = lax.broadcasted_iota(jnp.int32, b.shape, 0) == at[0]
    for i, v in enumerate((b, image, last)):
        own_out[i : i + 1, :] = jnp.sum(jnp.where(own, v, 0.0), axis=0, keepdims=True)


def final_kernel(held, own, x_out, r_out):
    pairs = [(held[j], pltpu.roll(held[j], 4, 0)) for j in range(held.shape[0])]
    while len(pairs) > 1:
        pairs = [pair_add(a, b) for a, b in zip(pairs[::2], pairs[1::2])]
    h, l = pairs[0]
    for shift in (64, 32, 16, 8, 4, 2, 1):
        h, l = pair_add((h, l), (pltpu.roll(h, shift, 1), pltpu.roll(l, shift, 1)))
    sums = [(h[i : i + 1], l[i : i + 1]) for i in range(4)]
    m0, m1, m2, m3 = sums
    alpha = pair_ratio(m0, m1)
    ratio = pair_ratio(m2, m1)
    v1 = pair_add(m2, minus(pair_product(m1, pair_ratio(m1, m0))))
    v2 = pair_add(m3, minus(pair_product(m2, ratio)))
    scale = pair_product(alpha, ratio)
    alpha0, grow = alpha[0], scale[0]
    alpha1 = (v1[0] + v1[1]) / (v2[0] + v2[1])
    b, image, last = own[0:1, :], own[1:2, :], own[2:3, :]
    x_out[...] = alpha0 * b + alpha1 * (grow * b - alpha0 * image)
    r_out[...] = (b - alpha0 * image) - alpha1 * (grow * image - alpha0 * last)


def exchange_z(blocks, step, size):
    return lax.ppermute(blocks, "z", [(i, i ^ step) for i in range(size)])


def exchange(blocks, axes):
    return lax.all_to_all(blocks, axes, 0, 0, tiled=True)


def local(runs, weights, points, high, len_low, len_high, rho, noise):
    n_row, n_col = lax.axis_size(ROWS), lax.axis_size(COLS)
    at = jnp.stack([lax.axis_index(ROWS), lax.axis_index(COLS)]).astype(jnp.int32)
    high = jnp.where(at[1] >= 0, high, 0.0).reshape(1, LANES)
    cols_len, rows_len = n_col * LANES, n_row * LANES
    size = lax.axis_size("z")
    to_col, scale_low, scale_high = pl.pallas_call(
        pack_kernel,
        out_shape=(shape((n_col, PACKED, LANES)), shape((FEATS, LANES)), shape((FEATS, LANES))),
        in_specs=[HBM] * 5,
        out_specs=(HBM, VMEM, VMEM),
        scratch_shapes=[
            pltpu.VMEM((FEATS, RUN_BLOCKS * LANES), F32),
            pltpu.VMEM((1, RUN_BLOCKS * LANES), F32),
            pltpu.VMEM((FEATS, LANES), F32),
            pltpu.SMEM((FEATS,), F32),
            pltpu.SMEM((FEATS,), F32),
            pltpu.VMEM((PACKED, LANES), F32),
            pltpu.SemaphoreType.DMA((5,)),
            pltpu.SemaphoreType.DMA((n_col,)),
        ],
        compiler_params=params(60),
        name="pack",
    )(runs, weights.reshape(1, RUN_BLOCKS * LANES), points, len_low, len_high)
    far = exchange_z(points, 1, size)
    by_col = exchange(to_col, COLS)
    near = jnp.stack([points, far])
    by_row = jnp.concatenate([near] + [exchange_z(near, step, size) for step in (2, 4, 6)], 0)
    by_row = lax.all_gather(by_row, "core", axis=0, tiled=True)
    row_low, row_parts = pl.pallas_call(
        prep_kernel,
        out_shape=(shape((rows_len, DEPTH), BF16), shape((DEPTH, rows_len), BF16)),
        in_specs=[VMEM] * 3 + [SMEM],
        out_specs=(VMEM,) * 2,
        compiler_params=params(4),
        name="prep",
    )(by_row, scale_low, scale_high, at)
    mu_terms, col_parts = pl.pallas_call(
        mu_kernel,
        out_shape=(shape((n_row, n_row, LANES)), shape((cols_len, DEPTH), BF16)),
        in_specs=[VMEM] * 5 + [SMEM] * 3,
        out_specs=(VMEM,) * 2,
        scratch_shapes=[
            pltpu.VMEM((DEPTH, RUN_BLOCKS * LANES), BF16),
            pltpu.VMEM((DEPTH, RUN_BLOCKS * LANES), BF16),
            pltpu.VMEM((rows_len, LANES), F32),
            pltpu.VMEM((n_row, LANES), F32),
        ],
        compiler_params=params(16),
        name="mu",
    )(by_col, row_low, scale_low, scale_high, high, rho, noise, at)
    mu_held = exchange(mu_terms, ROWS)
    image_terms, target, mu = pl.pallas_call(
        first_kernel,
        out_shape=(shape((n_col, n_col, LANES)), shape((n_row, LANES)), shape((1, LANES))),
        in_specs=[VMEM] * 4 + [SMEM] * 3,
        out_specs=(VMEM,) * 3,
        scratch_shapes=[pltpu.VMEM((n_col, LANES), F32)],
        compiler_params=params(4),
        name="first",
    )(mu_held, row_parts, col_parts, high, rho, noise, at)
    image_held = exchange(image_terms, COLS)
    last_terms = pl.pallas_call(
        second_kernel,
        out_shape=shape((n_row, n_row + 1, 1, LANES)),
        in_specs=[VMEM] * 3 + [SMEM] * 2,
        out_specs=VMEM,
        scratch_shapes=[pltpu.VMEM((cols_len, LANES), F32), pltpu.VMEM((8, rows_len), F32)],
        compiler_params=params(8),
        name="second",
    )(image_held, row_parts, col_parts, noise, at)
    last_held = exchange(last_terms, ROWS)
    moments, own = pl.pallas_call(
        moments_kernel,
        out_shape=(shape((n_col, 8, LANES)), shape((8, LANES))),
        in_specs=[VMEM] * 2 + [SMEM],
        out_specs=(VMEM,) * 2,
        compiler_params=params(4),
        name="moments",
    )(last_held, target, at)
    moments_held = exchange(moments, COLS)
    x, r = pl.pallas_call(
        final_kernel,
        out_shape=(shape((1, LANES)), shape((1, LANES))),
        in_specs=[VMEM] * 2,
        out_specs=(VMEM,) * 2,
        compiler_params=params(4),
        name="final",
    )(moments_held, own)
    return mu.reshape(LANES), x.reshape(LANES), r.reshape(LANES)


def solution(mesh):
    spread = P(AXES)
    wide = P(None, AXES)
    fine = Mesh(mesh.devices.reshape(4, 2, 4, 8), AXES)
    return jax.shard_map(
        local,
        mesh=fine,
        in_specs=(wide, spread, wide, spread, P(), P(), P(), P()),
        out_specs=(spread,) * 3,
        check_vma=False,
    )
```

```python
import math

import jax
import jax.numpy as jnp
from jax import lax
from jax.experimental import pallas as pl
from jax.experimental.pallas import tpu as pltpu
from jax.sharding import Mesh
from jax.sharding import PartitionSpec as P

F32 = jnp.float32
BF16 = jnp.bfloat16
FEATS = 24
LANES = 128
RUN_BLOCKS = 4
WIDE = CHUNK = 512
MU_CHUNK = 256
PACKED = RUN_BLOCKS * FEATS + FEATS + 8
DEPTH = 160
ROOT = math.sqrt(math.log2(math.e))
VMEM = pl.BlockSpec(memory_space=pltpu.VMEM)
AXES = ("y", "core", "x", "z")
ROWS = ("core", "z")
COLS = ("y", "x")
HBM = pl.BlockSpec(memory_space=pltpu.HBM)
SMEM = pl.BlockSpec(memory_space=pltpu.SMEM)


def params(mib):
    return pltpu.CompilerParams(vmem_limit_bytes=mib * 1024 * 1024)


def shape(dims, kind=F32):
    return jax.ShapeDtypeStruct(dims, kind)


def split(x):
    high = x.astype(BF16).astype(F32)
    rest = x - high
    mid = rest.astype(BF16).astype(F32)
    return high, mid, rest - mid


def norm_rows(norm, at):
    high, mid, low = split(norm)
    row = lax.broadcasted_iota(jnp.int32, (8, norm.shape[1]), 0)
    ones = jnp.where((row >= 3 - at) & (row < 6 - at), 1.0, 0.0)
    return jnp.where(row == at, high, jnp.where(row == at + 1, mid, jnp.where(row == at + 2, low, ones)))


def scaled(points, scale):
    return (points - 0.5) * scale


def half_norm(points):
    return -0.5 * jnp.sum(points * points, axis=0, keepdims=True)


def left(points, scale):
    u = scaled(points, scale)
    high, mid, low = split(u)
    norms = norm_rows(half_norm(u), 0)
    return jnp.concatenate([high, high, high, mid, mid, low, norms, jnp.zeros_like(norms)], 0)


def right(points, scale):
    v = scaled(points, scale)
    high, mid, low = split(v)
    norms = norm_rows(half_norm(v), 3)
    return jnp.concatenate([high, mid, low, high, mid, high, norms, jnp.zeros_like(norms)], 0)


def scale_column(lengths):
    row = lax.broadcasted_iota(jnp.int32, (FEATS, LANES), 0)
    column = jnp.ones((FEATS, LANES), F32)
    for i in range(FEATS):
        column = jnp.where(row == i, lengths[i], column)
    return ROOT / column


def pack_kernel(*refs):
    sources, (out, scale_low, scale_high) = refs[:5], refs[5:8]
    held, (block, sems, out_sems) = refs[8:13], refs[13:]
    copies = [pltpu.make_async_copy(a, b, sems.at[i]) for i, (a, b) in enumerate(zip(sources, held))]
    for copy in copies:
        copy.start()
    for copy in copies:
        copy.wait()
    runs, weights, points, len_low, len_high = held
    last = jnp.broadcast_to(weights[:, :LANES], (8, LANES))
    row = lax.broadcasted_iota(jnp.int32, (8, LANES), 0)
    for q in range(RUN_BLOCKS):
        lanes = slice(q * LANES, (q + 1) * LANES)
        block[q * FEATS : (q + 1) * FEATS, :] = runs[:, lanes]
        if q:
            last = jnp.where(row == q, weights[:, lanes], last)
    block[RUN_BLOCKS * FEATS : PACKED - 8, :] = points[...]
    block[PACKED - 8 :, :] = last
    copies = [pltpu.make_async_copy(block, out.at[i], out_sems.at[i]) for i in range(out.shape[0])]
    for copy in copies:
        copy.start()
    scale_low[...] = scale_column(len_low)
    scale_high[...] = scale_column(len_high)
    for copy in copies:
        copy.wait()


def place_of(m, at):
    block = (m >> 3) * 8 + ((at[0] & 7) ^ (m >> 1 & 3) ^ 4 * (m & 1))
    return pl.ds(pl.multiple_of(block * LANES, LANES), LANES)


def prep_kernel(points, scale_low, scale_high, at, out, rows_out):
    for m in range(points.shape[0]):
        place = place_of(m, at)
        out[place, :] = left(points[m], scale_low[...]).T.astype(BF16)
        rows_out[:, place] = left(points[m], scale_high[...]).astype(BF16)


def column_of(line, out, rows):
    out[rows, :] = jnp.broadcast_to(line, (LANES, LANES)).T


def weighted(cols, rows, column):
    term = jnp.exp2(jnp.dot(cols, rows, preferred_element_type=F32))
    count, wide = term.shape
    term = term * jnp.concatenate([column] * (wide // LANES), 1)
    return jnp.sum(term.reshape(count // 8, 8, wide), axis=0)


def mu_kernel(held, rows_in, scale, scale_high, high, rho, noise, at, out, cols_out, even, odd, total, lines):
    blocks = held.shape[0]

    def side(r):
        parts = [right(held[r, q * FEATS : (q + 1) * FEATS, :], scale[...]) for q in range(RUN_BLOCKS)]
        return jnp.concatenate([p.astype(BF16) for p in parts], 1)

    def work(r, runs):
        weights = held[r, PACKED - 8 :, :]
        for i in range(0, rows_in.shape[0], MU_CHUNK):
            rows = slice(i, i + MU_CHUNK)
            acc = total[rows, :]
            term = jnp.exp2(jnp.dot(rows_in[rows, :], runs[...], preferred_element_type=F32))
            for q in range(RUN_BLOCKS):
                acc = acc + term[:, q * LANES : (q + 1) * LANES] * weights[q : q + 1, :]
            total[rows, :] = acc

    total[...] = jnp.zeros_like(total)
    held_sides = (even, odd)
    even[...] = side(0)
    for r in range(blocks):
        if r + 1 < blocks:
            held_sides[(r + 1) % 2][...] = side(r + 1)
        work(r, held_sides[r % 2])
        cols = right(held[r, RUN_BLOCKS * FEATS : PACKED - 8, :], scale_high[...])
        cols_out[r * LANES : (r + 1) * LANES, :] = cols.T.astype(BF16)
    for k in range(lines.shape[0]):
        lines[k : k + 1, :] = jnp.sum(total[k * LANES : (k + 1) * LANES, :].T, axis=0, keepdims=True)
    mu = lines[...]
    row = lax.broadcasted_iota(jnp.int32, mu.shape, 0)
    target = -rho[0] * mu
    target = jnp.where(row == at[0], target + high[...], target)
    for i in range(out.shape[0]):
        out[i] = jnp.where(row == i, mu, target)


def lines_of(total):
    line = jnp.sum(total[...], axis=0, keepdims=True)
    return jnp.concatenate([line[:, k : k + LANES] for k in range(0, line.shape[1], LANES)], 0)


def first_kernel(held, rows_in, cols_in, high, rho, noise, at, at_col, out, target_out, mu_out, sums):
    total = jnp.sum(held[...], axis=0)
    row = lax.broadcasted_iota(jnp.int32, total.shape, 0)
    own = row == at[0]
    target = jnp.where(own, high[...] - rho[0] * total, total)
    target_out[...] = target
    mu_out[...] = jnp.sum(jnp.where(own, total, 0.0), axis=0, keepdims=True)
    own_target = jnp.sum(jnp.where(own, target, 0.0), axis=0, keepdims=True)
    size = 2 * LANES

    for k in range(0, cols_in.shape[0], size):
        cols = cols_in[k : k + size, :]
        acc = jnp.zeros((size, LANES), F32)
        for c in range(0, rows_in.shape[1], WIDE):
            term = jnp.exp2(jnp.dot(cols, rows_in[:, c : c + WIDE], preferred_element_type=F32))
            for q in range(0, WIDE, LANES):
                s = (c + q) // LANES
                acc = acc + term[:, q : q + LANES] * target_out[s : s + 1, :]
        for q in range(0, size, LANES):
            at_row = (k + q) // LANES
            sums[at_row : at_row + 1, :] = jnp.sum(acc[q : q + LANES, :].T, axis=0, keepdims=True)
    image = sums[...]
    image = jnp.where(lax.broadcasted_iota(jnp.int32, image.shape, 0) == at_col[0], image + noise[0] * own_target, image)
    for i in range(out.shape[0]):
        out[i] = image


def second_kernel(held, rows_in, cols_in, noise, at, at_col, out, column, total):
    image = jnp.sum(held[...], axis=0)
    mine = lax.broadcasted_iota(jnp.int32, image.shape, 0) == at_col[0]
    own = jnp.sum(jnp.where(mine, image, 0.0), axis=0, keepdims=True)
    for k in range(image.shape[0]):
        column_of(image[k : k + 1, :], column, slice(k * LANES, (k + 1) * LANES))
    total[...] = jnp.zeros_like(total)

    for i in range(0, cols_in.shape[0], CHUNK):
        rows = slice(i, i + CHUNK)
        for c in range(0, rows_in.shape[1], WIDE):
            total[:, c : c + WIDE] += weighted(cols_in[rows, :], rows_in[:, c : c + WIDE], column[rows, :])
    last = lines_of(total)
    row = lax.broadcasted_iota(jnp.int32, last.shape, 0)
    last = jnp.where(row == at[0], last + noise[0] * own, last)
    for i in range(out.shape[0]):
        for k in range(last.shape[0]):
            out[i, k] = last[k : k + 1, :]
        out[i, last.shape[0]] = own


def two_sum(a, b):
    s = a + b
    t = s - a
    return s, (a - (s - t)) + (b - t)


def pair_add(x, y):
    s, e = two_sum(x[0], y[0])
    return two_sum(s, e + (x[1] + y[1]))


def product(a, b):
    ah = a.astype(BF16).astype(F32)
    bh = b.astype(BF16).astype(F32)
    al, bl = a - ah, b - bh
    s, e = two_sum(ah * bh, ah * bl + al * bh)
    return two_sum(s, e + al * bl)


def pair_product(x, y):
    s, e = product(x[0], y[0])
    return two_sum(s, e + (x[0] * y[1] + x[1] * y[0]))


def minus(x):
    return -x[0], -x[1]


def pair_ratio(x, y):
    q = x[0] / y[0]
    rest = pair_add(x, minus(pair_product((q, jnp.zeros_like(q)), y)))
    return two_sum(q, (rest[0] + rest[1]) / y[0])


def fold_rows(x):
    high, low = x
    count = high.shape[0]
    while count > 8:
        count //= 2
        high, low = pair_add((high[:count], low[:count]), (high[count:], low[count:]))
    return high, low


def moments_kernel(held, target, at, out, own_out):
    count = target.shape[0]
    senders = range(held.shape[0])
    last = jnp.concatenate([sum(held[j, k] for j in senders) for k in range(count)], 0)
    image = jnp.concatenate([held[j, count] for j in senders], 0)
    b = target[...]
    for i, (p, q) in enumerate(((b, b), (b, image), (image, image), (image, last))):
        high, low = fold_rows(product(p, q))
        for shift in (4, 2, 1):
            high, low = pair_add((high, low), (pltpu.roll(high, shift, 0), pltpu.roll(low, shift, 0)))
        for j in range(out.shape[0]):
            out[j, i : i + 1, :] = high[:1]
            out[j, 4 + i : 5 + i, :] = low[:1]
    own = lax.broadcasted_iota(jnp.int32, b.shape, 0) == at[0]
    for i, v in enumerate((b, image, last)):
        own_out[i : i + 1, :] = jnp.sum(jnp.where(own, v, 0.0), axis=0, keepdims=True)


def final_kernel(held, own, x_out, r_out):
    pairs = [(held[j], pltpu.roll(held[j], 4, 0)) for j in range(held.shape[0])]
    while len(pairs) > 1:
        pairs = [pair_add(a, b) for a, b in zip(pairs[::2], pairs[1::2])]
    h, l = pairs[0]
    for shift in (64, 32, 16, 8, 4, 2, 1):
        h, l = pair_add((h, l), (pltpu.roll(h, shift, 1), pltpu.roll(l, shift, 1)))
    sums = [(h[i : i + 1], l[i : i + 1]) for i in range(4)]
    m0, m1, m2, m3 = sums
    alpha = pair_ratio(m0, m1)
    ratio = pair_ratio(m2, m1)
    v1 = pair_add(m2, minus(pair_product(m1, pair_ratio(m1, m0))))
    v2 = pair_add(m3, minus(pair_product(m2, ratio)))
    scale = pair_product(alpha, ratio)
    alpha0, grow = alpha[0], scale[0]
    alpha1 = (v1[0] + v1[1]) / (v2[0] + v2[1])
    b, image, last = own[0:1, :], own[1:2, :], own[2:3, :]
    x_out[...] = alpha0 * b + alpha1 * (grow * b - alpha0 * image)
    r_out[...] = (b - alpha0 * image) - alpha1 * (grow * image - alpha0 * last)


def exchange_z(blocks, step, size):
    return lax.ppermute(blocks, "z", [(i, i ^ step) for i in range(size)])


def exchange(blocks, axes):
    return lax.all_to_all(blocks, axes, 0, 0, tiled=True)


def local(runs, weights, points, high, len_low, len_high, rho, noise):
    n_row, n_col = lax.axis_size(ROWS), lax.axis_size(COLS)
    place = lax.axis_index(COLS)
    at, at_col = lax.axis_index(ROWS).reshape(1), place.reshape(1)
    high = jnp.where(place >= 0, high, 0.0).reshape(1, LANES)
    cols_len, rows_len = n_col * LANES, n_row * LANES
    size = lax.axis_size("z")
    to_col, scale_low, scale_high = pl.pallas_call(
        pack_kernel,
        out_shape=(shape((n_col, PACKED, LANES)), shape((FEATS, LANES)), shape((FEATS, LANES))),
        in_specs=[HBM] * 5,
        out_specs=(HBM, VMEM, VMEM),
        scratch_shapes=[
            pltpu.VMEM((FEATS, RUN_BLOCKS * LANES), F32),
            pltpu.VMEM((1, RUN_BLOCKS * LANES), F32),
            pltpu.VMEM((FEATS, LANES), F32),
            pltpu.SMEM((FEATS,), F32),
            pltpu.SMEM((FEATS,), F32),
            pltpu.VMEM((PACKED, LANES), F32),
            pltpu.SemaphoreType.DMA((5,)),
            pltpu.SemaphoreType.DMA((n_col,)),
        ],
        compiler_params=params(60),
        name="pack",
    )(runs, weights.reshape(1, RUN_BLOCKS * LANES), points, len_low, len_high)
    far = exchange_z(points, 4, size)
    by_col = exchange(to_col, COLS)
    near = jnp.stack([points, far])
    by_row = jnp.concatenate([near] + [exchange_z(near, step, size) for step in (1, 2, 3)], 0)
    by_row = lax.all_gather(by_row, "core", axis=0, tiled=True)
    row_low, row_parts = pl.pallas_call(
        prep_kernel,
        out_shape=(shape((rows_len, DEPTH), BF16), shape((DEPTH, rows_len), BF16)),
        in_specs=[VMEM] * 3 + [SMEM],
        out_specs=(VMEM,) * 2,
        compiler_params=params(4),
        name="prep",
    )(by_row, scale_low, scale_high, at)
    mu_terms, col_parts = pl.pallas_call(
        mu_kernel,
        out_shape=(shape((n_row, n_row, LANES)), shape((cols_len, DEPTH), BF16)),
        in_specs=[VMEM] * 5 + [SMEM] * 3,
        out_specs=(VMEM,) * 2,
        scratch_shapes=[
            pltpu.VMEM((DEPTH, RUN_BLOCKS * LANES), BF16),
            pltpu.VMEM((DEPTH, RUN_BLOCKS * LANES), BF16),
            pltpu.VMEM((rows_len, LANES), F32),
            pltpu.VMEM((n_row, LANES), F32),
        ],
        compiler_params=params(16),
        name="mu",
    )(by_col, row_low, scale_low, scale_high, high, rho, noise, at)
    mu_held = exchange(mu_terms, ROWS)
    image_terms, target, mu = pl.pallas_call(
        first_kernel,
        out_shape=(shape((n_col, n_col, LANES)), shape((n_row, LANES)), shape((1, LANES))),
        in_specs=[VMEM] * 4 + [SMEM] * 4,
        out_specs=(VMEM,) * 3,
        scratch_shapes=[pltpu.VMEM((n_col, LANES), F32)],
        compiler_params=params(4),
        name="first",
    )(mu_held, row_parts, col_parts, high, rho, noise, at, at_col)
    image_held = exchange(image_terms, COLS)
    last_terms = pl.pallas_call(
        second_kernel,
        out_shape=shape((n_row, n_row + 1, 1, LANES)),
        in_specs=[VMEM] * 3 + [SMEM] * 3,
        out_specs=VMEM,
        scratch_shapes=[pltpu.VMEM((cols_len, LANES), F32), pltpu.VMEM((8, rows_len), F32)],
        compiler_params=params(8),
        name="second",
    )(image_held, row_parts, col_parts, noise, at, at_col)
    last_held = exchange(last_terms, ROWS)
    moments, own = pl.pallas_call(
        moments_kernel,
        out_shape=(shape((n_col, 8, LANES)), shape((8, LANES))),
        in_specs=[VMEM] * 2 + [SMEM],
        out_specs=(VMEM,) * 2,
        compiler_params=params(4),
        name="moments",
    )(last_held, target, at)
    moments_held = exchange(moments, COLS)
    x, r = pl.pallas_call(
        final_kernel,
        out_shape=(shape((1, LANES)), shape((1, LANES))),
        in_specs=[VMEM] * 2,
        out_specs=(VMEM,) * 2,
        compiler_params=params(4),
        name="final",
    )(moments_held, own)
    return mu.reshape(LANES), x.reshape(LANES), r.reshape(LANES)


def solution(mesh):
    spread = P(AXES)
    wide = P(None, AXES)
    fine = Mesh(mesh.devices.reshape(4, 2, 4, 8), AXES)
    return jax.shard_map(
        local,
        mesh=fine,
        in_specs=(wide, spread, wide, spread, P(), P(), P(), P()),
        out_specs=(spread,) * 3,
        check_vma=False,
    )
```

```python
import math

import jax
import jax.numpy as jnp
from jax import lax
from jax.experimental import pallas as pl
from jax.experimental.pallas import tpu as pltpu
from jax.sharding import Mesh
from jax.sharding import PartitionSpec as P

F32 = jnp.float32
BF16 = jnp.bfloat16
FEATS = 24
LANES = 128
RUN_BLOCKS = 4
WIDE = CHUNK = 512
MU_CHUNK = 256
PACKED = RUN_BLOCKS * FEATS + FEATS + 8
DEPTH = 160
ROOT = math.sqrt(math.log2(math.e))
VMEM = pl.BlockSpec(memory_space=pltpu.VMEM)
AXES = ("y", "core", "x", "z")
ROWS = ("core", "z")
COLS = ("y", "x")
HBM = pl.BlockSpec(memory_space=pltpu.HBM)
SMEM = pl.BlockSpec(memory_space=pltpu.SMEM)


def params(mib):
    return pltpu.CompilerParams(vmem_limit_bytes=mib * 1024 * 1024)


def shape(dims, kind=F32):
    return jax.ShapeDtypeStruct(dims, kind)


def split(x):
    high = x.astype(BF16).astype(F32)
    rest = x - high
    mid = rest.astype(BF16).astype(F32)
    return high, mid, rest - mid


def norm_rows(norm, at):
    high, mid, low = split(norm)
    row = lax.broadcasted_iota(jnp.int32, (8, norm.shape[1]), 0)
    ones = jnp.where((row >= 3 - at) & (row < 6 - at), 1.0, 0.0)
    return jnp.where(row == at, high, jnp.where(row == at + 1, mid, jnp.where(row == at + 2, low, ones)))


def scaled(points, scale):
    return (points - 0.5) * scale


def half_norm(points):
    return -0.5 * jnp.sum(points * points, axis=0, keepdims=True)


def left(points, scale):
    u = scaled(points, scale)
    high, mid, low = split(u)
    norms = norm_rows(half_norm(u), 0)
    return jnp.concatenate([high, high, high, mid, mid, low, norms, jnp.zeros_like(norms)], 0)


def right(points, scale):
    v = scaled(points, scale)
    high, mid, low = split(v)
    norms = norm_rows(half_norm(v), 3)
    return jnp.concatenate([high, mid, low, high, mid, high, norms, jnp.zeros_like(norms)], 0)


def scale_column(lengths):
    row = lax.broadcasted_iota(jnp.int32, (FEATS, LANES), 0)
    column = jnp.ones((FEATS, LANES), F32)
    for i in range(FEATS):
        column = jnp.where(row == i, lengths[i], column)
    return ROOT / column


def pack_kernel(*refs):
    sources, (out, scale_low, scale_high) = refs[:5], refs[5:8]
    held, (block, sems, out_sems) = refs[8:13], refs[13:]
    copies = [pltpu.make_async_copy(a, b, sems.at[i]) for i, (a, b) in enumerate(zip(sources, held))]
    for copy in copies:
        copy.start()
    for copy in copies:
        copy.wait()
    runs, weights, points, len_low, len_high = held
    last = jnp.broadcast_to(weights[:, :LANES], (8, LANES))
    row = lax.broadcasted_iota(jnp.int32, (8, LANES), 0)
    for q in range(RUN_BLOCKS):
        lanes = slice(q * LANES, (q + 1) * LANES)
        block[q * FEATS : (q + 1) * FEATS, :] = runs[:, lanes]
        if q:
            last = jnp.where(row == q, weights[:, lanes], last)
    block[RUN_BLOCKS * FEATS : PACKED - 8, :] = points[...]
    block[PACKED - 8 :, :] = last
    copies = [pltpu.make_async_copy(block, out.at[i], out_sems.at[i]) for i in range(out.shape[0])]
    for copy in copies:
        copy.start()
    scale_low[...] = scale_column(len_low)
    scale_high[...] = scale_column(len_high)
    for copy in copies:
        copy.wait()


def place_of(m, at):
    block = (m >> 3) * 8 + ((at[0] & 7) ^ (m >> 1 & 3) ^ 4 * (m & 1))
    return pl.ds(pl.multiple_of(block * LANES, LANES), LANES)


def prep_kernel(points, scale_low, scale_high, at, out, rows_out):
    for m in range(points.shape[0]):
        place = place_of(m, at)
        out[place, :] = left(points[m], scale_low[...]).T.astype(BF16)
        rows_out[:, place] = left(points[m], scale_high[...]).astype(BF16)


def column_of(line, out, rows):
    out[rows, :] = jnp.broadcast_to(line, (LANES, LANES)).T


def weighted(cols, rows, column):
    term = jnp.exp2(jnp.dot(cols, rows, preferred_element_type=F32))
    count, wide = term.shape
    term = term * jnp.concatenate([column] * (wide // LANES), 1)
    return jnp.sum(term.reshape(count // 8, 8, wide), axis=0)


def mu_kernel(held, rows_in, scale, scale_high, high, rho, noise, at, out, cols_out, even, odd, total, lines):
    blocks = held.shape[0]

    def side(r):
        parts = [right(held[r, q * FEATS : (q + 1) * FEATS, :], scale[...]) for q in range(RUN_BLOCKS)]
        return jnp.concatenate([p.astype(BF16) for p in parts], 1)

    def work(r, runs):
        weights = held[r, PACKED - 8 :, :]
        for i in range(0, rows_in.shape[0], MU_CHUNK):
            rows = slice(i, i + MU_CHUNK)
            acc = total[rows, :]
            term = jnp.exp2(jnp.dot(rows_in[rows, :], runs[...], preferred_element_type=F32))
            for q in range(RUN_BLOCKS):
                acc = acc + term[:, q * LANES : (q + 1) * LANES] * weights[q : q + 1, :]
            total[rows, :] = acc

    total[...] = jnp.zeros_like(total)
    held_sides = (even, odd)
    even[...] = side(0)
    for r in range(blocks):
        if r + 1 < blocks:
            held_sides[(r + 1) % 2][...] = side(r + 1)
        work(r, held_sides[r % 2])
        cols = right(held[r, RUN_BLOCKS * FEATS : PACKED - 8, :], scale_high[...])
        cols_out[r * LANES : (r + 1) * LANES, :] = cols.T.astype(BF16)
    for k in range(lines.shape[0]):
        lines[k : k + 1, :] = jnp.sum(total[k * LANES : (k + 1) * LANES, :].T, axis=0, keepdims=True)
    mu = lines[...]
    row = lax.broadcasted_iota(jnp.int32, mu.shape, 0)
    target = -rho[0] * mu
    target = jnp.where(row == at[0], target + high[...], target)
    for i in range(out.shape[0]):
        out[i] = jnp.where(row == i, mu, target)


def lines_of(total):
    line = jnp.sum(total[...], axis=0, keepdims=True)
    return jnp.concatenate([line[:, k : k + LANES] for k in range(0, line.shape[1], LANES)], 0)


def first_kernel(held, rows_in, cols_in, high, rho, noise, at, at_col, out, target_out, mu_out, sums):
    total = jnp.sum(held[...], axis=0)
    row = lax.broadcasted_iota(jnp.int32, total.shape, 0)
    own = row == at[0]
    target = jnp.where(own, high[...] - rho[0] * total, total)
    target_out[...] = target
    mu_out[...] = jnp.sum(jnp.where(own, total, 0.0), axis=0, keepdims=True)
    own_target = jnp.sum(jnp.where(own, target, 0.0), axis=0, keepdims=True)
    size = 2 * LANES

    for k in range(0, cols_in.shape[0], size):
        cols = cols_in[k : k + size, :]
        acc = jnp.zeros((size, LANES), F32)
        for c in range(0, rows_in.shape[1], WIDE):
            term = jnp.exp2(jnp.dot(cols, rows_in[:, c : c + WIDE], preferred_element_type=F32))
            for q in range(0, WIDE, LANES):
                s = (c + q) // LANES
                acc = acc + term[:, q : q + LANES] * target_out[s : s + 1, :]
        for q in range(0, size, LANES):
            at_row = (k + q) // LANES
            sums[at_row : at_row + 1, :] = jnp.sum(acc[q : q + LANES, :].T, axis=0, keepdims=True)
    image = sums[...]
    image = jnp.where(lax.broadcasted_iota(jnp.int32, image.shape, 0) == at_col[0], image + noise[0] * own_target, image)
    for i in range(out.shape[0]):
        out[i] = image


def second_kernel(held, rows_in, cols_in, noise, at, at_col, out, column, total):
    image = jnp.sum(held[...], axis=0)
    mine = lax.broadcasted_iota(jnp.int32, image.shape, 0) == at_col[0]
    own = jnp.sum(jnp.where(mine, image, 0.0), axis=0, keepdims=True)
    for k in range(image.shape[0]):
        column_of(image[k : k + 1, :], column, slice(k * LANES, (k + 1) * LANES))
    total[...] = jnp.zeros_like(total)

    for i in range(0, cols_in.shape[0], CHUNK):
        rows = slice(i, i + CHUNK)
        for c in range(0, rows_in.shape[1], WIDE):
            total[:, c : c + WIDE] += weighted(cols_in[rows, :], rows_in[:, c : c + WIDE], column[rows, :])
    last = lines_of(total)
    row = lax.broadcasted_iota(jnp.int32, last.shape, 0)
    last = jnp.where(row == at[0], last + noise[0] * own, last)
    for i in range(out.shape[0]):
        for k in range(last.shape[0]):
            out[i, k] = last[k : k + 1, :]
        out[i, last.shape[0]] = own


def two_sum(a, b):
    s = a + b
    t = s - a
    return s, (a - (s - t)) + (b - t)


def pair_add(x, y):
    s, e = two_sum(x[0], y[0])
    return two_sum(s, e + (x[1] + y[1]))


def product(a, b):
    ah = a.astype(BF16).astype(F32)
    bh = b.astype(BF16).astype(F32)
    al, bl = a - ah, b - bh
    s, e = two_sum(ah * bh, ah * bl + al * bh)
    return two_sum(s, e + al * bl)


def pair_product(x, y):
    s, e = product(x[0], y[0])
    return two_sum(s, e + (x[0] * y[1] + x[1] * y[0]))


def minus(x):
    return -x[0], -x[1]


def pair_ratio(x, y):
    q = x[0] / y[0]
    rest = pair_add(x, minus(pair_product((q, jnp.zeros_like(q)), y)))
    return two_sum(q, (rest[0] + rest[1]) / y[0])


def fold_rows(x):
    high, low = x
    count = high.shape[0]
    while count > 8:
        count //= 2
        high, low = pair_add((high[:count], low[:count]), (high[count:], low[count:]))
    return high, low


def moments_kernel(held, target, at, out, own_out):
    count = target.shape[0]
    senders = range(held.shape[0])
    last = jnp.concatenate([sum(held[j, k] for j in senders) for k in range(count)], 0)
    image = jnp.concatenate([held[j, count] for j in senders], 0)
    b = target[...]
    for i, (p, q) in enumerate(((b, b), (b, image), (image, image), (image, last))):
        high, low = fold_rows(product(p, q))
        for shift in (4, 2, 1):
            high, low = pair_add((high, low), (pltpu.roll(high, shift, 0), pltpu.roll(low, shift, 0)))
        for j in range(out.shape[0]):
            out[j, i : i + 1, :] = high[:1]
            out[j, 4 + i : 5 + i, :] = low[:1]
    own = lax.broadcasted_iota(jnp.int32, b.shape, 0) == at[0]
    for i, v in enumerate((b, image, last)):
        own_out[i : i + 1, :] = jnp.sum(jnp.where(own, v, 0.0), axis=0, keepdims=True)


def final_kernel(held, own, mu, mu_out, x_out, r_out, x_held, r_held, sems):
    copies = [
        pltpu.make_async_copy(a, b, sems.at[i])
        for i, (a, b) in enumerate(((mu, mu_out), (x_held, x_out), (r_held, r_out)))
    ]
    copies[0].start()
    pairs = [(held[j], pltpu.roll(held[j], 4, 0)) for j in range(held.shape[0])]
    while len(pairs) > 1:
        pairs = [pair_add(a, b) for a, b in zip(pairs[::2], pairs[1::2])]
    h, l = pairs[0]
    for shift in (64, 32, 16, 8, 4, 2, 1):
        h, l = pair_add((h, l), (pltpu.roll(h, shift, 1), pltpu.roll(l, shift, 1)))
    sums = [(h[i : i + 1], l[i : i + 1]) for i in range(4)]
    m0, m1, m2, m3 = sums
    alpha = pair_ratio(m0, m1)
    ratio = pair_ratio(m2, m1)
    v1 = pair_add(m2, minus(pair_product(m1, pair_ratio(m1, m0))))
    v2 = pair_add(m3, minus(pair_product(m2, ratio)))
    scale = pair_product(alpha, ratio)
    alpha0, grow = alpha[0], scale[0]
    alpha1 = (v1[0] + v1[1]) / (v2[0] + v2[1])
    b, image, last = own[0:1, :], own[1:2, :], own[2:3, :]
    x_held[...] = alpha0 * b + alpha1 * (grow * b - alpha0 * image)
    copies[1].start()
    r_held[...] = (b - alpha0 * image) - alpha1 * (grow * image - alpha0 * last)
    copies[2].start()
    for copy in copies:
        copy.wait()


def exchange_z(blocks, step, size):
    return lax.ppermute(blocks, "z", [(i, i ^ step) for i in range(size)])


def exchange(blocks, axes):
    return lax.all_to_all(blocks, axes, 0, 0, tiled=True)


def local(runs, weights, points, high, len_low, len_high, rho, noise):
    n_row, n_col = lax.axis_size(ROWS), lax.axis_size(COLS)
    place = lax.axis_index(COLS)
    at, at_col = lax.axis_index(ROWS).reshape(1), place.reshape(1)
    high = jnp.where(place >= 0, high, 0.0).reshape(1, LANES)
    cols_len, rows_len = n_col * LANES, n_row * LANES
    size = lax.axis_size("z")
    to_col, scale_low, scale_high = pl.pallas_call(
        pack_kernel,
        out_shape=(shape((n_col, PACKED, LANES)), shape((FEATS, LANES)), shape((FEATS, LANES))),
        in_specs=[HBM] * 5,
        out_specs=(HBM, VMEM, VMEM),
        scratch_shapes=[
            pltpu.VMEM((FEATS, RUN_BLOCKS * LANES), F32),
            pltpu.VMEM((1, RUN_BLOCKS * LANES), F32),
            pltpu.VMEM((FEATS, LANES), F32),
            pltpu.SMEM((FEATS,), F32),
            pltpu.SMEM((FEATS,), F32),
            pltpu.VMEM((PACKED, LANES), F32),
            pltpu.SemaphoreType.DMA((5,)),
            pltpu.SemaphoreType.DMA((n_col,)),
        ],
        compiler_params=params(60),
        name="pack",
    )(runs, weights.reshape(1, RUN_BLOCKS * LANES), points, len_low, len_high)
    far = exchange_z(points, 4, size)
    by_col = exchange(to_col, COLS)
    near = jnp.stack([points, far])
    by_row = jnp.concatenate([near] + [exchange_z(near, step, size) for step in (1, 2, 3)], 0)
    by_row = lax.all_gather(by_row, "core", axis=0, tiled=True)
    row_low, row_parts = pl.pallas_call(
        prep_kernel,
        out_shape=(shape((rows_len, DEPTH), BF16), shape((DEPTH, rows_len), BF16)),
        in_specs=[VMEM] * 3 + [SMEM],
        out_specs=(VMEM,) * 2,
        compiler_params=params(4),
        name="prep",
    )(by_row, scale_low, scale_high, at)
    mu_terms, col_parts = pl.pallas_call(
        mu_kernel,
        out_shape=(shape((n_row, n_row, LANES)), shape((cols_len, DEPTH), BF16)),
        in_specs=[VMEM] * 5 + [SMEM] * 3,
        out_specs=(VMEM,) * 2,
        scratch_shapes=[
            pltpu.VMEM((DEPTH, RUN_BLOCKS * LANES), BF16),
            pltpu.VMEM((DEPTH, RUN_BLOCKS * LANES), BF16),
            pltpu.VMEM((rows_len, LANES), F32),
            pltpu.VMEM((n_row, LANES), F32),
        ],
        compiler_params=params(16),
        name="mu",
    )(by_col, row_low, scale_low, scale_high, high, rho, noise, at)
    mu_held = exchange(mu_terms, ROWS)
    image_terms, target, mu = pl.pallas_call(
        first_kernel,
        out_shape=(shape((n_col, n_col, LANES)), shape((n_row, LANES)), shape((1, LANES))),
        in_specs=[VMEM] * 4 + [SMEM] * 4,
        out_specs=(VMEM,) * 3,
        scratch_shapes=[pltpu.VMEM((n_col, LANES), F32)],
        compiler_params=params(4),
        name="first",
    )(mu_held, row_parts, col_parts, high, rho, noise, at, at_col)
    image_held = exchange(image_terms, COLS)
    last_terms = pl.pallas_call(
        second_kernel,
        out_shape=shape((n_row, n_row + 1, 1, LANES)),
        in_specs=[VMEM] * 3 + [SMEM] * 3,
        out_specs=VMEM,
        scratch_shapes=[pltpu.VMEM((cols_len, LANES), F32), pltpu.VMEM((8, rows_len), F32)],
        compiler_params=params(8),
        name="second",
    )(image_held, row_parts, col_parts, noise, at, at_col)
    last_held = exchange(last_terms, ROWS)
    moments, own = pl.pallas_call(
        moments_kernel,
        out_shape=(shape((n_col, 8, LANES)), shape((8, LANES))),
        in_specs=[VMEM] * 2 + [SMEM],
        out_specs=(VMEM,) * 2,
        compiler_params=params(4),
        name="moments",
    )(last_held, target, at)
    moments_held = exchange(moments, COLS)
    mu, x, r = pl.pallas_call(
        final_kernel,
        out_shape=(shape((1, LANES)),) * 3,
        in_specs=[VMEM] * 3,
        out_specs=(HBM,) * 3,
        scratch_shapes=[pltpu.VMEM((1, LANES), F32), pltpu.VMEM((1, LANES), F32), pltpu.SemaphoreType.DMA((3,))],
        compiler_params=params(4),
        name="final",
    )(moments_held, own, mu)
    return mu.reshape(LANES), x.reshape(LANES), r.reshape(LANES)


def solution(mesh):
    spread = P(AXES)
    wide = P(None, AXES)
    fine = Mesh(mesh.devices.reshape(4, 2, 4, 8), AXES)
    return jax.shard_map(
        local,
        mesh=fine,
        in_specs=(wide, spread, wide, spread, P(), P(), P(), P()),
        out_specs=(spread,) * 3,
        check_vma=False,
    )
```
